32 devices in a mesh: src: 8 (over z, x), tgt: 4 (over y, core).
Axes of the slice: x: 2, y: 2, z: 4, core: 2. Of those that a mesh axis runs over, the one named last changes fastest.
Arguments:
- sources: float32 [50, 4096], P(None, 'src'), may hold values from -1.2 to 1.2
- targets: float32 [50, 16384], P(None, 'tgt'), may hold values from -1.2 to 1.2
- pair_active: int32 [8, 4], P('src', 'tgt'), may hold values from 0 to 1, as said below
- count_src: int32 [8], replicated, may hold values from 256 to 512, as said below
- count_tgt: int32 [4], replicated, may hold values from 2048 to 4096, as said below
Outputs:
- source_potential: float32 [4096], P('src')
- target_potential: float32 [16384], P('tgt')
- ancestors: float32 [50, 16384], P(None, ('tgt', 'src'))
The draws below stay inside these ranges and needn't reach their ends.
Inputs may be any that keep to these rules, and one draw needn't show every extreme that they name: `pair_active`: every source block has at least one listed tile and every target tile is listed with at least one source block. `count_src`: some block holds exactly 512 live cells and another exactly 256. `count_tgt`: some tile holds exactly 4096 live cells and another exactly 2048.
All inputs are finite; a program needn't handle non-finite values.
Results may differ from the reference program's by a relative error of at most 0.0003.
Values sent between devices are 32-bit elements; how exact they have to be, the bound alone decides.
No kernel may reach another device: no remote copies, remote signals or barrier semaphores. Data moves between devices by JAX's collectives and lax.ppermute only.
A program may use at most 64 MiB of HBM per device.

```python
import jax
import jax.numpy as jnp
from jax import lax

DIMS = 50
SRC_DEV = 512
TILE = 4096
ITERS = 4
SOURCES = 4096
TARGETS = 16384
N_SRC = 8


def counts_with_ends(key, length, most):
    key_one, key_two, key_three = jax.random.split(key, 3)
    values = jax.random.randint(key_one, (length,), most // 2, most + 1)
    first = jax.random.randint(key_two, (), 0, length)
    second = (first + 1 + jax.random.randint(key_three, (), 0, length - 1)) % length
    values = values.at[first].set(most)
    return values.at[second].set(most // 2).astype(jnp.int32)


def draw_pair_active(key, part):
    key = jax.random.fold_in(key, 11)
    tiles = TARGETS // TILE
    listed = jax.random.randint(key, (N_SRC, tiles), 0, 3) > 0
    rows = jnp.arange(N_SRC, dtype=jnp.int32)[:, None]
    cols = jnp.arange(tiles, dtype=jnp.int32)[None, :]
    return (listed | (rows % tiles == cols)).astype(jnp.int32)


def draw_count_src(key, part):
    key = jax.random.fold_in(key, 23)
    return counts_with_ends(key, N_SRC, SRC_DEV)


def draw_count_tgt(key, part):
    key = jax.random.fold_in(key, 37)
    return counts_with_ends(key, TARGETS // TILE, TILE)


def levels(rng, shape, cuts, low, top_value):
    def one(position, parts):
        heights = jax.random.uniform(jax.random.fold_in(jax.random.fold_in(rng, 6), position), (parts,), jnp.float32, low / len(cuts), top_value / len(cuts))
        return jnp.repeat(jnp.exp(heights), shape[position] // parts).reshape((-1,) + (1,) * (len(shape) - position - 1))

    level = one(*cuts[0])
    for cut in cuts[1:]:
        level = level * one(*cut)
    return level


def noise(own_key, dims, width, reach, cuts=(), kind=jnp.bfloat16):
    values = width * jax.random.normal(own_key, dims, jnp.float32)
    if cuts:
        values = values * levels(own_key, dims, cuts, -0.22, 0.18)
    return jnp.clip(values, -reach, reach).astype(kind)


def setup_inputs(seed: int = 0) -> dict:
    streams_of = jax.random.split(jax.random.key(seed), 6)
    return {
        "sources": noise(streams_of[0], (DIMS, SOURCES), 0.2, 1.2, ((1, 8),), jnp.float32),
        "targets": noise(streams_of[1], (DIMS, TARGETS), 0.2, 1.2, ((1, 4),), jnp.float32),
        "pair_active": draw_pair_active(jax.random.fold_in(streams_of[5], 71), 0),
        "count_src": draw_count_src(jax.random.fold_in(streams_of[5], 71), 0),
        "count_tgt": draw_count_tgt(jax.random.fold_in(streams_of[5], 71), 0),
    }


EPS = 0.02
NEG = -1e30


def tile_cost(block, points):
    left = jnp.sum(block * block, axis=0)
    right = jnp.sum(points * points, axis=0)
    cross = lax.dot_general(block, points, (((0,), (0,)), ((), ())), precision=lax.Precision.HIGHEST)
    return left[:, None] + right[None, :] - 2.0 * cross


def reference(sources, targets, pair_active, count_src, count_tgt):
    log_a = -jnp.log(jnp.sum(count_src).astype(jnp.float32))
    log_b = -jnp.log(jnp.sum(count_tgt).astype(jnp.float32))
    within = jnp.arange(TARGETS, dtype=jnp.int32) % TILE
    col_ok = within < jnp.repeat(count_tgt, TILE)
    blocks = sources.reshape(DIMS, N_SRC, SRC_DEV).transpose(1, 0, 2)
    row_all = jnp.arange(SRC_DEV, dtype=jnp.int32)[None, :] < count_src[:, None]
    active_cols = jnp.repeat(pair_active > 0, TILE, axis=1) & col_ok[None, :]
    order = jnp.arange(N_SRC, dtype=jnp.int32)

    def pieces(b):
        cost = tile_cost(blocks[b], targets)
        allowed = row_all[b][:, None] & active_cols[b][None, :]
        return cost, allowed

    def row_step(g):
        def one(b):
            cost, allowed = pieces(b)
            logits = jnp.where(allowed, (g[None, :] - cost) / EPS, NEG)
            peak = jnp.max(logits, axis=1)
            total = jnp.sum(jnp.where(allowed, jnp.exp(logits - peak[:, None]), 0.0), axis=1)
            live = row_all[b]
            return jnp.where(live, EPS * (log_a - peak - jnp.log(jnp.where(live, total, 1.0))), 0.0)
        return lax.map(one, order)

    def column_step(f):
        def one(carry, b):
            cost, allowed = pieces(b)
            logits = jnp.where(allowed, (f[b][:, None] - cost) / EPS, NEG)
            peak = jnp.max(logits, axis=0)
            total = jnp.sum(jnp.where(allowed, jnp.exp(logits - peak[None, :]), 0.0), axis=0)
            best = jnp.maximum(carry[0], peak)
            joined = carry[1] * jnp.exp(carry[0] - best) + total * jnp.exp(peak - best)
            return (best, joined), None
        start = (jnp.full((TARGETS,), NEG, jnp.float32), jnp.zeros((TARGETS,), jnp.float32))
        (peak, total), _ = lax.scan(one, start, order)
        return jnp.where(col_ok, EPS * (log_b - peak - jnp.log(jnp.where(col_ok, total, 1.0))), 0.0)

    g = jnp.zeros((TARGETS,), jnp.float32)
    f = jnp.zeros((N_SRC, SRC_DEV), jnp.float32)
    for step in range(ITERS):
        f = row_step(g)
        g = column_step(f)

    def gather_one(acc, b):
        cost, allowed = pieces(b)
        expo = jnp.where(allowed, (f[b][:, None] + g[None, :] - cost) / EPS - log_b, NEG)
        weight = jnp.where(allowed, jnp.exp(expo), 0.0)
        return acc + jnp.dot(blocks[b], weight, precision=lax.Precision.HIGHEST), None

    ancestors, _ = lax.scan(gather_one, jnp.zeros((DIMS, TARGETS), jnp.float32), order)
    return f.reshape(SOURCES), g, ancestors
```

```python
import functools
import math

import jax
import jax.numpy as jnp
from jax import lax
from jax.experimental import pallas as pl
from jax.experimental.pallas import tpu as pltpu
from jax.sharding import PartitionSpec as P

ITERS = 4
EPS = 0.02
NEG = -1e30
LOG2E = math.log2(math.e)
SCALE = LOG2E / EPS
LANES = 128
DEPTH = 64
VMEM_LIMIT = 40 * 1024 * 1024

VMEM_SPEC = pl.BlockSpec(memory_space=pltpu.VMEM)
SMEM_SPEC = pl.BlockSpec(memory_space=pltpu.SMEM)


def pinned(x):
    return pltpu.with_memory_space_constraint(x, pltpu.VMEM)


def split(x):
    high = x.astype(jnp.bfloat16)
    rest = x - high.astype(jnp.float32)
    mid = rest.astype(jnp.bfloat16)
    low = (rest - mid.astype(jnp.float32)).astype(jnp.bfloat16)
    return high, mid, low


def to_sublanes(row_ref, col_ref, size):
    for start in range(0, size, LANES):
        piece = jnp.broadcast_to(row_ref[0:1, start : start + LANES], (LANES, LANES))
        col_ref[start : start + LANES, :] = piece.T


def fold_lanes(peak_ref, total_ref):
    peaks = peak_ref[...].T
    top = jnp.max(peaks, axis=0, keepdims=True)
    total = jnp.sum(total_ref[...].T * jnp.exp2(peaks - top), axis=0, keepdims=True)
    return top + jnp.log2(total)


def row_lse(score_ref, add_ref, peak_ref, total_ref, out_ref):
    rows, cols = score_ref.shape

    def block(i, _):
        here = pl.ds(pl.multiple_of(i * 8, 8), 8)
        z = []
        for start in range(0, cols, LANES):
            lanes = slice(start, start + LANES)
            value = score_ref[here, lanes]
            if add_ref is not None:
                value = value + add_ref[0:1, lanes]
            z.append(value)
        peak = functools.reduce(jnp.maximum, z)
        total = functools.reduce(jnp.add, [jnp.exp2(v - peak) for v in z])
        peak_ref[here, :] = peak
        total_ref[here, :] = total
        return 0

    lax.fori_loop(0, rows // 8, block, 0, unroll=2)
    out_ref[...] = fold_lanes(peak_ref, total_ref)


def col_lse(score_ref, add_ref, out_ref):
    rows, cols = score_ref.shape
    wide = 4

    def block(c, _):
        tops = [jnp.full((8, LANES), -jnp.inf, jnp.float32)] * wide
        spots = [pl.ds(pl.multiple_of((c * wide + k) * LANES, LANES), LANES) for k in range(wide)]
        for r in range(0, rows, 8):
            add = add_ref[r : r + 8, :]
            tops = [jnp.maximum(t, score_ref[r : r + 8, s] + add) for t, s in zip(tops, spots)]
        peaks = [jnp.broadcast_to(jnp.max(t, axis=0, keepdims=True), (8, LANES)) for t in tops]
        sums = [jnp.zeros((8, LANES), jnp.float32)] * wide
        for r in range(0, rows, 8):
            add = add_ref[r : r + 8, :]
            sums = [u + jnp.exp2(score_ref[r : r + 8, s] + (add - p)) for u, s, p in zip(sums, spots, peaks)]
        for s, p, u in zip(spots, peaks, sums):
            out_ref[0:1, s] = p[0:1] + jnp.log2(jnp.sum(u, axis=0, keepdims=True))
        return 0

    lax.fori_loop(0, cols // (LANES * wide), block, 0)


def transposed_terms(left):
    high, mid, low = split(left.T)
    return jnp.concatenate([high, high, mid, mid, high, low], axis=1)


def right_terms(right):
    high, mid, low = split(right)
    return jnp.concatenate([high, mid, high, mid, low, high], axis=0)


def pad_into(pad_ref, values):
    pad_ref[...] = jnp.zeros(pad_ref.shape, jnp.float32)
    pad_ref[0 : values.shape[0], :] = values


def live_sum(counts):
    total = counts[0]
    for i in range(1, counts.shape[0]):
        total = total + counts[i]
    return jnp.full((1, LANES), total, jnp.int32).astype(jnp.float32)


def wide(x, size):
    return jnp.concatenate([x] * (size // LANES), axis=1)


def first_kernel(
    src_hbm, tgt_hbm, count_src_hbm, count_tgt_hbm, pair,
    score_ref, lse_ref, row_aux, col_aux, own_ref, half_ref, token_ref,
    src_ref, tgt_ref, count_src, count_tgt, sems,
    right_pad, left_pad, own_pad, terms_ref, norm_ref, col_ref, peak_ref, total_ref,
):
    rows, cols = score_ref.shape
    dims = src_ref.shape[0]
    copies = [
        pltpu.make_async_copy(one, two, sems.at[i])
        for i, (one, two) in enumerate(
            [(count_src_hbm, count_src), (count_tgt_hbm, count_tgt), (src_hbm, src_ref), (tgt_hbm, tgt_ref)]
        )
    ]
    for copy in copies:
        copy.start()
    for ref in (right_pad, left_pad, own_pad, token_ref):
        ref[...] = jnp.zeros(ref.shape, jnp.float32)
    half = DEPTH // 2
    mine = pl.ds(pl.multiple_of((lax.axis_index("tgt") % 2) * half, half), half)
    theirs = pl.ds(pl.multiple_of((1 - lax.axis_index("tgt") % 2) * half, half), half)
    for copy in copies[:3]:
        copy.wait()
    n_rows = count_src[lax.axis_index("src")]
    n_cols = count_tgt[lax.axis_index("tgt")]
    listed = pair[0, 0] > 0
    row_live = lax.broadcasted_iota(jnp.int32, (1, rows), 1) < n_rows
    col_live = lax.broadcasted_iota(jnp.int32, (1, cols), 1) < n_cols
    row_aux[0:1, :] = row_live.astype(jnp.float32)
    row_aux[1:2, :] = jnp.where(row_live, wide(-jnp.log2(live_sum(count_src)), rows), 0.0)
    row_aux[2:3, :] = (row_live & listed).astype(jnp.float32)
    col_aux[0:1, :] = col_live.astype(jnp.float32)
    col_aux[1:2, :] = jnp.where(col_live, wide(-jnp.log2(live_sum(count_tgt)), cols), 0.0)
    left_pad[0:dims, :] = src_ref[...]
    half_ref[0] = left_pad[mine, :]
    left = left_pad[...]
    norm_ref[0:1, :] = jnp.where(row_live, -SCALE * jnp.sum(left * left, axis=0, keepdims=True), NEG)
    to_sublanes(norm_ref, col_ref, rows)
    terms_ref[...] = transposed_terms(left * (2.0 * SCALE))
    copies[3].wait()
    size = 512

    def block(c, _):
        here = pl.ds(pl.multiple_of(c * size, size), size)
        right_pad[0:dims, :] = tgt_ref[:, here]
        right = right_pad[...]
        spot = lax.broadcasted_iota(jnp.int32, (1, size), 1) + c * size
        norm = -SCALE * jnp.sum(right * right, axis=0, keepdims=True)
        norm = jnp.where((spot < n_cols) & listed, norm, NEG)
        cross = jnp.dot(terms_ref[...], right_terms(right), preferred_element_type=jnp.float32)
        score_ref[:, here] = cross + (wide(col_ref[...], size) + norm)
        return 0

    lax.fori_loop(0, cols // size, block, 0)
    share = own_ref.shape[1]
    own_pad[0:dims, :] = tgt_ref[:, pl.ds(pl.multiple_of(lax.axis_index("src") * share, share), share)]
    own_ref[0:half, :] = own_pad[mine, :]
    own_ref[half:, :] = own_pad[theirs, :]
    row_lse(score_ref, None, peak_ref, total_ref, lse_ref)


def slab_kernel(own_ref, mine_ref, theirs_ref, slab_ref, token_ref, right_pad, terms_ref, norm_ref, col_ref, *, first):
    share = own_ref.shape[1]
    _, half, rows = mine_ref.shape
    left = own_ref[...]
    norm_ref[0:1, :] = -SCALE * jnp.sum(left * left, axis=0, keepdims=True)
    to_sublanes(norm_ref, col_ref, share)
    terms_ref[...] = transposed_terms(left * (2.0 * SCALE))
    for b in range(slab_ref.shape[1] // rows):
        right_pad[0:half, :] = mine_ref[first + b]
        right_pad[half:, :] = theirs_ref[first + b]
        right = right_pad[...]
        norm = -SCALE * jnp.sum(right * right, axis=0, keepdims=True)
        cross = jnp.dot(terms_ref[...], right_terms(right), preferred_element_type=jnp.float32)
        slab_ref[:, b * rows : (b + 1) * rows] = cross + (wide(col_ref[...], rows) + norm)
    token_ref[...] = jnp.zeros(token_ref.shape, jnp.float32)


def col_kernel(score_ref, lse_ref, aux_ref, out_ref, f_ref, masked_ref, col_ref):
    f = aux_ref[1:2, :] - lse_ref[...] * aux_ref[0:1, :]
    f_ref[...] = f
    masked_ref[...] = jnp.where(aux_ref[2:3, :] > 0, f, NEG)
    to_sublanes(f_ref, col_ref, f_ref.shape[1])
    col_lse(score_ref, col_ref, out_ref)


def row_kernel(score_ref, lse_ref, aux_ref, out_ref, g_ref, peak_ref, total_ref):
    g_ref[...] = aux_ref[1:2, :] - lse_ref[...] * aux_ref[0:1, :]
    row_lse(score_ref, g_ref, peak_ref, total_ref, out_ref)


def last_kernel(*refs, pieces, groups):
    slabs, refs = refs[: len(pieces)], refs[len(pieces) :]
    mine, refs = refs[:groups], refs[groups:]
    theirs, refs = refs[:groups], refs[groups:]
    f_all_ref, lse_ref, aux_ref, f_ref, _, out_ref, f_out, g_out, row_ref, col_ref, right_pad, sum_ref, turn_ref = refs
    share = slabs[0].shape[0]
    _, half, rows = mine[0].shape
    f_out[...] = f_ref[...] * (1.0 / SCALE)
    g_out[...] = (aux_ref[1:2, :] - lse_ref[...] * aux_ref[0:1, :]) * (1.0 / SCALE)
    own = pl.ds(pl.multiple_of(lax.axis_index("src") * share, share), share)
    row_ref[0:1, :] = jnp.where(aux_ref[0:1, own] > 0, -lse_ref[0:1, own], NEG)
    to_sublanes(row_ref, col_ref, share)
    spot = 0
    for slab_ref, (group, first) in zip(slabs, pieces):
        for b in range(slab_ref.shape[1] // rows):
            right_pad[0:half, :] = mine[group][first + b]
            right_pad[half:, :] = theirs[group][first + b]
            terms = jnp.concatenate(split(right_pad[...]), axis=0)
            add = wide(col_ref[...], rows) + f_all_ref[0:1, spot : spot + rows]
            high, mid, _ = split(jnp.exp2(slab_ref[:, b * rows : (b + 1) * rows] + add))
            sums = lax.dot_general(
                jnp.concatenate([high, mid], axis=1), jnp.concatenate([terms, terms], axis=1),
                (((1,), (1,)), ((), ())), preferred_element_type=jnp.float32,
            )
            if spot == 0:
                sum_ref[...] = sums
            else:
                sum_ref[...] += sums
            spot += rows
    sums = sum_ref[...].T
    turn_ref[...] = sums[0:DEPTH] + sums[DEPTH : 2 * DEPTH] + sums[2 * DEPTH :]
    core = lax.axis_index("tgt") % 2
    out_ref[0:half, :] = turn_ref[pl.ds(pl.multiple_of(core * half, half), half), :]
    out_ref[half:, :] = turn_ref[pl.ds(pl.multiple_of((1 - core) * half, half), half), :][: out_ref.shape[0] - half]


def merge(one, two):
    top = jnp.maximum(one, two)
    return top + jnp.log2(1.0 + jnp.exp2(jnp.minimum(one, two) - top))


def swap(value, axis, step):
    return lax.ppermute(value, axis, [(i, i ^ step) for i in range(lax.axis_size(axis))])


def doubling(size):
    return [1 << k for k in range(size.bit_length() - 1)]


def call(kernel, outs, scratch, ins, flops, expos=0, pin=True):
    return pl.pallas_call(
        kernel,
        out_shape=[(pltpu.VMEM if pin else jax.ShapeDtypeStruct)(shape, jnp.float32) for shape in outs],
        in_specs=[VMEM_SPEC] * len(ins),
        out_specs=[VMEM_SPEC] * len(outs),
        scratch_shapes=[pltpu.VMEM(*s) if isinstance(s[-1], type) else pltpu.VMEM(s, jnp.float32) for s in scratch],
        compiler_params=pltpu.CompilerParams(vmem_limit_bytes=VMEM_LIMIT),
        cost_estimate=pl.CostEstimate(flops=flops, bytes_accessed=0, transcendentals=expos),
    )(*[pinned(x) for x in ins])


def tie(*values):
    return lax.optimization_barrier(values)


class Beside:
    def __init__(self, half, token, own, steps):
        self.parts = half
        self.token = token
        self.own = own
        self.steps = list(steps)
        self.coming = None
        self.mine = []
        self.theirs = []
        self.todo = []
        self.done = []
        self.slabs = []

    def plain(self, value, axis, step):
        return swap(value, axis, step)

    def start(self, value, axis, step):
        if self.coming is not None or not self.steps:
            return swap(value, axis, step)
        value, self.parts = tie(value, self.parts)
        other = swap(value, axis, step)
        self.coming = swap(self.parts, "src", self.steps.pop(0))
        return other

    def land(self, value, delay=0):
        if self.coming is None:
            return value
        coming, self.coming = self.coming, None
        for _ in range(delay):
            self.token, coming = tie(self.token, coming)
            self.token = swap(self.token, "tgt", 1)
        value, coming, self.token = tie(value, coming, self.token)
        if self.steps:
            self.parts = jnp.concatenate([self.parts, coming], axis=0)
        else:
            self.mine = [self.parts, coming]
        return value

    def trade(self, value, axis, step):
        if len(self.theirs) == len(self.mine):
            return swap(value, axis, step)
        group = len(self.theirs)
        value, self.mine[group] = tie(value, self.mine[group])
        other = swap(value, axis, step)
        self.theirs.append(swap(self.mine[group], "tgt", 1))
        other, self.theirs[group] = tie(other, self.theirs[group])
        size = max(self.mine[group].shape[0] // 2, 1)
        self.todo += [(group, first, size) for first in range(0, self.mine[group].shape[0], size)]
        return other

    def piece(self):
        group, first, size = self.todo.pop(0)
        mine, theirs = self.mine[group], self.theirs[group]
        share = self.own.shape[1]
        rows = mine.shape[2]
        slab, token = call(
            functools.partial(slab_kernel, first=first),
            [(share, size * rows), (8, LANES)],
            [(DEPTH, rows), ((share, 6 * DEPTH), jnp.bfloat16), (8, share), (share, LANES)],
            [self.own, mine, theirs],
            12 * DEPTH * share * size * rows,
        )
        self.done.append((group, first))
        self.slabs.append(slab)
        return token

    def work(self, value, axis, step):
        if not self.todo:
            return swap(value, axis, step)
        value, self.own = tie(value, self.own)
        other = swap(value, axis, step)
        other, _ = tie(other, self.piece())
        return other

    def finish(self, value):
        while self.steps or self.coming is not None:
            if self.coming is None:
                self.coming = swap(self.parts, "src", self.steps.pop(0))
            value = self.land(value)
        while len(self.theirs) < len(self.mine):
            value = self.trade(value, "tgt", 1)
        while self.todo:
            self.piece()


def shards(sources, targets, pair_active, count_src, count_tgt):
    dims, rows = sources.shape
    cols = targets.shape[1]
    share = cols // lax.axis_size("src")
    column = (rows, LANES)
    pairs = rows * cols
    hbm = [pltpu.with_memory_space_constraint(x, pltpu.HBM) for x in (sources, targets, count_src, count_tgt)]
    outs = [(rows, cols), (1, rows), (8, rows), (8, cols), (DEPTH, share), (1, DEPTH // 2, rows), (1, LANES)]
    score, lse, row_aux, col_aux, own, half, token = pl.pallas_call(
        first_kernel,
        out_shape=[pltpu.VMEM(shape, jnp.float32) for shape in outs],
        in_specs=[pl.BlockSpec(memory_space=pltpu.HBM)] * 4 + [SMEM_SPEC],
        out_specs=[VMEM_SPEC] * len(outs),
        scratch_shapes=[
            pltpu.VMEM((dims, rows), jnp.float32),
            pltpu.VMEM((dims, cols), jnp.float32),
            pltpu.SMEM(count_src.shape, jnp.int32),
            pltpu.SMEM(count_tgt.shape, jnp.int32),
            pltpu.SemaphoreType.DMA((4,)),
            pltpu.VMEM((DEPTH, 512), jnp.float32),
            pltpu.VMEM((DEPTH, rows), jnp.float32),
            pltpu.VMEM((DEPTH, share), jnp.float32),
            pltpu.VMEM((rows, 6 * DEPTH), jnp.bfloat16),
            pltpu.VMEM((8, rows), jnp.float32),
            pltpu.VMEM(column, jnp.float32),
            pltpu.VMEM(column, jnp.float32),
            pltpu.VMEM(column, jnp.float32),
        ],
        compiler_params=pltpu.CompilerParams(vmem_limit_bytes=VMEM_LIMIT),
        cost_estimate=pl.CostEstimate(flops=12 * DEPTH * pairs, bytes_accessed=0, transcendentals=pairs),
    )(*hbm, pair_active)
    over_tgt = doubling(lax.axis_size("tgt"))
    over_src = doubling(lax.axis_size("src"))
    over_src = over_src[1:] + over_src[:1]
    side = Beside(half, token, own, over_src)
    beside = {
        (0, "tgt", over_tgt[-1]): side.start,
        (0, "src", over_src[-1]): side.start,
        (1, "src", over_src[-1]): side.start,
        (2, "src", over_src[0]): side.trade,
        (2, "src", over_src[1 % len(over_src)]): side.trade,
    }
    for step in range(ITERS):
        for bit in over_tgt:
            exchange = beside.get((step, "tgt", bit), side.work if step > 1 and bit == over_tgt[-1] else side.plain)
            lse = merge(lse, exchange(lse, "tgt", bit))
        if step > 1:
            lse = side.land(lse)
        lse, f, masked = call(
            col_kernel, [(1, cols), (1, rows), (1, rows)], [column], [score, lse, row_aux], 4 * pairs, pairs
        )
        if step < 2:
            lse = side.land(lse)
        if step < ITERS - 1:
            for bit in over_src:
                exchange = beside.get((step, "src", bit), side.work)
                lse = merge(lse, exchange(lse, "src", bit))
            lse, _ = call(
                row_kernel, [(1, rows), (1, cols)], [column, column], [score, lse, col_aux], 4 * pairs, pairs
            )
    for bit in over_src:
        both = jnp.concatenate([lse, masked], axis=1)
        other = side.work(both, "src", bit)
        lse = merge(lse, other[:, :cols])
        masked = jnp.concatenate([masked, other[:, cols:]], axis=1)
    side.finish(lse)
    ancestors, f, g = call(
        functools.partial(last_kernel, pieces=side.done, groups=len(side.mine)),
        [(dims, share), (1, rows), (1, cols)],
        [(8, share), (share, LANES), (DEPTH, rows), (share, 3 * DEPTH), (DEPTH, share)],
        [*side.slabs, *side.mine, *side.theirs, masked, lse, col_aux, f, side.token],
        18 * DEPTH * pairs, pairs, pin=False,
    )
    return (f[0], g[0], ancestors)


def solution(mesh):
    return jax.shard_map(
        shards,
        mesh=mesh,
        in_specs=(P(None, "src"), P(None, "tgt"), P("src", "tgt"), P(), P()),
        out_specs=(P("src"), P("tgt"), P(None, ("tgt", "src"))),
        check_vma=False,
    )
```

```python
import functools
import math

import jax
import jax.numpy as jnp
from jax import lax
from jax.experimental import pallas as pl
from jax.experimental.pallas import tpu as pltpu
from jax.sharding import PartitionSpec as P

ITERS = 4
EPS = 0.02
NEG = -1e30
LOG2E = math.log2(math.e)
SCALE = LOG2E / EPS
LANES = 128
DEPTH = 64
FACTOR_MAX = 2.0**20
SUM_MIN = 2.0**-70
TOTAL_MAX = 2.0**100
VMEM_LIMIT = 14 * 1024 * 1024

VMEM_SPEC = pl.BlockSpec(memory_space=pltpu.VMEM)
SMEM_SPEC = pl.BlockSpec(memory_space=pltpu.SMEM)


def pinned(x):
    return pltpu.with_memory_space_constraint(x, pltpu.VMEM)


def split(x):
    high = x.astype(jnp.bfloat16)
    rest = x - high.astype(jnp.float32)
    mid = rest.astype(jnp.bfloat16)
    low = (rest - mid.astype(jnp.float32)).astype(jnp.bfloat16)
    return high, mid, low


def put(ref, row):
    for k in range(row.shape[1] // LANES):
        ref[k : k + 1, :] = row[:, k * LANES : (k + 1) * LANES]


def positions(shape):
    return lax.broadcasted_iota(jnp.int32, shape, 0) * LANES + lax.broadcasted_iota(jnp.int32, shape, 1)


def to_sublanes(vector_ref, col_ref):
    for k in range(vector_ref.shape[0]):
        col_ref[k * LANES : (k + 1) * LANES, :] = jnp.broadcast_to(vector_ref[k : k + 1, :], (LANES, LANES)).T


def fold_lanes(peak_ref, total_ref, out_ref):
    for k in range(out_ref.shape[0]):
        here = slice(k * LANES, (k + 1) * LANES)
        peaks = peak_ref[here, :].T
        top = jnp.max(peaks, axis=0, keepdims=True)
        total = jnp.sum(total_ref[here, :].T * jnp.exp2(peaks - top), axis=0, keepdims=True)
        out_ref[k : k + 1, :] = top + jnp.log2(total)


def row_lse(score_ref, add_ref, peak_ref, total_ref, out_ref):
    rows, cols = score_ref.shape

    def block(i, _):
        here = pl.ds(pl.multiple_of(i * 8, 8), 8)
        z = []
        for k in range(cols // LANES):
            value = score_ref[here, k * LANES : (k + 1) * LANES]
            if add_ref is not None:
                value = value + add_ref[k : k + 1, :]
            z.append(value)
        peak = functools.reduce(jnp.maximum, z)
        peak_ref[here, :] = peak
        total_ref[here, :] = functools.reduce(jnp.add, [jnp.exp2(v - peak) for v in z])
        return 0

    lax.fori_loop(0, rows // 8, block, 0)
    fold_lanes(peak_ref, total_ref, out_ref)


def col_lse(score_ref, add_ref, out_ref, kernel_ref=None, top_ref=None):
    rows, cols = score_ref.shape
    wide = 4

    def block(c, _):
        tops = [jnp.full((8, LANES), -jnp.inf, jnp.float32)] * wide
        spots = [pl.ds(pl.multiple_of((c * wide + k) * LANES, LANES), LANES) for k in range(wide)]
        for r in range(0, rows, 8):
            add = add_ref[r : r + 8, :]
            tops = [jnp.maximum(t, score_ref[r : r + 8, s] + add) for t, s in zip(tops, spots)]
        peaks = [jnp.broadcast_to(jnp.max(t, axis=0, keepdims=True), (8, LANES)) for t in tops]
        sums = [jnp.zeros((8, LANES), jnp.float32)] * wide
        for r in range(0, rows, 8):
            add = add_ref[r : r + 8, :]
            terms = [jnp.exp2(score_ref[r : r + 8, s] + (add - p)) for s, p in zip(spots, peaks)]
            sums = [u + t for u, t in zip(sums, terms)]
            if kernel_ref is not None:
                for s, t in zip(spots, terms):
                    kernel_ref[r : r + 8, s] = t
        for k, (p, u) in enumerate(zip(peaks, sums)):
            spot = pl.ds(c * wide + k, 1)
            if top_ref is not None:
                top_ref[spot, :] = p[0:1]
            out_ref[spot, :] = p[0:1] + jnp.log2(jnp.sum(u, axis=0, keepdims=True))
        return 0

    lax.fori_loop(0, cols // (LANES * wide), block, 0)


def source_terms(x):
    high, mid, low = split(x * (2.0 * SCALE))
    return [high, high, mid, mid, high, low]


def target_terms(y):
    high, mid, low = split(y)
    return [high, mid, high, mid, low, high]


def pad_into(pad_ref, values):
    pad_ref[...] = jnp.zeros(pad_ref.shape, jnp.float32)
    pad_ref[0 : values.shape[0], :] = values


def live_sum(counts):
    total = counts[0]
    for i in range(1, counts.shape[0]):
        total = total + counts[i]
    return jnp.full((1, LANES), total, jnp.int32).astype(jnp.float32)


def wide(x, size):
    return jnp.concatenate([x] * (size // LANES), axis=1)


def first_kernel(
    src_hbm, tgt_hbm, count_src_hbm, count_tgt_hbm, pair,
    score_ref, lse_ref, row_aux, col_aux, own_ref, half_ref,
    src_ref, tgt_ref, count_src, count_tgt, sems,
    right_pad, left_pad, terms_ref, norm_ref, col_ref, peak_ref, total_ref,
):
    rows, cols = score_ref.shape
    dims = src_ref.shape[0]
    copies = [
        pltpu.make_async_copy(one, two, sems.at[i])
        for i, (one, two) in enumerate(
            [(count_src_hbm, count_src), (count_tgt_hbm, count_tgt), (src_hbm, src_ref), (tgt_hbm, tgt_ref)]
        )
    ]
    for copy in copies:
        copy.start()
    for ref in (right_pad, left_pad, own_ref):
        ref[...] = jnp.zeros(ref.shape, jnp.float32)
    half = DEPTH // 2
    for copy in copies[:3]:
        copy.wait()
    n_rows = count_src[lax.axis_index("src")]
    n_cols = count_tgt[lax.axis_index("tgt")]
    listed = pair[0, 0] > 0
    row_live = positions(row_aux.shape[1:]) < n_rows
    col_live = positions(col_aux.shape[1:]) < n_cols
    row_aux[0] = row_live.astype(jnp.float32)
    row_aux[1] = jnp.where(row_live, -jnp.log2(live_sum(count_src)), 0.0)
    row_aux[2] = (row_live & listed).astype(jnp.float32)
    col_aux[0] = col_live.astype(jnp.float32)
    col_aux[1] = jnp.where(col_live, -jnp.log2(live_sum(count_tgt)), 0.0)
    left_pad[0:dims, :] = src_ref[...]
    half_ref[0] = left_pad[pl.ds(pl.multiple_of((lax.axis_index("tgt") % 2) * half, half), half), :]
    left = left_pad[...]
    put(norm_ref, -SCALE * jnp.sum(left * left, axis=0, keepdims=True))
    norm_ref[...] = jnp.where(row_live, norm_ref[...], NEG)
    to_sublanes(norm_ref, col_ref)
    terms_ref[...] = jnp.concatenate(source_terms(left.T), axis=1)
    copies[3].wait()
    size = 512

    def scores(c):
        here = pl.ds(pl.multiple_of(c * size, size), size)
        right_pad[0:dims, :] = tgt_ref[:, here]
        right = right_pad[...]
        spot = lax.broadcasted_iota(jnp.int32, (1, size), 1) + c * size
        norm = -SCALE * jnp.sum(right * right, axis=0, keepdims=True)
        norm = jnp.where((spot < n_cols) & listed, norm, NEG)
        terms = jnp.concatenate(target_terms(right), axis=0)
        cross = jnp.dot(terms_ref[...], terms, preferred_element_type=jnp.float32)
        score = cross + (wide(col_ref[...], size) + norm)
        score_ref[:, here] = score
        return [score[:, k : k + LANES] for k in range(0, size, LANES)]

    first = scores(0)
    peak = jnp.max(functools.reduce(jnp.maximum, first), axis=1, keepdims=True)
    peak_ref[...] = jnp.broadcast_to(peak, peak_ref.shape)
    total_ref[...] = functools.reduce(jnp.add, [jnp.exp2(z - peak_ref[...]) for z in first])

    def block(c, _):
        total_ref[...] += functools.reduce(jnp.add, [jnp.exp2(z - peak_ref[...]) for z in scores(c)])
        return 0

    lax.fori_loop(1, cols // size, block, 0)
    share = own_ref.shape[1]
    own_ref[0:dims, :] = tgt_ref[:, pl.ds(pl.multiple_of(lax.axis_index("src") * share, share), share)]
    fold_lanes(peak_ref, total_ref, lse_ref)

    @pl.when(jnp.logical_not(jnp.max(total_ref[...]) <= TOTAL_MAX))
    def _():
        row_lse(score_ref, None, peak_ref, total_ref, lse_ref)


def slab_kernel(own_ref, mine_ref, theirs_ref, slab_ref, token_ref, right_pad, terms_ref, norm_ref, col_ref, *, first):
    share = own_ref.shape[1]
    _, half, rows = mine_ref.shape
    left = own_ref[...]
    put(norm_ref, -SCALE * jnp.sum(left * left, axis=0, keepdims=True))
    to_sublanes(norm_ref, col_ref)
    terms_ref[...] = jnp.concatenate(target_terms(left.T), axis=1)
    core = lax.axis_index("tgt") % 2
    here = pl.ds(pl.multiple_of(core * half, half), half)
    there = pl.ds(pl.multiple_of((1 - core) * half, half), half)
    for b in range(slab_ref.shape[1] // rows):
        right_pad[here, :] = mine_ref[first + b]
        right_pad[there, :] = theirs_ref[first + b]
        right = right_pad[...]
        norm = -SCALE * jnp.sum(right * right, axis=0, keepdims=True)
        terms = jnp.concatenate(source_terms(right), axis=0)
        cross = jnp.dot(terms_ref[...], terms, preferred_element_type=jnp.float32)
        slab_ref[:, b * rows : (b + 1) * rows] = cross + (wide(col_ref[...], rows) + norm)
    token_ref[...] = jnp.zeros(token_ref.shape, jnp.float32)


def row_sums(kernel_ref, factor_ref, total_ref, out_ref):
    rows, cols = kernel_ref.shape
    tall = 8

    def block(i, _):
        spots = [pl.ds(pl.multiple_of((i * tall + k) * 8, 8), 8) for k in range(tall)]
        sums = [jnp.zeros((8, LANES), jnp.float32)] * tall
        for t in range(cols // LANES):
            lanes = slice(t * LANES, (t + 1) * LANES)
            factor = jnp.broadcast_to(factor_ref[t : t + 1, :], (8, LANES))
            sums = [u + kernel_ref[s, lanes] * factor for u, s in zip(sums, spots)]
        for s, u in zip(spots, sums):
            total_ref[s, :] = u
        return 0

    lax.fori_loop(0, rows // (8 * tall), block, 0)
    for k in range(out_ref.shape[0]):
        out_ref[k : k + 1, :] = jnp.sum(total_ref[k * LANES : (k + 1) * LANES, :].T, axis=0, keepdims=True)


def col_sums(kernel_ref, factor_ref, out_ref):
    rows, cols = kernel_ref.shape
    wide = 8

    def block(c, _):
        spots = [pl.ds(pl.multiple_of((c * wide + k) * LANES, LANES), LANES) for k in range(wide)]
        sums = [jnp.zeros((8, LANES), jnp.float32)] * wide
        for r in range(0, rows, 8):
            factor = factor_ref[r : r + 8, :]
            sums = [u + kernel_ref[r : r + 8, s] * factor for u, s in zip(sums, spots)]
        for k, u in enumerate(sums):
            out_ref[pl.ds(c * wide + k, 1), :] = jnp.sum(u, axis=0, keepdims=True)
        return 0

    lax.fori_loop(0, cols // (LANES * wide), block, 0)


def out_of_range(total, needed, factor):
    small = jnp.where(needed & jnp.logical_not(total >= SUM_MIN), 1.0, 0.0)
    large = jnp.where(factor <= FACTOR_MAX, 0.0, 1.0)
    return jnp.max(jnp.maximum(jnp.max(small, axis=0, keepdims=True), jnp.max(large, axis=0, keepdims=True))) > 0.5


def set_f(lse_ref, aux_ref, f_ref, masked_ref):
    f = aux_ref[1] - lse_ref[...] * aux_ref[0]
    f_ref[...] = f
    masked_ref[...] = jnp.where(aux_ref[2] > 0, f, NEG)


def first_col_kernel(score_ref, lse_ref, aux_ref, out_ref, f_ref, masked_ref, kernel_ref, top_ref, col_ref):
    set_f(lse_ref, aux_ref, f_ref, masked_ref)
    to_sublanes(f_ref, col_ref)
    col_lse(score_ref, col_ref, out_ref, kernel_ref, top_ref)


def col_kernel(
    score_ref, kernel_ref, top_ref, base_ref, lse_ref, aux_ref, out_ref, f_ref, masked_ref, factor_ref, col_ref
):
    set_f(lse_ref, aux_ref, f_ref, masked_ref)
    factor_ref[...] = jnp.exp2(f_ref[...] - base_ref[...])
    to_sublanes(factor_ref, col_ref)
    col_sums(kernel_ref, col_ref, out_ref)
    total = out_ref[...]
    top = top_ref[...]
    redo = out_of_range(total, top > 0.5 * NEG, factor_ref[...])
    out_ref[...] = jnp.where(total > 0, top + jnp.log2(total), NEG)

    @pl.when(redo)
    def _():
        to_sublanes(f_ref, col_ref)
        col_lse(score_ref, col_ref, out_ref)


def row_kernel(
    score_ref, kernel_ref, top_ref, base_ref, parts_ref, row_aux, col_aux, out_ref,
    g_ref, factor_ref, peak_ref, total_ref,
):
    parts = parts_ref[...]
    peak = jnp.max(parts, axis=0)
    lse = peak + jnp.log2(jnp.sum(jnp.exp2(parts - peak[None]), axis=0))
    g_ref[...] = col_aux[1] - lse * col_aux[0]
    factor_ref[...] = jnp.where(col_aux[0] > 0, jnp.exp2(top_ref[...] - lse), 0.0)
    row_sums(kernel_ref, factor_ref, total_ref, out_ref)
    total = out_ref[...]
    redo = out_of_range(total, row_aux[2] > 0, factor_ref[...])
    log_b = col_aux[1, 0:1, 0:1]
    out_ref[...] = jnp.where(total > 0, jnp.log2(total) - base_ref[...] + log_b, NEG)

    @pl.when(redo)
    def _():
        row_lse(score_ref, g_ref, peak_ref, total_ref, out_ref)


def last_kernel(*refs, pieces, groups):
    slabs, refs = refs[: len(pieces)], refs[len(pieces) :]
    mine, refs = refs[:groups], refs[groups:]
    theirs, refs = refs[:groups], refs[groups:]
    f_all_ref, lse_ref, aux_ref, f_ref, out_ref, f_out, g_out, own_ref, col_ref, right_pad, sum_ref = refs
    _, half, rows = mine[0].shape
    f_out[...] = f_ref[...] * (1.0 / SCALE)
    g_out[...] = (aux_ref[1] - lse_ref[...] * aux_ref[0]) * (1.0 / SCALE)
    n_own = own_ref.shape[0]
    for k in range(n_own):
        spot = pl.ds(lax.axis_index("src") * n_own + k, 1)
        own_ref[k : k + 1, :] = jnp.where(aux_ref[0, spot, :] > 0, -lse_ref[spot, :], NEG)
    to_sublanes(own_ref, col_ref)
    core = lax.axis_index("tgt") % 2
    here = pl.ds(pl.multiple_of(core * half, half), half)
    there = pl.ds(pl.multiple_of((1 - core) * half, half), half)
    spot = 0
    for slab_ref, (group, first) in zip(slabs, pieces):
        for b in range(slab_ref.shape[1] // rows):
            right_pad[here, :] = mine[group][first + b]
            right_pad[there, :] = theirs[group][first + b]
            terms = jnp.concatenate(split(right_pad[...]), axis=0)
            high, mid = [], []
            for k in range(rows // LANES):
                start = b * rows + k * LANES
                add = col_ref[...] + f_all_ref[spot : spot + 1, :]
                parts = split(jnp.exp2(slab_ref[:, start : start + LANES] + add))
                high.append(parts[0])
                mid.append(parts[1])
                spot += 1
            sums = lax.dot_general(
                jnp.concatenate(high + mid, axis=1), jnp.concatenate([terms, terms], axis=1),
                (((1,), (1,)), ((), ())), preferred_element_type=jnp.float32,
            )
            if spot == rows // LANES:
                sum_ref[...] = sums
            else:
                sum_ref[...] += sums
    sums = sum_ref[...].T
    out_ref[...] = (sums[0:DEPTH] + sums[DEPTH : 2 * DEPTH] + sums[2 * DEPTH :])[0 : out_ref.shape[0]]


def merge(one, two):
    top = jnp.maximum(one, two)
    return top + jnp.log2(1.0 + jnp.exp2(jnp.minimum(one, two) - top))


def swap(value, axis, step):
    return lax.ppermute(value, axis, [(i, i ^ step) for i in range(lax.axis_size(axis))])


def doubling(size):
    return [1 << k for k in range(size.bit_length() - 1)]


def call(kernel, outs, scratch, ins, flops, expos=0, pin=True):
    return pl.pallas_call(
        kernel,
        out_shape=[(pltpu.VMEM if pin else jax.ShapeDtypeStruct)(shape, jnp.float32) for shape in outs],
        in_specs=[VMEM_SPEC] * len(ins),
        out_specs=[VMEM_SPEC] * len(outs),
        scratch_shapes=[pltpu.VMEM(*s) if isinstance(s[-1], type) else pltpu.VMEM(s, jnp.float32) for s in scratch],
        compiler_params=pltpu.CompilerParams(vmem_limit_bytes=VMEM_LIMIT),
        cost_estimate=pl.CostEstimate(flops=flops, bytes_accessed=0, transcendentals=expos),
    )(*[pinned(x) for x in ins])


def tie(*values):
    return lax.optimization_barrier(values)


class Beside:
    def __init__(self, half, own, steps):
        self.parts = half
        self.own = own
        self.steps = list(steps)
        self.coming = None
        self.mine = []
        self.theirs = []
        self.ready = []
        self.todo = []
        self.done = []
        self.slabs = []

    def start(self, value, axis, step):
        if self.coming is not None or not self.steps:
            return swap(value, axis, step)
        value, parts = tie(value, self.parts)
        if self.mine:
            self.mine = [parts]
        self.parts = parts
        other = swap(value, axis, step)
        self.coming = swap(parts, "src", self.steps.pop(0))
        return other

    def land(self, value):
        if self.coming is None:
            return value
        value, coming = tie(value, self.coming)
        self.coming = None
        if self.steps:
            self.parts = jnp.concatenate([self.parts, coming], axis=0)
            if len(self.steps) == 1:
                self.mine = [self.parts]
        else:
            self.mine.append(coming)
        return value

    def trade(self, value):
        group = len(self.theirs)
        if group == len(self.mine):
            return value
        value, self.mine[group] = tie(value, self.mine[group])
        self.theirs.append(swap(self.mine[group], "tgt", 1))
        return value

    def traded(self, value):
        for group in range(len(self.ready), len(self.theirs)):
            value, self.theirs[group] = tie(value, self.theirs[group])
            self.ready.append(group)
            size = max(self.mine[group].shape[0] // 2, 1)
            self.todo += [(group, first, size) for first in range(0, self.mine[group].shape[0], size)]
        return value

    def piece(self):
        group, first, size = self.todo.pop(0)
        mine, theirs = self.mine[group], self.theirs[group]
        share = self.own.shape[1]
        rows = mine.shape[2]
        slab, token = call(
            functools.partial(slab_kernel, first=first),
            [(share, size * rows), (8, LANES)],
            [(DEPTH, rows), ((share, 6 * DEPTH), jnp.bfloat16), (share // LANES, LANES), (share, LANES)],
            [self.own, mine, theirs],
            12 * DEPTH * share * size * rows,
        )
        self.done.append((group, first))
        self.slabs.append(slab)
        return token

    def work(self, value, axis, step):
        if not self.todo:
            return swap(value, axis, step)
        value, self.own = tie(value, self.own)
        other = swap(value, axis, step)
        other, _ = tie(other, self.piece())
        return other

    def finish(self, value):
        while self.steps or self.coming is not None:
            if self.coming is None:
                self.coming = swap(self.parts, "src", self.steps.pop(0))
            value = self.land(value)
        while len(self.theirs) < len(self.mine):
            value = self.trade(value)
        self.traded(value)
        while self.todo:
            self.piece()


def shards(sources, targets, pair_active, count_src, count_tgt):
    dims, rows = sources.shape
    cols = targets.shape[1]
    share = cols // lax.axis_size("src")
    column = (rows, LANES)
    by_row = (rows // LANES, LANES)
    by_col = (cols // LANES, LANES)
    pairs = rows * cols
    hbm = [pltpu.with_memory_space_constraint(x, pltpu.HBM) for x in (sources, targets, count_src, count_tgt)]
    outs = [(rows, cols), by_row, (3, *by_row), (3, *by_col), (DEPTH, share), (1, DEPTH // 2, rows)]
    score, lse, row_aux, col_aux, own, half = pl.pallas_call(
        first_kernel,
        out_shape=[pltpu.VMEM(shape, jnp.float32) for shape in outs],
        in_specs=[pl.BlockSpec(memory_space=pltpu.HBM)] * 4 + [SMEM_SPEC],
        out_specs=[VMEM_SPEC] * len(outs),
        scratch_shapes=[
            pltpu.VMEM((dims, rows), jnp.float32),
            pltpu.VMEM((dims, cols), jnp.float32),
            pltpu.SMEM(count_src.shape, jnp.int32),
            pltpu.SMEM(count_tgt.shape, jnp.int32),
            pltpu.SemaphoreType.DMA((4,)),
            pltpu.VMEM((DEPTH, 512), jnp.float32),
            pltpu.VMEM((DEPTH, rows), jnp.float32),
            pltpu.VMEM((rows, 6 * DEPTH), jnp.bfloat16),
            pltpu.VMEM(by_row, jnp.float32),
            pltpu.VMEM(column, jnp.float32),
            pltpu.VMEM(column, jnp.float32),
            pltpu.VMEM(column, jnp.float32),
        ],
        compiler_params=pltpu.CompilerParams(vmem_limit_bytes=VMEM_LIMIT),
        cost_estimate=pl.CostEstimate(flops=12 * DEPTH * pairs, bytes_accessed=0, transcendentals=pairs),
    )(*hbm, pair_active)
    over_tgt = doubling(lax.axis_size("tgt"))
    over_src = doubling(lax.axis_size("src"))
    over_src = over_src[1:] + over_src[:1]
    side = Beside(half, own, over_src)
    for step in range(ITERS):
        for bit in over_tgt:
            if step == ITERS - 1 and bit == over_tgt[0]:
                lse = side.trade(lse)
            if bit != over_tgt[-1]:
                other = swap(lse, "tgt", bit)
            elif step < ITERS - 1:
                other = side.start(lse, "tgt", bit)
            else:
                other = side.work(lse, "tgt", bit)
            lse = merge(lse, other)
        if step == ITERS - 2:
            lse = side.trade(lse)
        if step == 0:
            lse, base, masked, kernel, top = call(
                first_col_kernel,
                [by_col, by_row, by_row, (rows, cols), by_col],
                [column], [score, lse, row_aux], 0,
            )
        else:
            lse, f, masked = call(
                col_kernel,
                [by_col, by_row, by_row],
                [by_row, column], [score, kernel, top, base, lse, row_aux], 0,
            )
        if step < ITERS - 1:
            lse = side.traded(side.land(lse))
            lse = jnp.broadcast_to(lse, (lax.axis_size("src"), *by_col))
            lse = lax.all_to_all(lse, "src", 0, 0, tiled=True)
            (lse,) = call(
                row_kernel,
                [by_row],
                [by_col, by_col, column, column],
                [score, kernel, top, base, lse, row_aux, col_aux], 0,
            )
    lse = side.traded(lse)
    for bit in over_src:
        both = jnp.concatenate([lse, masked], axis=0)
        other = side.work(both, "src", bit)
        lse = merge(lse, other[: by_col[0]])
        masked = jnp.concatenate([masked, other[by_col[0] :]], axis=0)
    side.finish(lse)
    ancestors, f, g = call(
        functools.partial(last_kernel, pieces=side.done, groups=len(side.mine)),
        [(dims, share), by_row, by_col],
        [(share // LANES, LANES), (share, LANES), (DEPTH, rows), (share, 3 * DEPTH)],
        [*side.slabs, *side.mine, *side.theirs, masked, lse, col_aux, f],
        18 * DEPTH * pairs, pairs, pin=False,
    )
    return (f.reshape(rows), g.reshape(cols), ancestors)


def solution(mesh):
    return jax.shard_map(
        shards,
        mesh=mesh,
        in_specs=(P(None, "src"), P(None, "tgt"), P("src", "tgt"), P(), P()),
        out_specs=(P("src"), P("tgt"), P(None, ("tgt", "src"))),
        check_vma=False,
    )
```

```python
import functools
import math

import jax
import jax.numpy as jnp
from jax import lax
from jax.experimental import pallas as pl
from jax.experimental.pallas import tpu as pltpu
from jax.sharding import PartitionSpec as P

ITERS = 4
EPS = 0.02
NEG = -1e30
LOG2E = math.log2(math.e)
SCALE = LOG2E / EPS
LANES = 128
DEPTH = 64
FACTOR_MAX = 2.0**20
SUM_MIN = 2.0**-70
TOTAL_MAX = 2.0**100
VMEM_LIMIT = 14 * 1024 * 1024

VMEM_SPEC = pl.BlockSpec(memory_space=pltpu.VMEM)
SMEM_SPEC = pl.BlockSpec(memory_space=pltpu.SMEM)


def pinned(x):
    return pltpu.with_memory_space_constraint(x, pltpu.VMEM)


def split(x):
    high = x.astype(jnp.bfloat16)
    rest = x - high.astype(jnp.float32)
    mid = rest.astype(jnp.bfloat16)
    low = (rest - mid.astype(jnp.float32)).astype(jnp.bfloat16)
    return high, mid, low


def put(ref, row):
    for k in range(row.shape[1] // LANES):
        ref[k : k + 1, :] = row[:, k * LANES : (k + 1) * LANES]


def positions(shape):
    return lax.broadcasted_iota(jnp.int32, shape, 0) * LANES + lax.broadcasted_iota(jnp.int32, shape, 1)


def to_sublanes(vector_ref, col_ref):
    for k in range(vector_ref.shape[0]):
        col_ref[k * LANES : (k + 1) * LANES, :] = jnp.broadcast_to(vector_ref[k : k + 1, :], (LANES, LANES)).T


def fold_lanes(peak_ref, total_ref, out_ref):
    for k in range(out_ref.shape[0]):
        here = slice(k * LANES, (k + 1) * LANES)
        peaks = peak_ref[here, :].T
        top = jnp.max(peaks, axis=0, keepdims=True)
        total = jnp.sum(total_ref[here, :].T * jnp.exp2(peaks - top), axis=0, keepdims=True)
        out_ref[k : k + 1, :] = top + jnp.log2(total)


def row_lse(score_ref, add_ref, peak_ref, total_ref, out_ref):
    rows, cols = score_ref.shape

    def block(i, _):
        here = pl.ds(pl.multiple_of(i * 8, 8), 8)
        z = []
        for k in range(cols // LANES):
            value = score_ref[here, k * LANES : (k + 1) * LANES]
            if add_ref is not None:
                value = value + add_ref[k : k + 1, :]
            z.append(value)
        peak = functools.reduce(jnp.maximum, z)
        peak_ref[here, :] = peak
        total_ref[here, :] = functools.reduce(jnp.add, [jnp.exp2(v - peak) for v in z])
        return 0

    lax.fori_loop(0, rows // 8, block, 0)
    fold_lanes(peak_ref, total_ref, out_ref)


def col_lse(score_ref, add_ref, out_ref, kernel_ref=None, top_ref=None):
    rows, cols = score_ref.shape
    group = 16
    tall = 4

    for first in range(0, cols // LANES, group):
        lanes = [slice((first + k) * LANES, (first + k + 1) * LANES) for k in range(group)]

        def peaks(i, tops):
            for r in range(tall):
                here = pl.ds(pl.multiple_of((i * tall + r) * 8, 8), 8)
                add = add_ref[here, :]
                tops = tuple(jnp.maximum(t, score_ref[here, s] + add) for t, s in zip(tops, lanes))
            return tops

        start = (jnp.full((8, LANES), -jnp.inf, jnp.float32),) * group
        tops = lax.fori_loop(0, rows // (8 * tall), peaks, start)
        tops = [jnp.max(t, axis=0, keepdims=True) for t in tops]
        wide_tops = [jnp.broadcast_to(t, (8, LANES)) for t in tops]

        def totals(i, sums):
            for r in range(tall):
                here = pl.ds(pl.multiple_of((i * tall + r) * 8, 8), 8)
                add = add_ref[here, :]
                terms = [jnp.exp2(score_ref[here, s] + (add - t)) for t, s in zip(wide_tops, lanes)]
                if kernel_ref is not None:
                    for s, t in zip(lanes, terms):
                        kernel_ref[here, s] = t
                sums = tuple(u + t for u, t in zip(sums, terms))
            return sums

        start = (jnp.zeros((8, LANES), jnp.float32),) * group
        sums = lax.fori_loop(0, rows // (8 * tall), totals, start)
        for k, (t, u) in enumerate(zip(tops, sums)):
            spot = slice(first + k, first + k + 1)
            if top_ref is not None:
                top_ref[spot, :] = t
            out_ref[spot, :] = t + jnp.log2(jnp.sum(u, axis=0, keepdims=True))


def source_terms(x):
    high, mid, low = split(x * (2.0 * SCALE))
    return [high, high, mid, mid, high, low]


def target_terms(y):
    high, mid, low = split(y)
    return [high, mid, high, mid, low, high]


def pad_into(pad_ref, values):
    pad_ref[...] = jnp.zeros(pad_ref.shape, jnp.float32)
    pad_ref[0 : values.shape[0], :] = values


def live_sum(counts):
    total = counts[0]
    for i in range(1, counts.shape[0]):
        total = total + counts[i]
    return jnp.full((1, LANES), total, jnp.int32).astype(jnp.float32)


def wide(x, size):
    return jnp.concatenate([x] * (size // LANES), axis=1)


def first_kernel(
    src_hbm, tgt_hbm, count_src_hbm, count_tgt_hbm, pair,
    score_ref, lse_ref, row_aux, col_aux, own_ref, half_ref,
    src_ref, tgt_ref, count_src, count_tgt, sems,
    right_pad, left_pad, terms_ref, norm_ref, col_ref, peak_ref, total_ref,
):
    rows, cols = score_ref.shape
    dims = src_ref.shape[0]
    copies = [
        pltpu.make_async_copy(one, two, sems.at[i])
        for i, (one, two) in enumerate(
            [(count_src_hbm, count_src), (count_tgt_hbm, count_tgt), (src_hbm, src_ref), (tgt_hbm, tgt_ref)]
        )
    ]
    for copy in copies:
        copy.start()
    for ref in (right_pad, left_pad, own_ref):
        ref[...] = jnp.zeros(ref.shape, jnp.float32)
    n_half = -(-dims // 2)
    for copy in copies[:3]:
        copy.wait()
    n_rows = count_src[lax.axis_index("src")]
    n_cols = count_tgt[lax.axis_index("tgt")]
    listed = pair[0, 0] > 0
    row_live = positions(row_aux.shape[1:]) < n_rows
    col_live = positions(col_aux.shape[1:]) < n_cols
    row_aux[0] = row_live.astype(jnp.float32)
    row_aux[1] = jnp.where(row_live, -jnp.log2(live_sum(count_src)), 0.0)
    row_aux[2] = (row_live & listed).astype(jnp.float32)
    col_aux[0] = col_live.astype(jnp.float32)
    col_aux[1] = jnp.where(col_live, -jnp.log2(live_sum(count_tgt)), 0.0)
    left_pad[0:dims, :] = src_ref[...]
    left = left_pad[...]
    half = jnp.where(lax.axis_index("tgt") % 2 == 0, left[0:n_half], left[n_half : 2 * n_half])
    half_ref[...] = jnp.zeros(half_ref.shape, jnp.float32)
    for k in range(rows // LANES):
        half_ref[0, k * n_half : (k + 1) * n_half, :] = half[:, k * LANES : (k + 1) * LANES]
    put(norm_ref, -SCALE * jnp.sum(left * left, axis=0, keepdims=True))
    norm_ref[...] = jnp.where(row_live, norm_ref[...], NEG)
    to_sublanes(norm_ref, col_ref)
    terms_ref[...] = jnp.concatenate(source_terms(left.T), axis=1)
    copies[3].wait()
    size = 512

    def scores(c):
        here = pl.ds(pl.multiple_of(c * size, size), size)
        right_pad[0:dims, :] = tgt_ref[:, here]
        right = right_pad[...]
        spot = lax.broadcasted_iota(jnp.int32, (1, size), 1) + c * size
        norm = -SCALE * jnp.sum(right * right, axis=0, keepdims=True)
        norm = jnp.where((spot < n_cols) & listed, norm, NEG)
        terms = jnp.concatenate(target_terms(right), axis=0)
        cross = jnp.dot(terms_ref[...], terms, preferred_element_type=jnp.float32)
        score = cross + (wide(col_ref[...], size) + norm)
        score_ref[:, here] = score
        return [score[:, k : k + LANES] for k in range(0, size, LANES)]

    first = scores(0)
    peak = jnp.max(functools.reduce(jnp.maximum, first), axis=1, keepdims=True)
    peak_ref[...] = jnp.broadcast_to(peak, peak_ref.shape)
    total_ref[...] = functools.reduce(jnp.add, [jnp.exp2(z - peak_ref[...]) for z in first])

    def block(c, _):
        total_ref[...] += functools.reduce(jnp.add, [jnp.exp2(z - peak_ref[...]) for z in scores(c)])
        return 0

    lax.fori_loop(1, cols // size, block, 0)
    share = own_ref.shape[1]
    own_ref[0:dims, :] = tgt_ref[:, pl.ds(pl.multiple_of(lax.axis_index("src") * share, share), share)]
    fold_lanes(peak_ref, total_ref, lse_ref)

    @pl.when(jnp.logical_not(jnp.max(total_ref[...]) <= TOTAL_MAX))
    def _():
        row_lse(score_ref, None, peak_ref, total_ref, lse_ref)


def slab_kernel(
    own_ref, mine_ref, theirs_ref, slab_ref, terms_out, token_ref, right_pad, terms_ref, norm_ref, col_ref,
    *, first, n_half,
):
    share = own_ref.shape[1]
    rows = right_pad.shape[1]
    left = own_ref[...]
    put(norm_ref, -SCALE * jnp.sum(left * left, axis=0, keepdims=True))
    to_sublanes(norm_ref, col_ref)
    terms_ref[...] = jnp.concatenate(target_terms(left.T), axis=1)
    even = lax.axis_index("tgt") % 2 == 0
    right_pad[...] = jnp.zeros(right_pad.shape, jnp.float32)
    for b in range(slab_ref.shape[1] // rows):
        mine, theirs = mine_ref[first + b], theirs_ref[first + b]
        upper = jnp.where(even, mine, theirs)
        lower = jnp.where(even, theirs, mine)
        for k in range(rows // LANES):
            here = slice(k * n_half, (k + 1) * n_half)
            right_pad[0:n_half, k * LANES : (k + 1) * LANES] = upper[here]
            right_pad[n_half : 2 * n_half, k * LANES : (k + 1) * LANES] = lower[here]
        right = right_pad[...]
        norm = -SCALE * jnp.sum(right * right, axis=0, keepdims=True)
        terms = jnp.concatenate(source_terms(right), axis=0)
        cross = jnp.dot(terms_ref[...], terms, preferred_element_type=jnp.float32)
        here = slice(b * rows, (b + 1) * rows)
        slab_ref[:, here] = cross + (wide(col_ref[...], rows) + norm)
        terms_out[here, :] = jnp.concatenate(split(right.T), axis=1)
    token_ref[...] = jnp.zeros(token_ref.shape, jnp.float32)


def row_sums(kernel_ref, factor_ref, total_ref, out_ref):
    rows, cols = kernel_ref.shape
    tall = 8

    def block(i, _):
        spots = [pl.ds(pl.multiple_of((i * tall + k) * 8, 8), 8) for k in range(tall)]
        sums = [jnp.zeros((8, LANES), jnp.float32)] * tall
        for t in range(cols // LANES):
            lanes = slice(t * LANES, (t + 1) * LANES)
            factor = jnp.broadcast_to(factor_ref[t : t + 1, :], (8, LANES))
            sums = [u + kernel_ref[s, lanes] * factor for u, s in zip(sums, spots)]
        for s, u in zip(spots, sums):
            total_ref[s, :] = u
        return 0

    lax.fori_loop(0, rows // (8 * tall), block, 0)
    for k in range(out_ref.shape[0]):
        out_ref[k : k + 1, :] = jnp.sum(total_ref[k * LANES : (k + 1) * LANES, :].T, axis=0, keepdims=True)


def col_sums(kernel_ref, factor_ref, out_ref):
    rows, cols = kernel_ref.shape
    lanes = [slice(start, start + LANES) for start in range(0, cols, LANES)]
    tall = 4

    def block(i, sums):
        for r in range(tall):
            here = pl.ds(pl.multiple_of((i * tall + r) * 8, 8), 8)
            factor = factor_ref[here, :]
            sums = tuple(u + kernel_ref[here, s] * factor for u, s in zip(sums, lanes))
        return sums

    sums = lax.fori_loop(0, rows // (8 * tall), block, (jnp.zeros((8, LANES), jnp.float32),) * len(lanes))
    for k, u in enumerate(sums):
        out_ref[k : k + 1, :] = jnp.sum(u, axis=0, keepdims=True)


def out_of_range(total, needed, factor):
    small = jnp.where(needed & jnp.logical_not(total >= SUM_MIN), 1.0, 0.0)
    large = jnp.where(factor <= FACTOR_MAX, 0.0, 1.0)
    return jnp.max(jnp.maximum(jnp.max(small, axis=0, keepdims=True), jnp.max(large, axis=0, keepdims=True))) > 0.5


def set_f(lse_ref, aux_ref, f_ref, masked_ref):
    f = aux_ref[1] - lse_ref[...] * aux_ref[0]
    f_ref[...] = f
    masked_ref[...] = jnp.where(aux_ref[2] > 0, f, NEG)


def first_col_kernel(score_ref, lse_ref, aux_ref, out_ref, f_ref, masked_ref, kernel_ref, top_ref, col_ref):
    set_f(lse_ref, aux_ref, f_ref, masked_ref)
    to_sublanes(f_ref, col_ref)
    col_lse(score_ref, col_ref, out_ref, kernel_ref, top_ref)


def col_kernel(
    score_ref, kernel_ref, top_ref, base_ref, lse_ref, aux_ref, out_ref, f_ref, masked_ref, factor_ref, col_ref
):
    set_f(lse_ref, aux_ref, f_ref, masked_ref)
    factor_ref[...] = jnp.exp2(f_ref[...] - base_ref[...])
    to_sublanes(factor_ref, col_ref)
    col_sums(kernel_ref, col_ref, out_ref)
    total = out_ref[...]
    top = top_ref[...]
    redo = out_of_range(total, top > 0.5 * NEG, factor_ref[...])
    out_ref[...] = jnp.where(total > 0, top + jnp.log2(total), NEG)

    @pl.when(redo)
    def _():
        to_sublanes(f_ref, col_ref)
        col_lse(score_ref, col_ref, out_ref)


def row_kernel(
    score_ref, kernel_ref, top_ref, base_ref, parts_ref, row_aux, col_aux, out_ref,
    g_ref, factor_ref, peak_ref, total_ref,
):
    parts = parts_ref[...]
    peak = jnp.max(parts, axis=0)
    lse = peak + jnp.log2(jnp.sum(jnp.exp2(parts - peak[None]), axis=0))
    g_ref[...] = col_aux[1] - lse * col_aux[0]
    factor_ref[...] = jnp.where(col_aux[0] > 0, jnp.exp2(top_ref[...] - lse), 0.0)
    row_sums(kernel_ref, factor_ref, total_ref, out_ref)
    total = out_ref[...]
    redo = out_of_range(total, row_aux[2] > 0, factor_ref[...])
    log_b = col_aux[1, 0:1, 0:1]
    out_ref[...] = jnp.where(total > 0, jnp.log2(total) - base_ref[...] + log_b, NEG)

    @pl.when(redo)
    def _():
        row_lse(score_ref, g_ref, peak_ref, total_ref, out_ref)


def last_kernel(*refs, pieces):
    slabs, refs = refs[:pieces], refs[pieces:]
    terms, refs = refs[:pieces], refs[pieces:]
    f_all_ref, lse_ref, aux_ref, f_ref, out_ref, f_out, g_out, own_ref, col_ref, sum_ref = refs
    f_out[...] = f_ref[...] * (1.0 / SCALE)
    g_out[...] = (aux_ref[1] - lse_ref[...] * aux_ref[0]) * (1.0 / SCALE)
    n_own = own_ref.shape[0]
    for k in range(n_own):
        spot = pl.ds(lax.axis_index("src") * n_own + k, 1)
        own_ref[k : k + 1, :] = jnp.where(aux_ref[0, spot, :] > 0, -lse_ref[spot, :], NEG)
    to_sublanes(own_ref, col_ref)
    spot = 0
    for slab_ref, terms_ref in zip(slabs, terms):
        high, mid = [], []
        first = spot == 0
        for start in range(0, slab_ref.shape[1], LANES):
            add = col_ref[...] + f_all_ref[spot : spot + 1, :]
            parts = split(jnp.exp2(slab_ref[:, start : start + LANES] + add))
            high.append(parts[0])
            mid.append(parts[1])
            spot += 1
        sums = jnp.dot(
            jnp.concatenate(high + mid, axis=1), jnp.concatenate([terms_ref[...]] * 2, axis=0),
            preferred_element_type=jnp.float32,
        )
        if first:
            sum_ref[...] = sums
        else:
            sum_ref[...] += sums
    sums = sum_ref[...].T
    out_ref[...] = (sums[0:DEPTH] + sums[DEPTH : 2 * DEPTH] + sums[2 * DEPTH :])[0 : out_ref.shape[0]]


def merge(one, two):
    top = jnp.maximum(one, two)
    return top + jnp.log2(1.0 + jnp.exp2(jnp.minimum(one, two) - top))


def swap(value, axis, step):
    return lax.ppermute(value, axis, [(i, i ^ step) for i in range(lax.axis_size(axis))])


def doubling(size):
    return [1 << k for k in range(size.bit_length() - 1)]


def buffer(space, shape):
    return space(*shape) if isinstance(shape[0], tuple) else space(shape, jnp.float32)


def call(kernel, outs, scratch, ins, flops, expos=0, pin=True):
    return pl.pallas_call(
        kernel,
        out_shape=[buffer(pltpu.VMEM if pin else jax.ShapeDtypeStruct, shape) for shape in outs],
        in_specs=[VMEM_SPEC] * len(ins),
        out_specs=[VMEM_SPEC] * len(outs),
        scratch_shapes=[buffer(pltpu.VMEM, shape) for shape in scratch],
        compiler_params=pltpu.CompilerParams(vmem_limit_bytes=VMEM_LIMIT),
        cost_estimate=pl.CostEstimate(flops=flops, bytes_accessed=0, transcendentals=expos),
    )(*[pinned(x) for x in ins])


def tie(*values):
    return lax.optimization_barrier(values)


class Beside:
    def __init__(self, half, own, steps, rows, n_half):
        self.parts = half
        self.own = own
        self.steps = list(steps)
        self.coming = None
        self.mine = []
        self.theirs = []
        self.ready = []
        self.todo = []
        self.terms = []
        self.rows = rows
        self.n_half = n_half
        self.slabs = []

    def start(self, value, axis, step):
        if self.coming is not None or not self.steps:
            return swap(value, axis, step)
        value, parts = tie(value, self.parts)
        if self.mine:
            self.mine = [parts]
        self.parts = parts
        other = swap(value, axis, step)
        self.coming = swap(parts, "src", self.steps.pop(0))
        return other

    def land(self, value):
        if self.coming is None:
            return value
        value, coming = tie(value, self.coming)
        self.coming = None
        if self.steps:
            self.parts = jnp.concatenate([self.parts, coming], axis=0)
            if len(self.steps) == 1:
                self.mine = [self.parts]
        else:
            self.mine.append(coming)
        return value

    def trade(self, value):
        group = len(self.theirs)
        if group == len(self.mine):
            return value
        value, self.mine[group] = tie(value, self.mine[group])
        self.theirs.append(swap(self.mine[group], "tgt", 1))
        return value

    def traded(self, value):
        for group in range(len(self.ready), len(self.theirs)):
            value, self.theirs[group] = tie(value, self.theirs[group])
            self.ready.append(group)
            size = max(self.mine[group].shape[0] // 2, 1)
            self.todo += [(group, first, size) for first in range(0, self.mine[group].shape[0], size)]
        return value

    def piece(self):
        group, first, size = self.todo.pop(0)
        mine, theirs = self.mine[group], self.theirs[group]
        share = self.own.shape[1]
        rows = self.rows
        slab, terms, token = call(
            functools.partial(slab_kernel, first=first, n_half=self.n_half),
            [(share, size * rows), ((size * rows, 3 * DEPTH), jnp.bfloat16), (8, LANES)],
            [(DEPTH, rows), ((share, 6 * DEPTH), jnp.bfloat16), (share // LANES, LANES), (share, LANES)],
            [self.own, mine, theirs],
            12 * DEPTH * share * size * rows,
        )
        self.terms.append(terms)
        self.slabs.append(slab)
        return token

    def work(self, value, axis, step):
        if not self.todo:
            return swap(value, axis, step)
        value, self.own = tie(value, self.own)
        other = swap(value, axis, step)
        other, _ = tie(other, self.piece())
        return other

    def finish(self, value):
        while self.steps or self.coming is not None:
            if self.coming is None:
                self.coming = swap(self.parts, "src", self.steps.pop(0))
            value = self.land(value)
        while len(self.theirs) < len(self.mine):
            value = self.trade(value)
        self.traded(value)
        while self.todo:
            self.piece()


def shards(sources, targets, pair_active, count_src, count_tgt):
    dims, rows = sources.shape
    cols = targets.shape[1]
    share = cols // lax.axis_size("src")
    column = (rows, LANES)
    by_row = (rows // LANES, LANES)
    by_col = (cols // LANES, LANES)
    pairs = rows * cols
    hbm = [pltpu.with_memory_space_constraint(x, pltpu.HBM) for x in (sources, targets, count_src, count_tgt)]
    n_half = -(-dims // 2)
    packed = -(-n_half * by_row[0] // 8) * 8
    outs = [(rows, cols), by_row, (3, *by_row), (3, *by_col), (DEPTH, share), (1, packed, LANES)]
    score, lse, row_aux, col_aux, own, half = pl.pallas_call(
        first_kernel,
        out_shape=[pltpu.VMEM(shape, jnp.float32) for shape in outs],
        in_specs=[pl.BlockSpec(memory_space=pltpu.HBM)] * 4 + [SMEM_SPEC],
        out_specs=[VMEM_SPEC] * len(outs),
        scratch_shapes=[
            pltpu.VMEM((dims, rows), jnp.float32),
            pltpu.VMEM((dims, cols), jnp.float32),
            pltpu.SMEM(count_src.shape, jnp.int32),
            pltpu.SMEM(count_tgt.shape, jnp.int32),
            pltpu.SemaphoreType.DMA((4,)),
            pltpu.VMEM((DEPTH, 512), jnp.float32),
            pltpu.VMEM((DEPTH, rows), jnp.float32),
            pltpu.VMEM((rows, 6 * DEPTH), jnp.bfloat16),
            pltpu.VMEM(by_row, jnp.float32),
            pltpu.VMEM(column, jnp.float32),
            pltpu.VMEM(column, jnp.float32),
            pltpu.VMEM(column, jnp.float32),
        ],
        compiler_params=pltpu.CompilerParams(vmem_limit_bytes=VMEM_LIMIT),
        cost_estimate=pl.CostEstimate(flops=12 * DEPTH * pairs, bytes_accessed=0, transcendentals=pairs),
    )(*hbm, pair_active)
    over_tgt = doubling(lax.axis_size("tgt"))
    over_src = doubling(lax.axis_size("src"))
    over_src = over_src[1:] + over_src[:1]
    side = Beside(half, own, over_src, rows, n_half)
    for step in range(ITERS):
        for bit in over_tgt:
            if step == ITERS - 1 and bit == over_tgt[0]:
                lse = side.trade(lse)
            if bit != over_tgt[-1]:
                other = swap(lse, "tgt", bit)
            elif step < ITERS - 1:
                other = side.start(lse, "tgt", bit)
            else:
                other = side.work(lse, "tgt", bit)
            lse = merge(lse, other)
        if step == ITERS - 2:
            lse = side.trade(lse)
        if step == 0:
            lse, base, masked, kernel, top = call(
                first_col_kernel,
                [by_col, by_row, by_row, (rows, cols), by_col],
                [column], [score, lse, row_aux], 0,
            )
        else:
            lse, f, masked = call(
                col_kernel,
                [by_col, by_row, by_row],
                [by_row, column], [score, kernel, top, base, lse, row_aux], 0,
            )
        if step < ITERS - 1:
            lse = side.traded(side.land(lse))
            lse = jnp.broadcast_to(lse, (lax.axis_size("src"), *by_col))
            lse = lax.all_to_all(lse, "src", 0, 0, tiled=True)
            (lse,) = call(
                row_kernel,
                [by_row],
                [by_col, by_col, column, column],
                [score, kernel, top, base, lse, row_aux, col_aux], 0,
            )
    lse = side.traded(lse)
    for bit in over_src:
        both = jnp.concatenate([lse, masked], axis=0)
        other = side.work(both, "src", bit)
        lse = merge(lse, other[: by_col[0]])
        masked = jnp.concatenate([masked, other[by_col[0] :]], axis=0)
    side.finish(lse)
    ancestors, f, g = call(
        functools.partial(last_kernel, pieces=len(side.slabs)),
        [(dims, share), by_row, by_col],
        [(share // LANES, LANES), (share, LANES), (share, 3 * DEPTH)],
        [*side.slabs, *side.terms, masked, lse, col_aux, f],
        18 * DEPTH * pairs, pairs, pin=False,
    )
    return (f.reshape(rows), g.reshape(cols), ancestors)


def solution(mesh):
    return jax.shard_map(
        shards,
        mesh=mesh,
        in_specs=(P(None, "src"), P(None, "tgt"), P("src", "tgt"), P(), P()),
        out_specs=(P("src"), P("tgt"), P(None, ("tgt", "src"))),
        check_vma=False,
    )
```

```python
import functools
import math

import jax
import jax.numpy as jnp
from jax import lax
from jax.experimental import pallas as pl
from jax.experimental.pallas import tpu as pltpu
from jax.sharding import PartitionSpec as P

ITERS = 4
EPS = 0.02
NEG = -1e30
LOG2E = math.log2(math.e)
SCALE = LOG2E / EPS
LANES = 128
DEPTH = 64
SHIFT = 40.0
ROW_FACTOR_MAX = 2.0**20
COL_FACTOR_MAX = 2.0**60
SUM_MIN = 2.0**-30
VMEM_LIMIT = 14 * 1024 * 1024

VMEM_SPEC = pl.BlockSpec(memory_space=pltpu.VMEM)
SMEM_SPEC = pl.BlockSpec(memory_space=pltpu.SMEM)


def pinned(x):
    return pltpu.with_memory_space_constraint(x, pltpu.VMEM)


def split(x):
    high = x.astype(jnp.bfloat16)
    rest = x - high.astype(jnp.float32)
    mid = rest.astype(jnp.bfloat16)
    low = (rest - mid.astype(jnp.float32)).astype(jnp.bfloat16)
    return high, mid, low


def put(ref, row):
    for k in range(row.shape[1] // LANES):
        ref[k : k + 1, :] = row[:, k * LANES : (k + 1) * LANES]


def positions(shape):
    return lax.broadcasted_iota(jnp.int32, shape, 0) * LANES + lax.broadcasted_iota(jnp.int32, shape, 1)


def to_sublanes(vector_ref, col_ref):
    for k in range(vector_ref.shape[0]):
        col_ref[k * LANES : (k + 1) * LANES, :] = jnp.broadcast_to(vector_ref[k : k + 1, :], (LANES, LANES)).T


def fold_lanes(peak_ref, total_ref, out_ref):
    for k in range(out_ref.shape[0]):
        here = slice(k * LANES, (k + 1) * LANES)
        peaks = peak_ref[here, :].T
        top = jnp.max(peaks, axis=0, keepdims=True)
        total = jnp.sum(total_ref[here, :].T * jnp.exp2(peaks - top), axis=0, keepdims=True)
        out_ref[k : k + 1, :] = top + jnp.log2(total)


def row_lse(score_ref, add_ref, peak_ref, total_ref, out_ref):
    rows, cols = score_ref.shape

    def block(i, _):
        here = pl.ds(pl.multiple_of(i * 8, 8), 8)
        z = []
        for k in range(cols // LANES):
            z.append(score_ref[here, k * LANES : (k + 1) * LANES] + add_ref[k : k + 1, :])
        peak = functools.reduce(jnp.maximum, z)
        peak_ref[here, :] = peak
        total_ref[here, :] = functools.reduce(jnp.add, [jnp.exp2(v - peak) for v in z])
        return 0

    lax.fori_loop(0, rows // 8, block, 0)
    fold_lanes(peak_ref, total_ref, out_ref)


def col_lse(score_ref, add_ref, out_ref, kernel_ref=None, top_ref=None):
    rows, cols = score_ref.shape
    group = 16
    tall = 4

    for first in range(0, cols // LANES, group):
        lanes = [slice((first + k) * LANES, (first + k + 1) * LANES) for k in range(group)]

        def peaks(i, tops):
            for r in range(tall):
                here = pl.ds(pl.multiple_of((i * tall + r) * 8, 8), 8)
                add = add_ref[here, :]
                tops = tuple(jnp.maximum(t, score_ref[here, s] + add) for t, s in zip(tops, lanes))
            return tops

        start = (jnp.full((8, LANES), -jnp.inf, jnp.float32),) * group
        tops = lax.fori_loop(0, rows // (8 * tall), peaks, start)
        tops = [jnp.max(t, axis=0, keepdims=True) - SHIFT for t in tops]
        wide_tops = [jnp.broadcast_to(t, (8, LANES)) for t in tops]

        def totals(i, sums):
            for r in range(tall):
                here = pl.ds(pl.multiple_of((i * tall + r) * 8, 8), 8)
                add = add_ref[here, :]
                terms = [jnp.exp2(score_ref[here, s] + (add - t)) for t, s in zip(wide_tops, lanes)]
                if kernel_ref is not None:
                    for s, t in zip(lanes, terms):
                        kernel_ref[here, s] = t
                sums = tuple(u + t for u, t in zip(sums, terms))
            return sums

        start = (jnp.zeros((8, LANES), jnp.float32),) * group
        sums = lax.fori_loop(0, rows // (8 * tall), totals, start)
        for k, (t, u) in enumerate(zip(tops, sums)):
            spot = slice(first + k, first + k + 1)
            if top_ref is not None:
                top_ref[spot, :] = t
            out_ref[spot, :] = t + jnp.log2(jnp.sum(u, axis=0, keepdims=True))


def source_terms(x):
    high, mid, low = split(x * (2.0 * SCALE))
    return [high, high, mid, mid, high, low]


def target_terms(y):
    high, mid, low = split(y)
    return [high, mid, high, mid, low, high]


def pad_into(pad_ref, values):
    pad_ref[...] = jnp.zeros(pad_ref.shape, jnp.float32)
    pad_ref[0 : values.shape[0], :] = values


def live_sum(counts):
    total = counts[0]
    for i in range(1, counts.shape[0]):
        total = total + counts[i]
    return jnp.full((1, LANES), total, jnp.int32).astype(jnp.float32)


def wide(x, size):
    return jnp.concatenate([x] * (size // LANES), axis=1)


def first_kernel(
    src_hbm, tgt_hbm, count_src_hbm, count_tgt_hbm, pair,
    score_ref, lse_ref, row_aux, col_aux, own_ref, half_ref,
    src_ref, tgt_ref, count_src, count_tgt, sems,
    right_pad, left_pad, terms_ref, norm_ref, col_ref, peak_ref, total_ref,
):
    rows, cols = score_ref.shape
    dims = src_ref.shape[0]
    copies = [
        pltpu.make_async_copy(one, two, sems.at[i])
        for i, (one, two) in enumerate(
            [(count_src_hbm, count_src), (count_tgt_hbm, count_tgt), (src_hbm, src_ref), (tgt_hbm, tgt_ref)]
        )
    ]
    for copy in copies:
        copy.start()
    for ref in (right_pad, left_pad, own_ref):
        ref[...] = jnp.zeros(ref.shape, jnp.float32)
    n_half = -(-dims // 2)
    for copy in copies[:3]:
        copy.wait()
    n_rows = count_src[lax.axis_index("src")]
    n_cols = count_tgt[lax.axis_index("tgt")]
    listed = pair[0, 0] > 0
    row_live = positions(row_aux.shape[1:]) < n_rows
    col_live = positions(col_aux.shape[1:]) < n_cols
    row_aux[0] = row_live.astype(jnp.float32)
    row_aux[1] = jnp.where(row_live, -jnp.log2(live_sum(count_src)), 0.0)
    row_aux[2] = (row_live & listed).astype(jnp.float32)
    col_aux[0] = col_live.astype(jnp.float32)
    col_aux[1] = jnp.where(col_live, -jnp.log2(live_sum(count_tgt)), 0.0)
    left_pad[0:dims, :] = src_ref[...]
    left = left_pad[...]
    half = jnp.where(lax.axis_index("tgt") % 2 == 0, left[0:n_half], left[n_half : 2 * n_half])
    half_ref[...] = jnp.zeros(half_ref.shape, jnp.float32)
    for k in range(rows // LANES):
        half_ref[0, k * n_half : (k + 1) * n_half, :] = half[:, k * LANES : (k + 1) * LANES]
    put(norm_ref, -SCALE * jnp.sum(left * left, axis=0, keepdims=True))
    norm_ref[...] = jnp.where(row_live, norm_ref[...], NEG)
    to_sublanes(norm_ref, col_ref)
    terms_ref[...] = jnp.concatenate(source_terms(left.T), axis=1)
    copies[3].wait()
    size = 512

    def scores(c):
        here = pl.ds(pl.multiple_of(c * size, size), size)
        right_pad[0:dims, :] = tgt_ref[:, here]
        right = right_pad[...]
        spot = lax.broadcasted_iota(jnp.int32, (1, size), 1) + c * size
        norm = -SCALE * jnp.sum(right * right, axis=0, keepdims=True)
        norm = jnp.where((spot < n_cols) & listed, norm, NEG)
        terms = jnp.concatenate(target_terms(right), axis=0)
        cross = jnp.dot(terms_ref[...], terms, preferred_element_type=jnp.float32)
        score = cross + (wide(col_ref[...], size) + norm)
        score_ref[:, here] = score
        return [score[:, k : k + LANES] for k in range(0, size, LANES)]

    peak_ref[...] = jnp.full(peak_ref.shape, 2.0 * NEG, jnp.float32)
    total_ref[...] = jnp.zeros(total_ref.shape, jnp.float32)

    def block(c, _):
        z = scores(c)
        before = peak_ref[...]
        peak = functools.reduce(jnp.maximum, z, before)
        total_ref[...] = functools.reduce(
            jnp.add, [jnp.exp2(v - peak) for v in z], total_ref[...] * jnp.exp2(before - peak)
        )
        peak_ref[...] = peak
        return 0

    lax.fori_loop(0, cols // size, block, 0)
    share = own_ref.shape[1]
    own_ref[0:dims, :] = tgt_ref[:, pl.ds(pl.multiple_of(lax.axis_index("src") * share, share), share)]
    fold_lanes(peak_ref, total_ref, lse_ref)


def slab_kernel(
    own_ref, mine_ref, theirs_ref, slab_ref, terms_out, token_ref, right_pad, terms_ref, norm_ref, col_ref,
    *, first, n_half,
):
    share = own_ref.shape[1]
    rows = right_pad.shape[1]
    left = own_ref[...]
    put(norm_ref, -SCALE * jnp.sum(left * left, axis=0, keepdims=True))
    to_sublanes(norm_ref, col_ref)
    terms_ref[...] = jnp.concatenate(target_terms(left.T), axis=1)
    even = lax.axis_index("tgt") % 2 == 0
    right_pad[...] = jnp.zeros(right_pad.shape, jnp.float32)
    for b in range(slab_ref.shape[1] // rows):
        mine, theirs = mine_ref[first + b], theirs_ref[first + b]
        upper = jnp.where(even, mine, theirs)
        lower = jnp.where(even, theirs, mine)
        for k in range(rows // LANES):
            here = slice(k * n_half, (k + 1) * n_half)
            right_pad[0:n_half, k * LANES : (k + 1) * LANES] = upper[here]
            right_pad[n_half : 2 * n_half, k * LANES : (k + 1) * LANES] = lower[here]
        right = right_pad[...]
        norm = -SCALE * jnp.sum(right * right, axis=0, keepdims=True)
        terms = jnp.concatenate(source_terms(right), axis=0)
        cross = jnp.dot(terms_ref[...], terms, preferred_element_type=jnp.float32)
        here = slice(b * rows, (b + 1) * rows)
        slab_ref[:, here] = cross + (wide(col_ref[...], rows) + norm)
        terms_out[here, :] = jnp.concatenate(split(right.T), axis=1)
    token_ref[...] = jnp.zeros(token_ref.shape, jnp.float32)


def row_sums(kernel_ref, factor_ref, total_ref, out_ref):
    rows, cols = kernel_ref.shape
    tall = 8

    def block(i, _):
        spots = [pl.ds(pl.multiple_of((i * tall + k) * 8, 8), 8) for k in range(tall)]
        sums = [jnp.zeros((8, LANES), jnp.float32)] * tall
        for t in range(cols // LANES):
            lanes = slice(t * LANES, (t + 1) * LANES)
            factor = jnp.broadcast_to(factor_ref[t : t + 1, :], (8, LANES))
            sums = [u + kernel_ref[s, lanes] * factor for u, s in zip(sums, spots)]
        for s, u in zip(spots, sums):
            total_ref[s, :] = u
        return 0

    lax.fori_loop(0, rows // (8 * tall), block, 0)
    for k in range(out_ref.shape[0]):
        out_ref[k : k + 1, :] = jnp.sum(total_ref[k * LANES : (k + 1) * LANES, :].T, axis=0, keepdims=True)


def col_sums(kernel_ref, factor_ref, out_ref):
    rows, cols = kernel_ref.shape
    lanes = [slice(start, start + LANES) for start in range(0, cols, LANES)]
    tall = 4

    def block(i, sums):
        for r in range(tall):
            here = pl.ds(pl.multiple_of((i * tall + r) * 8, 8), 8)
            factor = factor_ref[here, :]
            sums = tuple(u + kernel_ref[here, s] * factor for u, s in zip(sums, lanes))
        return sums

    sums = lax.fori_loop(0, rows // (8 * tall), block, (jnp.zeros((8, LANES), jnp.float32),) * len(lanes))
    for k, u in enumerate(sums):
        out_ref[k : k + 1, :] = jnp.sum(u, axis=0, keepdims=True)


def out_of_range(total, needed, factor, most):
    small = jnp.where(needed & jnp.logical_not(total >= SUM_MIN), 1.0, 0.0)
    large = jnp.where(factor <= most, 0.0, 1.0)
    return jnp.max(jnp.maximum(jnp.max(small, axis=0, keepdims=True), jnp.max(large, axis=0, keepdims=True))) > 0.5


def set_f(lse_ref, aux_ref, f_ref, masked_ref):
    f = aux_ref[1] - lse_ref[...] * aux_ref[0]
    f_ref[...] = f
    masked_ref[...] = jnp.where(aux_ref[2] > 0, f, NEG)


def first_col_kernel(score_ref, lse_ref, aux_ref, out_ref, f_ref, masked_ref, kernel_ref, top_ref, col_ref):
    set_f(lse_ref, aux_ref, f_ref, masked_ref)
    to_sublanes(f_ref, col_ref)
    col_lse(score_ref, col_ref, out_ref, kernel_ref, top_ref)


def col_kernel(
    score_ref, kernel_ref, top_ref, base_ref, lse_ref, aux_ref, out_ref, f_ref, masked_ref, factor_ref, col_ref
):
    set_f(lse_ref, aux_ref, f_ref, masked_ref)
    factor_ref[...] = jnp.exp2(f_ref[...] - base_ref[...])
    to_sublanes(factor_ref, col_ref)
    col_sums(kernel_ref, col_ref, out_ref)
    total = out_ref[...]
    top = top_ref[...]
    redo = out_of_range(total, top > 0.5 * NEG, factor_ref[...], ROW_FACTOR_MAX)
    out_ref[...] = jnp.where(total > 0, top + jnp.log2(total), NEG)

    @pl.when(redo)
    def _():
        to_sublanes(f_ref, col_ref)
        col_lse(score_ref, col_ref, out_ref)


def merged(parts):
    peak = jnp.max(parts, axis=0)
    return peak + jnp.log2(jnp.sum(jnp.exp2(parts - peak[None]), axis=0))


def row_kernel(
    score_ref, kernel_ref, top_ref, base_ref, parts_ref, row_aux, col_aux, out_ref,
    g_ref, factor_ref, peak_ref, total_ref,
):
    lse = merged(parts_ref[...])
    g_ref[...] = col_aux[1] - lse * col_aux[0]
    factor_ref[...] = jnp.where(col_aux[0] > 0, jnp.exp2(top_ref[...] - lse + 2.0 * SHIFT), 0.0)
    row_sums(kernel_ref, factor_ref, total_ref, out_ref)
    total = out_ref[...]
    redo = out_of_range(total, row_aux[2] > 0, factor_ref[...], COL_FACTOR_MAX)
    log_b = col_aux[1, 0:1, 0:1]
    out_ref[...] = jnp.where(total > 0, jnp.log2(total) - 2.0 * SHIFT - base_ref[...] + log_b, NEG)

    @pl.when(redo)
    def _():
        row_lse(score_ref, g_ref, peak_ref, total_ref, out_ref)


def last_kernel(*refs, pieces):
    slabs, refs = refs[: len(pieces)], refs[len(pieces) :]
    terms, refs = refs[: len(pieces)], refs[len(pieces) :]
    parts_ref, aux_ref, f_ref, *_, out_ref, f_out, g_out, lse_ref, own_ref, col_ref, sum_ref = refs
    n_col = aux_ref.shape[1]
    lse = merged(parts_ref[:, 0:n_col, :])
    lse_ref[...] = lse
    f_out[...] = f_ref[...] * (1.0 / SCALE)
    g_out[...] = (aux_ref[1] - lse * aux_ref[0]) * (1.0 / SCALE)
    me = lax.axis_index("src")
    n_own = own_ref.shape[0]
    for k in range(n_own):
        spot = pl.ds(me * n_own + k, 1)
        own_ref[k : k + 1, :] = jnp.where(aux_ref[0, spot, :] > 0, -lse_ref[spot, :], NEG)
    to_sublanes(own_ref, col_ref)
    for i, (slab_ref, terms_ref, offsets) in enumerate(zip(slabs, terms, pieces)):
        high, mid = [], []
        start = 0
        for offset in offsets:
            for row in range(n_col, parts_ref.shape[1]):
                add = col_ref[...] + parts_ref[me ^ offset, row : row + 1, :]
                term = split(jnp.exp2(slab_ref[:, start : start + LANES] + add))
                high.append(term[0])
                mid.append(term[1])
                start += LANES
        sums = jnp.dot(
            jnp.concatenate(high + mid, axis=1), jnp.concatenate([terms_ref[...]] * 2, axis=0),
            preferred_element_type=jnp.float32,
        )
        if i == 0:
            sum_ref[...] = sums
        else:
            sum_ref[...] += sums
    sums = sum_ref[...].T
    out_ref[...] = (sums[0:DEPTH] + sums[DEPTH : 2 * DEPTH] + sums[2 * DEPTH :])[0 : out_ref.shape[0]]


def merge(one, two):
    top = jnp.maximum(one, two)
    return top + jnp.log2(1.0 + jnp.exp2(jnp.minimum(one, two) - top))


def swap(value, axis, step):
    return lax.ppermute(value, axis, [(i, i ^ step) for i in range(lax.axis_size(axis))])


def doubling(size):
    return [1 << k for k in range(size.bit_length() - 1)]


def buffer(space, shape):
    return space(*shape) if isinstance(shape[0], tuple) else space(shape, jnp.float32)


def call(kernel, outs, scratch, ins, flops, expos=0, pin=True):
    return pl.pallas_call(
        kernel,
        out_shape=[buffer(pltpu.VMEM if pin else jax.ShapeDtypeStruct, shape) for shape in outs],
        in_specs=[VMEM_SPEC] * len(ins),
        out_specs=[VMEM_SPEC] * len(outs),
        scratch_shapes=[buffer(pltpu.VMEM, shape) for shape in scratch],
        compiler_params=pltpu.CompilerParams(vmem_limit_bytes=VMEM_LIMIT),
        cost_estimate=pl.CostEstimate(flops=flops, bytes_accessed=0, transcendentals=expos),
    )(*[pinned(x) for x in ins])


def tie(*values):
    return lax.optimization_barrier(values)


class Beside:
    def __init__(self, half, own, steps, rows, n_half):
        self.parts = half
        self.own = own
        self.steps = list(steps)
        self.coming = None
        self.come = None
        self.mine = []
        self.theirs = []
        self.ready = []
        self.todo = []
        self.terms = []
        self.tokens = []
        self.done = []
        self.offsets = [0]
        for bit in steps:
            self.offsets += [offset ^ bit for offset in self.offsets]
        self.rows = rows
        self.n_half = n_half
        self.slabs = []

    def launch(self):
        self.coming = swap(self.parts, "src", self.steps.pop(0))
        if not self.steps:
            self.mine = [self.parts]
            self.trade()

    def start(self, value, axis, step):
        if self.coming is not None or not self.steps:
            return swap(value, axis, step)
        value, self.parts = tie(value, self.parts)
        other = swap(value, axis, step)
        self.launch()
        return other

    def land(self, value):
        if self.coming is not None:
            value, self.come = tie(value, self.coming)
            self.coming = None
        return value

    def join(self, value):
        if self.come is None:
            return value
        value, parts, come = tie(value, self.parts, self.come)
        self.come = None
        if self.steps:
            self.parts = jnp.concatenate([parts, come], axis=0)
        else:
            self.mine.append(come)
            self.trade()
        return value

    def trade(self):
        self.theirs.append(swap(self.mine[-1], "tgt", 1))

    def traded(self, value):
        for group in range(len(self.ready), len(self.theirs)):
            value, self.theirs[group] = tie(value, self.theirs[group])
            self.ready.append(group)
            size = max(self.mine[group].shape[0] // 2, 1)
            self.todo += [(group, first, size) for first in range(0, self.mine[group].shape[0], size)]
        return value

    def piece(self):
        group, first, size = self.todo.pop(0)
        mine, theirs = self.mine[group], self.theirs[group]
        share = self.own.shape[1]
        rows = self.rows
        slab, terms, token = call(
            functools.partial(slab_kernel, first=first, n_half=self.n_half),
            [(share, size * rows), ((size * rows, 3 * DEPTH), jnp.bfloat16), (8, LANES)],
            [(DEPTH, rows), ((share, 6 * DEPTH), jnp.bfloat16), (share // LANES, LANES), (share, LANES)],
            [self.own, mine, theirs],
            12 * DEPTH * share * size * rows,
        )
        self.terms.append(terms)
        self.done.append(self.offsets[group * mine.shape[0] + first :][:size])
        self.slabs.append(slab)
        return token

    def work(self, value, axis, step):
        if not self.todo:
            return swap(value, axis, step)
        value, self.own = tie(value, self.own)
        return self.pieces(swap(value, axis, step))

    def pieces(self, value):
        while self.todo:
            value, token = tie(value, self.piece())
            self.tokens.append(token)
        return value

    def finish(self, value):
        while self.steps or self.coming is not None or self.come is not None:
            if self.coming is None and self.come is None:
                self.launch()
            value = self.join(self.land(value))
        return self.pieces(self.traded(value))


def shards(sources, targets, pair_active, count_src, count_tgt):
    dims, rows = sources.shape
    cols = targets.shape[1]
    n_src = lax.axis_size("src")
    share = cols // n_src
    column = (rows, LANES)
    by_row = (rows // LANES, LANES)
    by_col = (cols // LANES, LANES)
    pairs = rows * cols
    hbm = [pltpu.with_memory_space_constraint(x, pltpu.HBM) for x in (sources, targets, count_src, count_tgt)]
    n_half = -(-dims // 2)
    packed = -(-n_half * by_row[0] // 8) * 8
    outs = [(rows, cols), by_row, (3, *by_row), (3, *by_col), (DEPTH, share), (1, packed, LANES)]
    score, lse, row_aux, col_aux, own, half = pl.pallas_call(
        first_kernel,
        out_shape=[pltpu.VMEM(shape, jnp.float32) for shape in outs],
        in_specs=[pl.BlockSpec(memory_space=pltpu.HBM)] * 4 + [SMEM_SPEC],
        out_specs=[VMEM_SPEC] * len(outs),
        scratch_shapes=[
            pltpu.VMEM((dims, rows), jnp.float32),
            pltpu.VMEM((dims, cols), jnp.float32),
            pltpu.SMEM(count_src.shape, jnp.int32),
            pltpu.SMEM(count_tgt.shape, jnp.int32),
            pltpu.SemaphoreType.DMA((4,)),
            pltpu.VMEM((DEPTH, 512), jnp.float32),
            pltpu.VMEM((DEPTH, rows), jnp.float32),
            pltpu.VMEM((rows, 6 * DEPTH), jnp.bfloat16),
            pltpu.VMEM(by_row, jnp.float32),
            pltpu.VMEM(column, jnp.float32),
            pltpu.VMEM(column, jnp.float32),
            pltpu.VMEM(column, jnp.float32),
        ],
        compiler_params=pltpu.CompilerParams(vmem_limit_bytes=VMEM_LIMIT),
        cost_estimate=pl.CostEstimate(flops=12 * DEPTH * pairs, bytes_accessed=0, transcendentals=pairs),
    )(*hbm, pair_active)
    over_tgt = doubling(lax.axis_size("tgt"))
    over_src = doubling(n_src)
    over_src = over_src[1:] + over_src[:1]
    side = Beside(half, own, over_src, rows, n_half)
    for step in range(ITERS):
        lse = side.join(lse)
        for bit in over_tgt:
            if bit != over_tgt[-1]:
                other = swap(lse, "tgt", bit)
            elif step < ITERS - 1:
                other = side.start(lse, "tgt", bit)
            else:
                other = side.work(side.traded(lse), "tgt", bit)
            lse = merge(lse, other)
        lse = side.traded(lse)
        if step == 0:
            lse, base, masked, kernel, top = call(
                first_col_kernel,
                [by_col, by_row, by_row, (rows, cols), by_col],
                [column], [score, lse, row_aux], 0,
            )
        else:
            lse, f, masked = call(
                col_kernel,
                [by_col, by_row, by_row],
                [by_row, column], [score, kernel, top, base, lse, row_aux], 0,
            )
        if step < ITERS - 1:
            lse = side.land(side.pieces(lse))
            lse = lax.all_to_all(jnp.broadcast_to(lse, (n_src, *by_col)), "src", 0, 0, tiled=True)
            (lse,) = call(
                row_kernel,
                [by_row],
                [by_col, by_col, column, column],
                [score, kernel, top, base, lse, row_aux, col_aux], 0,
            )
    lse = side.finish(lse)
    both = jnp.concatenate([lse, masked], axis=0)
    both = lax.all_to_all(jnp.broadcast_to(both, (n_src, *both.shape)), "src", 0, 0, tiled=True)
    ancestors, f, g = call(
        functools.partial(last_kernel, pieces=side.done),
        [(dims, share), by_row, by_col],
        [by_col, (share // LANES, LANES), (share, LANES), (share, 3 * DEPTH)],
        [*side.slabs, *side.terms, both, col_aux, f, *side.tokens],
        18 * DEPTH * pairs, pairs, pin=False,
    )
    return (f.reshape(rows), g.reshape(cols), ancestors)


def solution(mesh):
    return jax.shard_map(
        shards,
        mesh=mesh,
        in_specs=(P(None, "src"), P(None, "tgt"), P("src", "tgt"), P(), P()),
        out_specs=(P("src"), P("tgt"), P(None, ("tgt", "src"))),
        check_vma=False,
    )
```

```python
import functools
import math

import jax
import jax.numpy as jnp
from jax import lax
from jax.experimental import pallas as pl
from jax.experimental.pallas import tpu as pltpu
from jax.sharding import PartitionSpec as P

ITERS = 4
EPS = 0.02
NEG = -1e30
LOG2E = math.log2(math.e)
SCALE = LOG2E / EPS
LANES = 128
DEPTH = 64
SHIFT = 40.0
ROW_FACTOR_MAX = 2.0**20
COL_FACTOR_MAX = 2.0**60
SUM_MIN = 2.0**-30
VMEM_LIMIT = 14 * 1024 * 1024

VMEM_SPEC = pl.BlockSpec(memory_space=pltpu.VMEM)
SMEM_SPEC = pl.BlockSpec(memory_space=pltpu.SMEM)


def pinned(x):
    return pltpu.with_memory_space_constraint(x, pltpu.VMEM)


def split(x):
    high = x.astype(jnp.bfloat16)
    rest = x - high.astype(jnp.float32)
    mid = rest.astype(jnp.bfloat16)
    low = (rest - mid.astype(jnp.float32)).astype(jnp.bfloat16)
    return high, mid, low


def put(ref, row):
    for k in range(row.shape[1] // LANES):
        ref[k : k + 1, :] = row[:, k * LANES : (k + 1) * LANES]


def positions(shape):
    return lax.broadcasted_iota(jnp.int32, shape, 0) * LANES + lax.broadcasted_iota(jnp.int32, shape, 1)


def to_sublanes(vector_ref, col_ref):
    for k in range(vector_ref.shape[0]):
        col_ref[k * LANES : (k + 1) * LANES, :] = jnp.broadcast_to(vector_ref[k : k + 1, :], (LANES, LANES)).T


def fold_lanes(peak_ref, total_ref, out_ref):
    for k in range(out_ref.shape[0]):
        here = slice(k * LANES, (k + 1) * LANES)
        peaks = peak_ref[here, :].T
        top = jnp.max(peaks, axis=0, keepdims=True)
        total = jnp.sum(total_ref[here, :].T * jnp.exp2(peaks - top), axis=0, keepdims=True)
        out_ref[k : k + 1, :] = top + jnp.log2(total)


def row_lse(score_ref, add_ref, peak_ref, total_ref, out_ref):
    rows, cols = score_ref.shape

    def block(i, _):
        here = pl.ds(pl.multiple_of(i * 8, 8), 8)
        z = []
        for k in range(cols // LANES):
            z.append(score_ref[here, k * LANES : (k + 1) * LANES] + add_ref[k : k + 1, :])
        peak = functools.reduce(jnp.maximum, z)
        peak_ref[here, :] = peak
        total_ref[here, :] = functools.reduce(jnp.add, [jnp.exp2(v - peak) for v in z])
        return 0

    lax.fori_loop(0, rows // 8, block, 0)
    fold_lanes(peak_ref, total_ref, out_ref)


def col_lse(score_ref, add_ref, out_ref, kernel_ref=None, top_ref=None):
    rows, cols = score_ref.shape
    group = 16
    tall = 4

    for first in range(0, cols // LANES, group):
        lanes = [slice((first + k) * LANES, (first + k + 1) * LANES) for k in range(group)]

        def peaks(i, tops):
            for r in range(tall):
                here = pl.ds(pl.multiple_of((i * tall + r) * 8, 8), 8)
                add = add_ref[here, :]
                tops = tuple(jnp.maximum(t, score_ref[here, s] + add) for t, s in zip(tops, lanes))
            return tops

        start = (jnp.full((8, LANES), -jnp.inf, jnp.float32),) * group
        tops = lax.fori_loop(0, rows // (8 * tall), peaks, start)
        tops = [jnp.max(t, axis=0, keepdims=True) - SHIFT for t in tops]
        wide_tops = [jnp.broadcast_to(t, (8, LANES)) for t in tops]

        def totals(i, sums):
            for r in range(tall):
                here = pl.ds(pl.multiple_of((i * tall + r) * 8, 8), 8)
                add = add_ref[here, :]
                terms = [jnp.exp2(score_ref[here, s] + (add - t)) for t, s in zip(wide_tops, lanes)]
                if kernel_ref is not None:
                    for s, t in zip(lanes, terms):
                        kernel_ref[here, s] = t
                sums = tuple(u + t for u, t in zip(sums, terms))
            return sums

        start = (jnp.zeros((8, LANES), jnp.float32),) * group
        sums = lax.fori_loop(0, rows // (8 * tall), totals, start)
        for k, (t, u) in enumerate(zip(tops, sums)):
            spot = slice(first + k, first + k + 1)
            if top_ref is not None:
                top_ref[spot, :] = t
            out_ref[spot, :] = t + jnp.log2(jnp.sum(u, axis=0, keepdims=True))


def source_terms(x):
    high, mid, low = split(x * (2.0 * SCALE))
    return [high, high, mid, mid, high, low]


def target_terms(y):
    high, mid, low = split(y)
    return [high, mid, high, mid, low, high]


def pad_into(pad_ref, values):
    pad_ref[...] = jnp.zeros(pad_ref.shape, jnp.float32)
    pad_ref[0 : values.shape[0], :] = values


def live_sum(counts):
    total = counts[0]
    for i in range(1, counts.shape[0]):
        total = total + counts[i]
    return jnp.full((1, LANES), total, jnp.int32).astype(jnp.float32)


def wide(x, size):
    return jnp.concatenate([x] * (size // LANES), axis=1)


def first_kernel(
    src_hbm, tgt_hbm, count_src_hbm, count_tgt_hbm, pair,
    score_ref, lse_ref, row_aux, col_aux, own_ref, half_ref,
    src_ref, tgt_ref, count_src, count_tgt, sems,
    right_pad, left_pad, terms_ref, norm_ref, col_ref, peak_ref, total_ref,
):
    rows, cols = score_ref.shape
    dims = src_ref.shape[0]
    copies = [
        pltpu.make_async_copy(one, two, sems.at[i])
        for i, (one, two) in enumerate(
            [(count_src_hbm, count_src), (count_tgt_hbm, count_tgt), (src_hbm, src_ref), (tgt_hbm, tgt_ref)]
        )
    ]
    for copy in copies:
        copy.start()
    for ref in (right_pad, left_pad, own_ref):
        ref[...] = jnp.zeros(ref.shape, jnp.float32)
    n_half = -(-dims // 2)
    for copy in copies[:3]:
        copy.wait()
    n_rows = count_src[lax.axis_index("src")]
    n_cols = count_tgt[lax.axis_index("tgt")]
    listed = pair[0, 0] > 0
    row_live = positions(row_aux.shape[1:]) < n_rows
    col_live = positions(col_aux.shape[1:]) < n_cols
    row_aux[0] = row_live.astype(jnp.float32)
    row_aux[1] = jnp.where(row_live, -jnp.log2(live_sum(count_src)), 0.0)
    row_aux[2] = (row_live & listed).astype(jnp.float32)
    col_aux[0] = col_live.astype(jnp.float32)
    col_aux[1] = jnp.where(col_live, -jnp.log2(live_sum(count_tgt)), 0.0)
    left_pad[0:dims, :] = src_ref[...]
    left = left_pad[...]
    half = jnp.where(lax.axis_index("tgt") % 2 == 0, left[0:n_half], left[n_half : 2 * n_half])
    half_ref[...] = jnp.zeros(half_ref.shape, jnp.float32)
    for k in range(rows // LANES):
        half_ref[0, k * n_half : (k + 1) * n_half, :] = half[:, k * LANES : (k + 1) * LANES]
    put(norm_ref, -SCALE * jnp.sum(left * left, axis=0, keepdims=True))
    norm_ref[...] = jnp.where(row_live, norm_ref[...], NEG)
    to_sublanes(norm_ref, col_ref)
    terms_ref[...] = jnp.concatenate(source_terms(left.T), axis=1)
    copies[3].wait()
    size = 512

    def scores(c):
        here = pl.ds(pl.multiple_of(c * size, size), size)
        right_pad[0:dims, :] = tgt_ref[:, here]
        right = right_pad[...]
        spot = lax.broadcasted_iota(jnp.int32, (1, size), 1) + c * size
        norm = -SCALE * jnp.sum(right * right, axis=0, keepdims=True)
        norm = jnp.where((spot < n_cols) & listed, norm, NEG)
        terms = jnp.concatenate(target_terms(right), axis=0)
        cross = jnp.dot(terms_ref[...], terms, preferred_element_type=jnp.float32)
        score_ref[:, here] = cross + (wide(col_ref[...], size) + norm)

    peak_ref[...] = jnp.full(peak_ref.shape, 2.0 * NEG, jnp.float32)
    total_ref[...] = jnp.zeros(total_ref.shape, jnp.float32)

    def sums(c):
        here = pl.ds(pl.multiple_of(c * size, size), size)
        z = score_ref[:, here]
        z = [z[:, k : k + LANES] for k in range(0, size, LANES)]
        before = peak_ref[...]
        peak = functools.reduce(jnp.maximum, z, before)
        total_ref[...] = functools.reduce(
            jnp.add, [jnp.exp2(v - peak) for v in z], total_ref[...] * jnp.exp2(before - peak)
        )
        peak_ref[...] = peak

    def block(c, _):
        sums(c - 1)
        scores(c)
        return 0

    scores(0)
    lax.fori_loop(1, cols // size, block, 0)
    sums(cols // size - 1)
    share = own_ref.shape[1]
    own_ref[0:dims, :] = tgt_ref[:, pl.ds(pl.multiple_of(lax.axis_index("src") * share, share), share)]
    fold_lanes(peak_ref, total_ref, lse_ref)


def slab_kernel(
    own_ref, mine_ref, theirs_ref, slab_ref, terms_out, token_ref, right_pad, terms_ref, norm_ref, col_ref,
    *, first, n_half,
):
    share = own_ref.shape[1]
    rows = right_pad.shape[1]
    left = own_ref[...]
    put(norm_ref, -SCALE * jnp.sum(left * left, axis=0, keepdims=True))
    to_sublanes(norm_ref, col_ref)
    terms_ref[...] = jnp.concatenate(target_terms(left.T), axis=1)
    even = lax.axis_index("tgt") % 2 == 0
    right_pad[...] = jnp.zeros(right_pad.shape, jnp.float32)
    for b in range(slab_ref.shape[1] // rows):
        mine, theirs = mine_ref[first + b], theirs_ref[first + b]
        upper = jnp.where(even, mine, theirs)
        lower = jnp.where(even, theirs, mine)
        for k in range(rows // LANES):
            here = slice(k * n_half, (k + 1) * n_half)
            right_pad[0:n_half, k * LANES : (k + 1) * LANES] = upper[here]
            right_pad[n_half : 2 * n_half, k * LANES : (k + 1) * LANES] = lower[here]
        right = right_pad[...]
        norm = -SCALE * jnp.sum(right * right, axis=0, keepdims=True)
        terms = jnp.concatenate(source_terms(right), axis=0)
        cross = jnp.dot(terms_ref[...], terms, preferred_element_type=jnp.float32)
        here = slice(b * rows, (b + 1) * rows)
        slab_ref[:, here] = cross + (wide(col_ref[...], rows) + norm)
        terms_out[here, :] = jnp.concatenate(split(right.T), axis=1)
    token_ref[...] = jnp.zeros(token_ref.shape, jnp.float32)


def row_sums(kernel_ref, factor_ref, total_ref, out_ref):
    rows, cols = kernel_ref.shape
    tall = 8

    def block(i, _):
        spots = [pl.ds(pl.multiple_of((i * tall + k) * 8, 8), 8) for k in range(tall)]
        sums = [jnp.zeros((8, LANES), jnp.float32)] * tall
        for t in range(cols // LANES):
            lanes = slice(t * LANES, (t + 1) * LANES)
            factor = jnp.broadcast_to(factor_ref[t : t + 1, :], (8, LANES))
            sums = [u + kernel_ref[s, lanes] * factor for u, s in zip(sums, spots)]
        for s, u in zip(spots, sums):
            total_ref[s, :] = u
        return 0

    lax.fori_loop(0, rows // (8 * tall), block, 0)
    for k in range(out_ref.shape[0]):
        out_ref[k : k + 1, :] = jnp.sum(total_ref[k * LANES : (k + 1) * LANES, :].T, axis=0, keepdims=True)


def col_sums(kernel_ref, factor_ref, out_ref):
    rows, cols = kernel_ref.shape
    lanes = [slice(start, start + LANES) for start in range(0, cols, LANES)]
    tall = 4

    def block(i, sums):
        for r in range(tall):
            here = pl.ds(pl.multiple_of((i * tall + r) * 8, 8), 8)
            factor = factor_ref[here, :]
            sums = tuple(u + kernel_ref[here, s] * factor for u, s in zip(sums, lanes))
        return sums

    sums = lax.fori_loop(0, rows // (8 * tall), block, (jnp.zeros((8, LANES), jnp.float32),) * len(lanes))
    for k, u in enumerate(sums):
        out_ref[k : k + 1, :] = jnp.sum(u, axis=0, keepdims=True)


def out_of_range(total, needed, factor, most):
    small = jnp.where(needed & jnp.logical_not(total >= SUM_MIN), 1.0, 0.0)
    large = jnp.where(factor <= most, 0.0, 1.0)
    return jnp.max(jnp.maximum(jnp.max(small, axis=0, keepdims=True), jnp.max(large, axis=0, keepdims=True))) > 0.5


def set_f(lse_ref, aux_ref, f_ref, masked_ref):
    f = aux_ref[1] - lse_ref[...] * aux_ref[0]
    f_ref[...] = f
    masked_ref[...] = jnp.where(aux_ref[2] > 0, f, NEG)


def first_col_kernel(score_ref, lse_ref, aux_ref, out_ref, f_ref, masked_ref, kernel_ref, top_ref, col_ref):
    set_f(lse_ref, aux_ref, f_ref, masked_ref)
    to_sublanes(f_ref, col_ref)
    col_lse(score_ref, col_ref, out_ref, kernel_ref, top_ref)


def col_kernel(
    score_ref, kernel_ref, top_ref, base_ref, lse_ref, aux_ref, out_ref, f_ref, masked_ref, factor_ref, col_ref
):
    set_f(lse_ref, aux_ref, f_ref, masked_ref)
    factor_ref[...] = jnp.exp2(f_ref[...] - base_ref[...])
    to_sublanes(factor_ref, col_ref)
    col_sums(kernel_ref, col_ref, out_ref)
    total = out_ref[...]
    top = top_ref[...]
    redo = out_of_range(total, top > 0.5 * NEG, factor_ref[...], ROW_FACTOR_MAX)
    out_ref[...] = jnp.where(total > 0, top + jnp.log2(total), NEG)

    @pl.when(redo)
    def _():
        to_sublanes(f_ref, col_ref)
        col_lse(score_ref, col_ref, out_ref)


def merged(parts):
    peak = jnp.max(parts, axis=0)
    return peak + jnp.log2(jnp.sum(jnp.exp2(parts - peak[None]), axis=0))


def row_kernel(
    score_ref, kernel_ref, top_ref, base_ref, parts_ref, row_aux, col_aux, out_ref,
    g_ref, factor_ref, peak_ref, total_ref,
):
    lse = merged(parts_ref[...])
    g_ref[...] = col_aux[1] - lse * col_aux[0]
    factor_ref[...] = jnp.where(col_aux[0] > 0, jnp.exp2(top_ref[...] - lse + 2.0 * SHIFT), 0.0)
    row_sums(kernel_ref, factor_ref, total_ref, out_ref)
    total = out_ref[...]
    redo = out_of_range(total, row_aux[2] > 0, factor_ref[...], COL_FACTOR_MAX)
    log_b = col_aux[1, 0:1, 0:1]
    out_ref[...] = jnp.where(total > 0, jnp.log2(total) - 2.0 * SHIFT - base_ref[...] + log_b, NEG)

    @pl.when(redo)
    def _():
        row_lse(score_ref, g_ref, peak_ref, total_ref, out_ref)


def last_kernel(*refs, pieces):
    slabs, refs = refs[: len(pieces)], refs[len(pieces) :]
    terms, refs = refs[: len(pieces)], refs[len(pieces) :]
    parts_ref, aux_ref, f_ref, *_, out_ref, f_out, g_out, lse_ref, own_ref, col_ref, sum_ref = refs
    n_col = aux_ref.shape[1]
    lse = merged(parts_ref[:, 0:n_col, :])
    lse_ref[...] = lse
    f_out[...] = f_ref[...] * (1.0 / SCALE)
    g_out[...] = (aux_ref[1] - lse * aux_ref[0]) * (1.0 / SCALE)
    me = lax.axis_index("src")
    n_own = own_ref.shape[0]
    for k in range(n_own):
        spot = pl.ds(me * n_own + k, 1)
        own_ref[k : k + 1, :] = jnp.where(aux_ref[0, spot, :] > 0, -lse_ref[spot, :], NEG)
    to_sublanes(own_ref, col_ref)
    for i, (slab_ref, terms_ref, offsets) in enumerate(zip(slabs, terms, pieces)):
        high, mid = [], []
        start = 0
        for offset in offsets:
            for row in range(n_col, parts_ref.shape[1]):
                add = col_ref[...] + parts_ref[me ^ offset, row : row + 1, :]
                term = split(jnp.exp2(slab_ref[:, start : start + LANES] + add))
                high.append(term[0])
                mid.append(term[1])
                start += LANES
        sums = jnp.dot(
            jnp.concatenate(high + mid, axis=1), jnp.concatenate([terms_ref[...]] * 2, axis=0),
            preferred_element_type=jnp.float32,
        )
        if i == 0:
            sum_ref[...] = sums
        else:
            sum_ref[...] += sums
    sums = sum_ref[...].T
    out_ref[...] = (sums[0:DEPTH] + sums[DEPTH : 2 * DEPTH] + sums[2 * DEPTH :])[0 : out_ref.shape[0]]


def merge(one, two):
    top = jnp.maximum(one, two)
    return top + jnp.log2(1.0 + jnp.exp2(jnp.minimum(one, two) - top))


def swap(value, axis, step):
    return lax.ppermute(value, axis, [(i, i ^ step) for i in range(lax.axis_size(axis))])


def doubling(size):
    return [1 << k for k in range(size.bit_length() - 1)]


def buffer(space, shape):
    return space(*shape) if isinstance(shape[0], tuple) else space(shape, jnp.float32)


def call(kernel, outs, scratch, ins, flops, expos=0, pin=True):
    return pl.pallas_call(
        kernel,
        out_shape=[buffer(pltpu.VMEM if pin else jax.ShapeDtypeStruct, shape) for shape in outs],
        in_specs=[VMEM_SPEC] * len(ins),
        out_specs=[VMEM_SPEC] * len(outs),
        scratch_shapes=[buffer(pltpu.VMEM, shape) for shape in scratch],
        compiler_params=pltpu.CompilerParams(vmem_limit_bytes=VMEM_LIMIT),
        cost_estimate=pl.CostEstimate(flops=flops, bytes_accessed=0, transcendentals=expos),
    )(*[pinned(x) for x in ins])


def tie(*values):
    return lax.optimization_barrier(values)


class Beside:
    def __init__(self, half, own, steps, rows, n_half):
        self.parts = half
        self.own = own
        self.steps = list(steps)
        self.coming = None
        self.come = None
        self.mine = []
        self.theirs = []
        self.ready = 0
        self.todo = []
        self.terms = []
        self.tokens = []
        self.done = []
        self.offsets = [0]
        for bit in steps:
            self.offsets += [offset ^ bit for offset in self.offsets]
        self.rows = rows
        self.n_half = n_half
        self.slabs = []

    def launch(self):
        self.coming = swap(self.parts, "src", self.steps.pop(0))
        if not self.steps:
            self.mine = [self.parts]
            self.trade()

    def start(self, value, exchange):
        if self.coming is not None or not self.steps:
            return exchange(value)
        others = exchange(value)
        self.launch()
        return others

    def land(self, value):
        if self.coming is not None:
            value, self.come = tie(value, self.coming)
            self.coming = None
        return value

    def join(self, value):
        if self.come is None:
            return value
        value, parts, come = tie(value, self.parts, self.come)
        self.come = None
        if self.steps:
            self.parts = jnp.concatenate([parts, come], axis=0)
        else:
            self.mine.append(come)
            self.trade()
        return value

    def trade(self):
        self.theirs.append(swap(self.mine[-1], "tgt", 1))

    def traded(self, value):
        for group in range(len(self.theirs)):
            value, self.theirs[group] = tie(value, self.theirs[group])
        return self.listed(value)

    def listed(self, value):
        for group in range(self.ready, len(self.theirs)):
            size = max(self.mine[group].shape[0] // 2, 1)
            self.todo += [(group, first, size) for first in range(0, self.mine[group].shape[0], size)]
        self.ready = len(self.theirs)
        return value

    def piece(self):
        group, first, size = self.todo.pop(0)
        mine, theirs = self.mine[group], self.theirs[group]
        share = self.own.shape[1]
        rows = self.rows
        slab, terms, token = call(
            functools.partial(slab_kernel, first=first, n_half=self.n_half),
            [(share, size * rows), ((size * rows, 3 * DEPTH), jnp.bfloat16), (8, LANES)],
            [(DEPTH, rows), ((share, 6 * DEPTH), jnp.bfloat16), (share // LANES, LANES), (share, LANES)],
            [self.own, mine, theirs],
            12 * DEPTH * share * size * rows,
        )
        self.terms.append(terms)
        self.done.append(self.offsets[group * mine.shape[0] + first :][:size])
        self.slabs.append(slab)
        return token

    def work(self, value, exchange):
        if not self.todo:
            return exchange(value)
        value, self.own = tie(value, self.own)
        others = exchange(value)
        others[0] = self.pieces(others[0])
        return others

    def pieces(self, value):
        while self.todo:
            value, token = tie(value, self.piece())
            self.tokens.append(token)
        return value

    def finish(self, value):
        while self.steps or self.coming is not None or self.come is not None:
            if self.coming is None and self.come is None:
                self.launch()
            value = self.join(self.land(value))
        return self.pieces(self.traded(value))


def shards(sources, targets, pair_active, count_src, count_tgt):
    dims, rows = sources.shape
    cols = targets.shape[1]
    n_src = lax.axis_size("src")
    share = cols // n_src
    column = (rows, LANES)
    by_row = (rows // LANES, LANES)
    by_col = (cols // LANES, LANES)
    pairs = rows * cols
    hbm = [pltpu.with_memory_space_constraint(x, pltpu.HBM) for x in (sources, targets, count_src, count_tgt)]
    n_half = -(-dims // 2)
    packed = -(-n_half * by_row[0] // 8) * 8
    outs = [(rows, cols), by_row, (3, *by_row), (3, *by_col), (DEPTH, share), (1, packed, LANES)]
    score, lse, row_aux, col_aux, own, half = pl.pallas_call(
        first_kernel,
        out_shape=[pltpu.VMEM(shape, jnp.float32) for shape in outs],
        in_specs=[pl.BlockSpec(memory_space=pltpu.HBM)] * 4 + [SMEM_SPEC],
        out_specs=[VMEM_SPEC] * len(outs),
        scratch_shapes=[
            pltpu.VMEM((dims, rows), jnp.float32),
            pltpu.VMEM((dims, cols), jnp.float32),
            pltpu.SMEM(count_src.shape, jnp.int32),
            pltpu.SMEM(count_tgt.shape, jnp.int32),
            pltpu.SemaphoreType.DMA((4,)),
            pltpu.VMEM((DEPTH, 512), jnp.float32),
            pltpu.VMEM((DEPTH, rows), jnp.float32),
            pltpu.VMEM((rows, 6 * DEPTH), jnp.bfloat16),
            pltpu.VMEM(by_row, jnp.float32),
            pltpu.VMEM(column, jnp.float32),
            pltpu.VMEM(column, jnp.float32),
            pltpu.VMEM(column, jnp.float32),
        ],
        compiler_params=pltpu.CompilerParams(vmem_limit_bytes=VMEM_LIMIT),
        cost_estimate=pl.CostEstimate(flops=12 * DEPTH * pairs, bytes_accessed=0, transcendentals=pairs),
    )(*hbm, pair_active)
    over_tgt = doubling(lax.axis_size("tgt"))
    over_src = doubling(n_src)
    over_src = over_src[1:] + over_src[:1]
    side = Beside(half, own, over_src, rows, n_half)
    near = [bit for bit in (2, 3, 1) if bit < lax.axis_size("tgt")]

    def exchange(value):
        return [swap(value, "tgt", bit) for bit in near]

    def combine(value, others):
        values = dict(zip(near, others))
        value = merge(value, values[1])
        return merge(value, merge(values[2], values[3])) if 2 in values else value

    for step in range(ITERS):
        lse = side.join(lse)
        if step < ITERS - 1:
            others = side.start(lse, exchange)
        else:
            others = side.work(side.listed(lse), exchange)
        lse = combine(lse, others)
        for bit in over_tgt[2:]:
            lse = merge(lse, swap(lse, "tgt", bit))
        if step == ITERS - 2:
            lse = side.traded(lse)
        if step == 0:
            lse, base, masked, kernel, top = call(
                first_col_kernel,
                [by_col, by_row, by_row, (rows, cols), by_col],
                [column], [score, lse, row_aux], 0,
            )
        else:
            lse, f, masked = call(
                col_kernel,
                [by_col, by_row, by_row],
                [by_row, column], [score, kernel, top, base, lse, row_aux], 0,
            )
        if step < ITERS - 1:
            lse = side.land(side.pieces(lse))
            lse = lax.all_to_all(jnp.broadcast_to(lse, (n_src, *by_col)), "src", 0, 0, tiled=True)
            (lse,) = call(
                row_kernel,
                [by_row],
                [by_col, by_col, column, column],
                [score, kernel, top, base, lse, row_aux, col_aux], 0,
            )
    lse = side.finish(lse)
    both = jnp.concatenate([lse, masked], axis=0)
    both = lax.all_to_all(jnp.broadcast_to(both, (n_src, *both.shape)), "src", 0, 0, tiled=True)
    ancestors, f, g = call(
        functools.partial(last_kernel, pieces=side.done),
        [(dims, share), by_row, by_col],
        [by_col, (share // LANES, LANES), (share, LANES), (share, 3 * DEPTH)],
        [*side.slabs, *side.terms, both, col_aux, f, *side.tokens],
        18 * DEPTH * pairs, pairs, pin=False,
    )
    return (f.reshape(rows), g.reshape(cols), ancestors)


def solution(mesh):
    return jax.shard_map(
        shards,
        mesh=mesh,
        in_specs=(P(None, "src"), P(None, "tgt"), P("src", "tgt"), P(), P()),
        out_specs=(P("src"), P("tgt"), P(None, ("tgt", "src"))),
        check_vma=False,
    )
```

```python
import functools
import math

import jax
import jax.numpy as jnp
from jax import lax
from jax.experimental import pallas as pl
from jax.experimental.pallas import tpu as pltpu
from jax.sharding import PartitionSpec as P

ITERS = 4
EPS = 0.02
NEG = -1e30
LOG2E = math.log2(math.e)
SCALE = LOG2E / EPS
LANES = 128
DEPTH = 64
SHIFT = 40.0
ROW_FACTOR_MAX = 2.0**20
COL_FACTOR_MAX = 2.0**60
SUM_MIN = 2.0**-30
VMEM_LIMIT = 14 * 1024 * 1024

VMEM_SPEC = pl.BlockSpec(memory_space=pltpu.VMEM)
SMEM_SPEC = pl.BlockSpec(memory_space=pltpu.SMEM)


def pinned(x):
    return pltpu.with_memory_space_constraint(x, pltpu.VMEM)


def split(x):
    high = x.astype(jnp.bfloat16)
    rest = x - high.astype(jnp.float32)
    mid = rest.astype(jnp.bfloat16)
    low = (rest - mid.astype(jnp.float32)).astype(jnp.bfloat16)
    return high, mid, low


def put(ref, row):
    for k in range(row.shape[1] // LANES):
        ref[k : k + 1, :] = row[:, k * LANES : (k + 1) * LANES]


def positions(shape):
    return lax.broadcasted_iota(jnp.int32, shape, 0) * LANES + lax.broadcasted_iota(jnp.int32, shape, 1)


def to_sublanes(vector_ref, col_ref):
    for k in range(vector_ref.shape[0]):
        col_ref[k * LANES : (k + 1) * LANES, :] = jnp.broadcast_to(vector_ref[k : k + 1, :], (LANES, LANES)).T


def fold_lanes(peak_ref, total_ref, out_ref):
    for k in range(out_ref.shape[0]):
        here = slice(k * LANES, (k + 1) * LANES)
        peaks = peak_ref[here, :].T
        top = jnp.max(peaks, axis=0, keepdims=True)
        total = jnp.sum(total_ref[here, :].T * jnp.exp2(peaks - top), axis=0, keepdims=True)
        out_ref[k : k + 1, :] = top + jnp.log2(total)


def row_lse(score_ref, add_ref, peak_ref, total_ref, out_ref):
    rows, cols = score_ref.shape

    def block(i, _):
        here = pl.ds(pl.multiple_of(i * 8, 8), 8)
        z = []
        for k in range(cols // LANES):
            z.append(score_ref[here, k * LANES : (k + 1) * LANES] + add_ref[k : k + 1, :])
        peak = functools.reduce(jnp.maximum, z)
        peak_ref[here, :] = peak
        total_ref[here, :] = functools.reduce(jnp.add, [jnp.exp2(v - peak) for v in z])
        return 0

    lax.fori_loop(0, rows // 8, block, 0)
    fold_lanes(peak_ref, total_ref, out_ref)


def col_lse(score_ref, add_ref, out_ref, kernel_ref=None, top_ref=None):
    rows, cols = score_ref.shape
    group = 16
    tall = 4

    for first in range(0, cols // LANES, group):
        lanes = [slice((first + k) * LANES, (first + k + 1) * LANES) for k in range(group)]

        def peaks(i, tops):
            for r in range(tall):
                here = pl.ds(pl.multiple_of((i * tall + r) * 8, 8), 8)
                add = add_ref[here, :]
                tops = tuple(jnp.maximum(t, score_ref[here, s] + add) for t, s in zip(tops, lanes))
            return tops

        start = (jnp.full((8, LANES), -jnp.inf, jnp.float32),) * group
        tops = lax.fori_loop(0, rows // (8 * tall), peaks, start)
        tops = [jnp.max(t, axis=0, keepdims=True) - SHIFT for t in tops]
        wide_tops = [jnp.broadcast_to(t, (8, LANES)) for t in tops]

        def totals(i, sums):
            for r in range(tall):
                here = pl.ds(pl.multiple_of((i * tall + r) * 8, 8), 8)
                add = add_ref[here, :]
                terms = [jnp.exp2(score_ref[here, s] + (add - t)) for t, s in zip(wide_tops, lanes)]
                if kernel_ref is not None:
                    for s, t in zip(lanes, terms):
                        kernel_ref[here, s] = t
                sums = tuple(u + t for u, t in zip(sums, terms))
            return sums

        start = (jnp.zeros((8, LANES), jnp.float32),) * group
        sums = lax.fori_loop(0, rows // (8 * tall), totals, start)
        for k, (t, u) in enumerate(zip(tops, sums)):
            spot = slice(first + k, first + k + 1)
            if top_ref is not None:
                top_ref[spot, :] = t
            out_ref[spot, :] = t + jnp.log2(jnp.sum(u, axis=0, keepdims=True))


def source_terms(x):
    high, mid, low = split(x * (2.0 * SCALE))
    return [high, high, mid, mid, high, low]


def target_terms(y):
    high, mid, low = split(y)
    return [high, mid, high, mid, low, high]


def pad_into(pad_ref, values):
    pad_ref[...] = jnp.zeros(pad_ref.shape, jnp.float32)
    pad_ref[0 : values.shape[0], :] = values


def live_sum(counts):
    total = counts[0]
    for i in range(1, counts.shape[0]):
        total = total + counts[i]
    return jnp.full((1, LANES), total, jnp.int32).astype(jnp.float32)


def wide(x, size):
    return jnp.concatenate([x] * (size // LANES), axis=1)


def first_kernel(
    src_hbm, tgt_hbm, count_src_hbm, count_tgt_hbm, pair,
    score_ref, lse_ref, row_aux, col_aux, own_ref, half_ref,
    src_ref, tgt_ref, count_src, count_tgt, sems,
    right_pad, left_pad, terms_ref, norm_ref, col_ref, peak_ref, total_ref,
):
    rows, cols = score_ref.shape
    dims = src_ref.shape[0]
    copies = [
        pltpu.make_async_copy(one, two, sems.at[i])
        for i, (one, two) in enumerate(
            [(count_src_hbm, count_src), (count_tgt_hbm, count_tgt), (src_hbm, src_ref), (tgt_hbm, tgt_ref)]
        )
    ]
    for copy in copies:
        copy.start()
    for ref in (right_pad, left_pad, own_ref):
        ref[...] = jnp.zeros(ref.shape, jnp.float32)
    n_half = -(-dims // 2)
    for copy in copies[:3]:
        copy.wait()
    n_rows = count_src[lax.axis_index("src")]
    n_cols = count_tgt[lax.axis_index("tgt")]
    listed = pair[0, 0] > 0
    row_live = positions(row_aux.shape[1:]) < n_rows
    col_live = positions(col_aux.shape[1:]) < n_cols
    row_aux[0] = row_live.astype(jnp.float32)
    row_aux[1] = jnp.where(row_live, -jnp.log2(live_sum(count_src)), 0.0)
    row_aux[2] = (row_live & listed).astype(jnp.float32)
    col_aux[0] = col_live.astype(jnp.float32)
    col_aux[1] = jnp.where(col_live, -jnp.log2(live_sum(count_tgt)), 0.0)
    left_pad[0:dims, :] = src_ref[...]
    left = left_pad[...]
    half = jnp.where(lax.axis_index("tgt") % 2 == 0, left[0:n_half], left[n_half : 2 * n_half])
    half_ref[...] = jnp.zeros(half_ref.shape, jnp.float32)
    for k in range(rows // LANES):
        half_ref[0, k * n_half : (k + 1) * n_half, :] = half[:, k * LANES : (k + 1) * LANES]
    put(norm_ref, -SCALE * jnp.sum(left * left, axis=0, keepdims=True))
    norm_ref[...] = jnp.where(row_live, norm_ref[...], NEG)
    to_sublanes(norm_ref, col_ref)
    terms_ref[...] = jnp.concatenate(source_terms(left.T), axis=1)
    copies[3].wait()
    size = 512

    def scores(c):
        here = pl.ds(pl.multiple_of(c * size, size), size)
        right_pad[0:dims, :] = tgt_ref[:, here]
        right = right_pad[...]
        spot = lax.broadcasted_iota(jnp.int32, (1, size), 1) + c * size
        norm = -SCALE * jnp.sum(right * right, axis=0, keepdims=True)
        norm = jnp.where((spot < n_cols) & listed, norm, NEG)
        terms = jnp.concatenate(target_terms(right), axis=0)
        cross = jnp.dot(terms_ref[...], terms, preferred_element_type=jnp.float32)
        score = cross + (wide(col_ref[...], size) + norm)
        score_ref[:, here] = score
        return [score[:, k : k + LANES] for k in range(0, size, LANES)]

    peak_ref[...] = jnp.full(peak_ref.shape, 2.0 * NEG, jnp.float32)
    total_ref[...] = jnp.zeros(total_ref.shape, jnp.float32)

    def block(c, _):
        z = scores(c)
        before = peak_ref[...]
        peak = functools.reduce(jnp.maximum, z, before)
        total_ref[...] = functools.reduce(
            jnp.add, [jnp.exp2(v - peak) for v in z], total_ref[...] * jnp.exp2(before - peak)
        )
        peak_ref[...] = peak
        return 0

    lax.fori_loop(0, cols // size, block, 0)
    share = own_ref.shape[1]
    own_ref[0:dims, :] = tgt_ref[:, pl.ds(pl.multiple_of(lax.axis_index("src") * share, share), share)]
    fold_lanes(peak_ref, total_ref, lse_ref)


def slab_kernel(
    own_ref, mine_ref, theirs_ref, slab_ref, terms_out, token_ref, right_pad, terms_ref, norm_ref, col_ref,
    *, first, n_half,
):
    share = own_ref.shape[1]
    rows = right_pad.shape[1]
    left = own_ref[...]
    put(norm_ref, -SCALE * jnp.sum(left * left, axis=0, keepdims=True))
    to_sublanes(norm_ref, col_ref)
    terms_ref[...] = jnp.concatenate(target_terms(left.T), axis=1)
    even = lax.axis_index("tgt") % 2 == 0
    right_pad[...] = jnp.zeros(right_pad.shape, jnp.float32)
    for b in range(slab_ref.shape[1] // rows):
        mine, theirs = mine_ref[first + b], theirs_ref[first + b]
        upper = jnp.where(even, mine, theirs)
        lower = jnp.where(even, theirs, mine)
        for k in range(rows // LANES):
            here = slice(k * n_half, (k + 1) * n_half)
            right_pad[0:n_half, k * LANES : (k + 1) * LANES] = upper[here]
            right_pad[n_half : 2 * n_half, k * LANES : (k + 1) * LANES] = lower[here]
        right = right_pad[...]
        norm = -SCALE * jnp.sum(right * right, axis=0, keepdims=True)
        terms = jnp.concatenate(source_terms(right), axis=0)
        cross = jnp.dot(terms_ref[...], terms, preferred_element_type=jnp.float32)
        here = slice(b * rows, (b + 1) * rows)
        slab_ref[:, here] = cross + (wide(col_ref[...], rows) + norm)
        terms_out[here, :] = jnp.concatenate(split(right.T), axis=1)
    token_ref[...] = jnp.zeros(token_ref.shape, jnp.float32)


def row_sums(kernel_ref, factor_ref, total_ref, out_ref):
    rows, cols = kernel_ref.shape
    tall = 8

    def block(i, _):
        spots = [pl.ds(pl.multiple_of((i * tall + k) * 8, 8), 8) for k in range(tall)]
        sums = [jnp.zeros((8, LANES), jnp.float32)] * tall
        for t in range(cols // LANES):
            lanes = slice(t * LANES, (t + 1) * LANES)
            factor = jnp.broadcast_to(factor_ref[t : t + 1, :], (8, LANES))
            sums = [u + kernel_ref[s, lanes] * factor for u, s in zip(sums, spots)]
        for s, u in zip(spots, sums):
            total_ref[s, :] = u
        return 0

    lax.fori_loop(0, rows // (8 * tall), block, 0)
    for k in range(out_ref.shape[0]):
        out_ref[k : k + 1, :] = jnp.sum(total_ref[k * LANES : (k + 1) * LANES, :].T, axis=0, keepdims=True)


def col_sums(kernel_ref, factor_ref, out_ref):
    rows, cols = kernel_ref.shape
    lanes = [slice(start, start + LANES) for start in range(0, cols, LANES)]
    tall = 4

    def block(i, sums):
        for r in range(tall):
            here = pl.ds(pl.multiple_of((i * tall + r) * 8, 8), 8)
            factor = factor_ref[here, :]
            sums = tuple(u + kernel_ref[here, s] * factor for u, s in zip(sums, lanes))
        return sums

    sums = lax.fori_loop(0, rows // (8 * tall), block, (jnp.zeros((8, LANES), jnp.float32),) * len(lanes))
    for k, u in enumerate(sums):
        out_ref[k : k + 1, :] = jnp.sum(u, axis=0, keepdims=True)


def out_of_range(total, needed, factor, most):
    small = jnp.where(needed & jnp.logical_not(total >= SUM_MIN), 1.0, 0.0)
    large = jnp.where(factor <= most, 0.0, 1.0)
    return jnp.max(jnp.maximum(jnp.max(small, axis=0, keepdims=True), jnp.max(large, axis=0, keepdims=True))) > 0.5


def set_f(lse_ref, aux_ref, f_ref, masked_ref):
    f = aux_ref[1] - lse_ref[...] * aux_ref[0]
    f_ref[...] = f
    masked_ref[...] = jnp.where(aux_ref[2] > 0, f, NEG)


def first_col_kernel(score_ref, lse_ref, aux_ref, out_ref, f_ref, masked_ref, kernel_ref, top_ref, col_ref):
    set_f(lse_ref, aux_ref, f_ref, masked_ref)
    to_sublanes(f_ref, col_ref)
    col_lse(score_ref, col_ref, out_ref, kernel_ref, top_ref)


def col_kernel(
    score_ref, kernel_ref, top_ref, base_ref, lse_ref, aux_ref, out_ref, f_ref, masked_ref, factor_ref, col_ref
):
    set_f(lse_ref, aux_ref, f_ref, masked_ref)
    factor_ref[...] = jnp.exp2(f_ref[...] - base_ref[...])
    to_sublanes(factor_ref, col_ref)
    col_sums(kernel_ref, col_ref, out_ref)
    total = out_ref[...]
    top = top_ref[...]
    redo = out_of_range(total, top > 0.5 * NEG, factor_ref[...], ROW_FACTOR_MAX)
    out_ref[...] = jnp.where(total > 0, top + jnp.log2(total), NEG)

    @pl.when(redo)
    def _():
        to_sublanes(f_ref, col_ref)
        col_lse(score_ref, col_ref, out_ref)


def merged(parts):
    peak = jnp.max(parts, axis=0)
    return peak + jnp.log2(jnp.sum(jnp.exp2(parts - peak[None]), axis=0))


def row_kernel(
    score_ref, kernel_ref, top_ref, base_ref, parts_ref, row_aux, col_aux, out_ref,
    g_ref, factor_ref, peak_ref, total_ref,
):
    lse = merged(parts_ref[...])
    g_ref[...] = col_aux[1] - lse * col_aux[0]
    factor_ref[...] = jnp.where(col_aux[0] > 0, jnp.exp2(top_ref[...] - lse + 2.0 * SHIFT), 0.0)
    row_sums(kernel_ref, factor_ref, total_ref, out_ref)
    total = out_ref[...]
    redo = out_of_range(total, row_aux[2] > 0, factor_ref[...], COL_FACTOR_MAX)
    log_b = col_aux[1, 0:1, 0:1]
    out_ref[...] = jnp.where(total > 0, jnp.log2(total) - 2.0 * SHIFT - base_ref[...] + log_b, NEG)

    @pl.when(redo)
    def _():
        row_lse(score_ref, g_ref, peak_ref, total_ref, out_ref)


def last_kernel(*refs, pieces):
    slabs, refs = refs[: len(pieces)], refs[len(pieces) :]
    terms, refs = refs[: len(pieces)], refs[len(pieces) :]
    parts_ref, aux_ref, f_ref, *_, out_ref, f_out, g_out, lse_ref, own_ref, col_ref, sum_ref = refs
    n_col = aux_ref.shape[1]
    lse = merged(parts_ref[:, 0:n_col, :])
    lse_ref[...] = lse
    f_out[...] = f_ref[...] * (1.0 / SCALE)
    g_out[...] = (aux_ref[1] - lse * aux_ref[0]) * (1.0 / SCALE)
    me = lax.axis_index("src")
    n_own = own_ref.shape[0]
    for k in range(n_own):
        spot = pl.ds(me * n_own + k, 1)
        own_ref[k : k + 1, :] = jnp.where(aux_ref[0, spot, :] > 0, -lse_ref[spot, :], NEG)
    to_sublanes(own_ref, col_ref)
    for i, (slab_ref, terms_ref, offsets) in enumerate(zip(slabs, terms, pieces)):
        high, mid = [], []
        start = 0
        for offset in offsets:
            for row in range(n_col, parts_ref.shape[1]):
                add = col_ref[...] + parts_ref[me ^ offset, row : row + 1, :]
                term = split(jnp.exp2(slab_ref[:, start : start + LANES] + add))
                high.append(term[0])
                mid.append(term[1])
                start += LANES
        sums = jnp.dot(
            jnp.concatenate(high + mid, axis=1), jnp.concatenate([terms_ref[...]] * 2, axis=0),
            preferred_element_type=jnp.float32,
        )
        if i == 0:
            sum_ref[...] = sums
        else:
            sum_ref[...] += sums
    sums = sum_ref[...].T
    out_ref[...] = (sums[0:DEPTH] + sums[DEPTH : 2 * DEPTH] + sums[2 * DEPTH :])[0 : out_ref.shape[0]]


def merge(one, two):
    top = jnp.maximum(one, two)
    return top + jnp.log2(1.0 + jnp.exp2(jnp.minimum(one, two) - top))


def swap(value, axis, step):
    return lax.ppermute(value, axis, [(i, i ^ step) for i in range(lax.axis_size(axis))])


def doubling(size):
    return [1 << k for k in range(size.bit_length() - 1)]


def buffer(space, shape):
    return space(*shape) if isinstance(shape[0], tuple) else space(shape, jnp.float32)


def call(kernel, outs, scratch, ins, flops, expos=0, pin=True):
    return pl.pallas_call(
        kernel,
        out_shape=[buffer(pltpu.VMEM if pin else jax.ShapeDtypeStruct, shape) for shape in outs],
        in_specs=[VMEM_SPEC] * len(ins),
        out_specs=[VMEM_SPEC] * len(outs),
        scratch_shapes=[buffer(pltpu.VMEM, shape) for shape in scratch],
        compiler_params=pltpu.CompilerParams(vmem_limit_bytes=VMEM_LIMIT),
        cost_estimate=pl.CostEstimate(flops=flops, bytes_accessed=0, transcendentals=expos),
    )(*[pinned(x) for x in ins])


def tie(*values):
    return lax.optimization_barrier(values)


class Beside:
    def __init__(self, half, own, bits, rows, n_half):
        self.own = own
        self.rows = rows
        self.n_half = n_half
        self.blocks = {0: half}
        self.coming = {}
        if len(bits) >= 3:
            z, w, x = bits[:3]
            self.fetches = [[(0, z), (0, w), (0, x)], [(z, x), (w, z)], [(w, x), (w ^ z, x)], []]
            self.groups = [[], [0, z, w, x], [z ^ x, w ^ z], [w ^ x, w ^ z ^ x]]
            self.bits = bits[3:]
        else:
            self.fetches = [[]] * ITERS
            self.groups = [[]] * (ITERS - 1) + [[0]]
            self.bits = bits
        self.mine = []
        self.theirs = []
        self.offsets = []
        self.todo = []
        self.tokens = []
        self.slabs = []
        self.terms = []
        self.done = []

    def start(self, step, value, exchange):
        used = sorted({offset for offset, _ in self.fetches[step]} | set(self.groups[step]))
        if step and used:
            value, *held = tie(value, *[self.blocks[offset] for offset in used])
            self.blocks.update(zip(used, held))
        others = exchange(value)
        for offset, bit in self.fetches[step]:
            self.coming[offset ^ bit] = swap(self.blocks[offset], "src", bit)
        if self.groups[step]:
            held = [self.blocks[offset] for offset in self.groups[step]]
            self.add(held[0] if len(held) == 1 else jnp.concatenate(held, axis=0), self.groups[step])
        return others

    def add(self, mine, offsets):
        group = len(self.mine)
        self.mine.append(mine)
        self.theirs.append(swap(mine, "tgt", 1))
        self.offsets.append(offsets)
        self.todo += [(group, first, min(2, len(offsets))) for first in range(0, len(offsets), 2)]

    def land(self, value):
        if self.coming:
            value, *held = tie(value, *self.coming.values())
            self.blocks.update(zip(self.coming, held))
            self.coming = {}
        return value

    def piece(self):
        group, first, size = self.todo.pop(0)
        share = self.own.shape[1]
        rows = self.rows
        slab, terms, token = call(
            functools.partial(slab_kernel, first=first, n_half=self.n_half),
            [(share, size * rows), ((size * rows, 3 * DEPTH), jnp.bfloat16), (8, LANES)],
            [(DEPTH, rows), ((share, 6 * DEPTH), jnp.bfloat16), (share // LANES, LANES), (share, LANES)],
            [self.own, self.mine[group], self.theirs[group]],
            12 * DEPTH * share * size * rows,
        )
        self.terms.append(terms)
        self.slabs.append(slab)
        self.done.append(self.offsets[group][first : first + size])
        return token

    def pieces(self, value, most):
        for _ in range(min(most, len(self.todo))):
            value, token = tie(value, self.piece())
            self.tokens.append(token)
        return value

    def finish(self, value):
        for bit in self.bits:
            for mine, offsets in list(zip(self.mine, self.offsets)):
                self.add(swap(mine, "src", bit), [offset ^ bit for offset in offsets])
        return self.pieces(value, len(self.todo))


def shards(sources, targets, pair_active, count_src, count_tgt):
    dims, rows = sources.shape
    cols = targets.shape[1]
    n_src = lax.axis_size("src")
    share = cols // n_src
    column = (rows, LANES)
    by_row = (rows // LANES, LANES)
    by_col = (cols // LANES, LANES)
    pairs = rows * cols
    hbm = [pltpu.with_memory_space_constraint(x, pltpu.HBM) for x in (sources, targets, count_src, count_tgt)]
    n_half = -(-dims // 2)
    packed = -(-n_half * by_row[0] // 8) * 8
    outs = [(rows, cols), by_row, (3, *by_row), (3, *by_col), (DEPTH, share), (1, packed, LANES)]
    score, lse, row_aux, col_aux, own, half = pl.pallas_call(
        first_kernel,
        out_shape=[pltpu.VMEM(shape, jnp.float32) for shape in outs],
        in_specs=[pl.BlockSpec(memory_space=pltpu.HBM)] * 4 + [SMEM_SPEC],
        out_specs=[VMEM_SPEC] * len(outs),
        scratch_shapes=[
            pltpu.VMEM((dims, rows), jnp.float32),
            pltpu.VMEM((dims, cols), jnp.float32),
            pltpu.SMEM(count_src.shape, jnp.int32),
            pltpu.SMEM(count_tgt.shape, jnp.int32),
            pltpu.SemaphoreType.DMA((4,)),
            pltpu.VMEM((DEPTH, 512), jnp.float32),
            pltpu.VMEM((DEPTH, rows), jnp.float32),
            pltpu.VMEM((rows, 6 * DEPTH), jnp.bfloat16),
            pltpu.VMEM(by_row, jnp.float32),
            pltpu.VMEM(column, jnp.float32),
            pltpu.VMEM(column, jnp.float32),
            pltpu.VMEM(column, jnp.float32),
        ],
        compiler_params=pltpu.CompilerParams(vmem_limit_bytes=VMEM_LIMIT),
        cost_estimate=pl.CostEstimate(flops=12 * DEPTH * pairs, bytes_accessed=0, transcendentals=pairs),
    )(*hbm, pair_active)
    over_tgt = doubling(lax.axis_size("tgt"))
    over_src = doubling(n_src)
    over_src = over_src[1:] + over_src[:1]
    side = Beside(half, own, over_src, rows, n_half)
    near = [bit for bit in (2, 3, 1) if bit < lax.axis_size("tgt")]

    def exchange(value):
        return [swap(value, "tgt", bit) for bit in near]

    def combine(value, others):
        values = dict(zip(near, others))
        value = merge(value, values[1])
        return merge(value, merge(values[2], values[3])) if 2 in values else value

    for step in range(ITERS):
        others = side.start(step, lse, exchange)
        if step == ITERS - 1:
            others[0] = side.pieces(others[0], 1)
        lse = combine(lse, others)
        for bit in over_tgt[2:]:
            lse = merge(lse, swap(lse, "tgt", bit))
        if step == 0:
            lse, base, masked, kernel, top = call(
                first_col_kernel,
                [by_col, by_row, by_row, (rows, cols), by_col],
                [column], [score, lse, row_aux], 0,
            )
        else:
            lse, f, masked = call(
                col_kernel,
                [by_col, by_row, by_row],
                [by_row, column], [score, kernel, top, base, lse, row_aux], 0,
            )
        if step < ITERS - 1:
            lse = side.land(side.pieces(lse, step))
            lse = lax.all_to_all(jnp.broadcast_to(lse, (n_src, *by_col)), "src", 0, 0, tiled=True)
            (lse,) = call(
                row_kernel,
                [by_row],
                [by_col, by_col, column, column],
                [score, kernel, top, base, lse, row_aux, col_aux], 0,
            )
    lse = side.finish(lse)
    both = jnp.concatenate([lse, masked], axis=0)
    both = lax.all_to_all(jnp.broadcast_to(both, (n_src, *both.shape)), "src", 0, 0, tiled=True)
    ancestors, f, g = call(
        functools.partial(last_kernel, pieces=side.done),
        [(dims, share), by_row, by_col],
        [by_col, (share // LANES, LANES), (share, LANES), (share, 3 * DEPTH)],
        [*side.slabs, *side.terms, both, col_aux, f, *side.tokens],
        18 * DEPTH * pairs, pairs, pin=False,
    )
    return (f.reshape(rows), g.reshape(cols), ancestors)


def solution(mesh):
    return jax.shard_map(
        shards,
        mesh=mesh,
        in_specs=(P(None, "src"), P(None, "tgt"), P("src", "tgt"), P(), P()),
        out_specs=(P("src"), P("tgt"), P(None, ("tgt", "src"))),
        check_vma=False,
    )
```

```python
import functools
import math

import jax
import jax.numpy as jnp
from jax import lax
from jax.experimental import pallas as pl
from jax.experimental.pallas import tpu as pltpu
from jax.sharding import PartitionSpec as P

ITERS = 4
EPS = 0.02
NEG = -1e30
LOG2E = math.log2(math.e)
SCALE = LOG2E / EPS
LANES = 128
DEPTH = 64
SHIFT = 40.0
ROW_FACTOR_MAX = 2.0**20
COL_FACTOR_MAX = 2.0**60
SUM_MIN = 2.0**-30
VMEM_LIMIT = 14 * 1024 * 1024

VMEM_SPEC = pl.BlockSpec(memory_space=pltpu.VMEM)
SMEM_SPEC = pl.BlockSpec(memory_space=pltpu.SMEM)


def pinned(x):
    return pltpu.with_memory_space_constraint(x, pltpu.VMEM)


def split(x):
    high = x.astype(jnp.bfloat16)
    rest = x - high.astype(jnp.float32)
    mid = rest.astype(jnp.bfloat16)
    low = (rest - mid.astype(jnp.float32)).astype(jnp.bfloat16)
    return high, mid, low


def put(ref, row):
    for k in range(row.shape[1] // LANES):
        ref[k : k + 1, :] = row[:, k * LANES : (k + 1) * LANES]


def positions(shape):
    return lax.broadcasted_iota(jnp.int32, shape, 0) * LANES + lax.broadcasted_iota(jnp.int32, shape, 1)


def to_sublanes(vector_ref, col_ref):
    for k in range(vector_ref.shape[0]):
        col_ref[k * LANES : (k + 1) * LANES, :] = jnp.broadcast_to(vector_ref[k : k + 1, :], (LANES, LANES)).T


def fold_lanes(peak_ref, total_ref, out_ref):
    for k in range(out_ref.shape[0]):
        here = slice(k * LANES, (k + 1) * LANES)
        peaks = peak_ref[here, :].T
        top = jnp.max(peaks, axis=0, keepdims=True)
        total = jnp.sum(total_ref[here, :].T * jnp.exp2(peaks - top), axis=0, keepdims=True)
        out_ref[k : k + 1, :] = top + jnp.log2(total)


def row_lse(score_ref, add_ref, peak_ref, total_ref, out_ref):
    rows, cols = score_ref.shape

    def block(i, _):
        here = pl.ds(pl.multiple_of(i * 8, 8), 8)
        z = []
        for k in range(cols // LANES):
            z.append(score_ref[here, k * LANES : (k + 1) * LANES] + add_ref[k : k + 1, :])
        peak = functools.reduce(jnp.maximum, z)
        peak_ref[here, :] = peak
        total_ref[here, :] = functools.reduce(jnp.add, [jnp.exp2(v - peak) for v in z])
        return 0

    lax.fori_loop(0, rows // 8, block, 0)
    fold_lanes(peak_ref, total_ref, out_ref)


def col_lse(score_ref, add_ref, out_ref, kernel_ref=None, top_ref=None):
    rows, cols = score_ref.shape
    group = 16
    tall = 4

    for first in range(0, cols // LANES, group):
        lanes = [slice((first + k) * LANES, (first + k + 1) * LANES) for k in range(group)]

        def peaks(i, tops):
            for r in range(tall):
                here = pl.ds(pl.multiple_of((i * tall + r) * 8, 8), 8)
                add = add_ref[here, :]
                tops = tuple(jnp.maximum(t, score_ref[here, s] + add) for t, s in zip(tops, lanes))
            return tops

        start = (jnp.full((8, LANES), -jnp.inf, jnp.float32),) * group
        tops = lax.fori_loop(0, rows // (8 * tall), peaks, start)
        tops = [jnp.max(t, axis=0, keepdims=True) - SHIFT for t in tops]
        wide_tops = [jnp.broadcast_to(t, (8, LANES)) for t in tops]

        def totals(i, sums):
            for r in range(tall):
                here = pl.ds(pl.multiple_of((i * tall + r) * 8, 8), 8)
                add = add_ref[here, :]
                terms = [jnp.exp2(score_ref[here, s] + (add - t)) for t, s in zip(wide_tops, lanes)]
                if kernel_ref is not None:
                    for s, t in zip(lanes, terms):
                        kernel_ref[here, s] = t
                sums = tuple(u + t for u, t in zip(sums, terms))
            return sums

        start = (jnp.zeros((8, LANES), jnp.float32),) * group
        sums = lax.fori_loop(0, rows // (8 * tall), totals, start)
        for k, (t, u) in enumerate(zip(tops, sums)):
            spot = slice(first + k, first + k + 1)
            if top_ref is not None:
                top_ref[spot, :] = t
            out_ref[spot, :] = t + jnp.log2(jnp.sum(u, axis=0, keepdims=True))


def source_terms(x):
    high, mid, low = split(x * (2.0 * SCALE))
    return [high, high, mid, mid, high, low]


def target_terms(y):
    high, mid, low = split(y)
    return [high, mid, high, mid, low, high]


def pad_into(pad_ref, values):
    pad_ref[...] = jnp.zeros(pad_ref.shape, jnp.float32)
    pad_ref[0 : values.shape[0], :] = values


def live_sum(counts):
    total = counts[0]
    for i in range(1, counts.shape[0]):
        total = total + counts[i]
    return jnp.full((1, LANES), total, jnp.int32).astype(jnp.float32)


def wide(x, size):
    return jnp.concatenate([x] * (size // LANES), axis=1)


def first_kernel(
    src_hbm, tgt_hbm, count_src_hbm, count_tgt_hbm, pair,
    score_ref, lse_ref, row_aux, col_aux, own_ref, half_ref,
    src_ref, tgt_ref, count_src, count_tgt, sems,
    right_pad, left_pad, terms_ref, norm_ref, col_ref, peak_ref, total_ref,
):
    rows, cols = score_ref.shape
    dims = src_ref.shape[0]
    copies = [
        pltpu.make_async_copy(one, two, sems.at[i])
        for i, (one, two) in enumerate(
            [(count_src_hbm, count_src), (count_tgt_hbm, count_tgt), (src_hbm, src_ref), (tgt_hbm, tgt_ref)]
        )
    ]
    for copy in copies:
        copy.start()
    for ref in (right_pad, left_pad, own_ref):
        ref[...] = jnp.zeros(ref.shape, jnp.float32)
    n_half = -(-dims // 2)
    for copy in copies[:3]:
        copy.wait()
    n_rows = count_src[lax.axis_index("src")]
    n_cols = count_tgt[lax.axis_index("tgt")]
    listed = pair[0, 0] > 0
    row_live = positions(row_aux.shape[1:]) < n_rows
    col_live = positions(col_aux.shape[1:]) < n_cols
    row_aux[0] = row_live.astype(jnp.float32)
    row_aux[1] = jnp.where(row_live, -jnp.log2(live_sum(count_src)), 0.0)
    row_aux[2] = (row_live & listed).astype(jnp.float32)
    col_aux[0] = col_live.astype(jnp.float32)
    col_aux[1] = jnp.where(col_live, -jnp.log2(live_sum(count_tgt)), 0.0)
    left_pad[0:dims, :] = src_ref[...]
    left = left_pad[...]
    half = jnp.where(lax.axis_index("tgt") % 2 == 0, left[0:n_half], left[n_half : 2 * n_half])
    half_ref[...] = jnp.zeros(half_ref.shape, jnp.float32)
    for k in range(rows // LANES):
        half_ref[0, k * n_half : (k + 1) * n_half, :] = half[:, k * LANES : (k + 1) * LANES]
    put(norm_ref, -SCALE * jnp.sum(left * left, axis=0, keepdims=True))
    norm_ref[...] = jnp.where(row_live, norm_ref[...], NEG)
    to_sublanes(norm_ref, col_ref)
    terms_ref[...] = jnp.concatenate(source_terms(left.T), axis=1)
    copies[3].wait()
    size = 512

    def scores(c):
        here = pl.ds(pl.multiple_of(c * size, size), size)
        right_pad[0:dims, :] = tgt_ref[:, here]
        right = right_pad[...]
        spot = lax.broadcasted_iota(jnp.int32, (1, size), 1) + c * size
        norm = -SCALE * jnp.sum(right * right, axis=0, keepdims=True)
        norm = jnp.where((spot < n_cols) & listed, norm, NEG)
        terms = jnp.concatenate(target_terms(right), axis=0)
        cross = jnp.dot(terms_ref[...], terms, preferred_element_type=jnp.float32)
        score = cross + (wide(col_ref[...], size) + norm)
        score_ref[:, here] = score
        return [score[:, k : k + LANES] for k in range(0, size, LANES)]

    peak_ref[...] = jnp.full(peak_ref.shape, 2.0 * NEG, jnp.float32)
    total_ref[...] = jnp.zeros(total_ref.shape, jnp.float32)

    def block(c, _):
        z = scores(c)
        before = peak_ref[...]
        peak = functools.reduce(jnp.maximum, z, before)
        total_ref[...] = functools.reduce(
            jnp.add, [jnp.exp2(v - peak) for v in z], total_ref[...] * jnp.exp2(before - peak)
        )
        peak_ref[...] = peak
        return 0

    lax.fori_loop(0, cols // size, block, 0)
    share = own_ref.shape[1]
    own_ref[0:dims, :] = tgt_ref[:, pl.ds(pl.multiple_of(lax.axis_index("src") * share, share), share)]
    fold_lanes(peak_ref, total_ref, lse_ref)


def slab_kernel(
    own_ref, mine_ref, theirs_ref, slab_ref, terms_out, token_ref, right_pad, terms_ref, norm_ref, col_ref,
    *, first, n_half,
):
    share = own_ref.shape[1]
    rows = right_pad.shape[1]
    left = own_ref[...]
    put(norm_ref, -SCALE * jnp.sum(left * left, axis=0, keepdims=True))
    to_sublanes(norm_ref, col_ref)
    terms_ref[...] = jnp.concatenate(target_terms(left.T), axis=1)
    even = lax.axis_index("tgt") % 2 == 0
    right_pad[...] = jnp.zeros(right_pad.shape, jnp.float32)
    for b in range(slab_ref.shape[1] // rows):
        mine, theirs = mine_ref[first + b], theirs_ref[first + b]
        upper = jnp.where(even, mine, theirs)
        lower = jnp.where(even, theirs, mine)
        for k in range(rows // LANES):
            here = slice(k * n_half, (k + 1) * n_half)
            right_pad[0:n_half, k * LANES : (k + 1) * LANES] = upper[here]
            right_pad[n_half : 2 * n_half, k * LANES : (k + 1) * LANES] = lower[here]
        right = right_pad[...]
        norm = -SCALE * jnp.sum(right * right, axis=0, keepdims=True)
        terms = jnp.concatenate(source_terms(right), axis=0)
        cross = jnp.dot(terms_ref[...], terms, preferred_element_type=jnp.float32)
        here = slice(b * rows, (b + 1) * rows)
        slab_ref[:, here] = cross + (wide(col_ref[...], rows) + norm)
        terms_out[here, :] = jnp.concatenate(split(right.T), axis=1)
    token_ref[...] = jnp.zeros(token_ref.shape, jnp.float32)


def row_sums(kernel_ref, factor_ref, total_ref, out_ref):
    rows, cols = kernel_ref.shape
    tall = 8

    def block(i, _):
        spots = [pl.ds(pl.multiple_of((i * tall + k) * 8, 8), 8) for k in range(tall)]
        sums = [jnp.zeros((8, LANES), jnp.float32)] * tall
        for t in range(cols // LANES):
            lanes = slice(t * LANES, (t + 1) * LANES)
            factor = jnp.broadcast_to(factor_ref[t : t + 1, :], (8, LANES))
            sums = [u + kernel_ref[s, lanes] * factor for u, s in zip(sums, spots)]
        for s, u in zip(spots, sums):
            total_ref[s, :] = u
        return 0

    lax.fori_loop(0, rows // (8 * tall), block, 0)
    for k in range(out_ref.shape[0]):
        out_ref[k : k + 1, :] = jnp.sum(total_ref[k * LANES : (k + 1) * LANES, :].T, axis=0, keepdims=True)


def col_sums(kernel_ref, factor_ref, out_ref):
    rows, cols = kernel_ref.shape
    lanes = [slice(start, start + LANES) for start in range(0, cols, LANES)]
    tall = 4

    def block(i, sums):
        for r in range(tall):
            here = pl.ds(pl.multiple_of((i * tall + r) * 8, 8), 8)
            factor = factor_ref[here, :]
            sums = tuple(u + kernel_ref[here, s] * factor for u, s in zip(sums, lanes))
        return sums

    sums = lax.fori_loop(0, rows // (8 * tall), block, (jnp.zeros((8, LANES), jnp.float32),) * len(lanes))
    for k, u in enumerate(sums):
        out_ref[k : k + 1, :] = jnp.sum(u, axis=0, keepdims=True)


def out_of_range(total, needed, factor, most):
    small = jnp.where(needed & jnp.logical_not(total >= SUM_MIN), 1.0, 0.0)
    large = jnp.where(factor <= most, 0.0, 1.0)
    return jnp.max(jnp.maximum(jnp.max(small, axis=0, keepdims=True), jnp.max(large, axis=0, keepdims=True))) > 0.5


def set_f(lse_ref, aux_ref, f_ref, masked_ref):
    f = aux_ref[1] - lse_ref[...] * aux_ref[0]
    f_ref[...] = f
    masked_ref[...] = jnp.where(aux_ref[2] > 0, f, NEG)


def first_col_kernel(score_ref, lse_ref, aux_ref, out_ref, f_ref, masked_ref, kernel_ref, top_ref, col_ref):
    set_f(lse_ref, aux_ref, f_ref, masked_ref)
    to_sublanes(f_ref, col_ref)
    col_lse(score_ref, col_ref, out_ref, kernel_ref, top_ref)


def col_kernel(
    score_ref, kernel_ref, top_ref, base_ref, lse_ref, aux_ref, out_ref, f_ref, masked_ref, factor_ref, col_ref
):
    set_f(lse_ref, aux_ref, f_ref, masked_ref)
    factor_ref[...] = jnp.exp2(f_ref[...] - base_ref[...])
    to_sublanes(factor_ref, col_ref)
    col_sums(kernel_ref, col_ref, out_ref)
    total = out_ref[...]
    top = top_ref[...]
    redo = out_of_range(total, top > 0.5 * NEG, factor_ref[...], ROW_FACTOR_MAX)
    out_ref[...] = jnp.where(total > 0, top + jnp.log2(total), NEG)

    @pl.when(redo)
    def _():
        to_sublanes(f_ref, col_ref)
        col_lse(score_ref, col_ref, out_ref)


def merged(parts):
    peak = jnp.max(parts, axis=0)
    return peak + jnp.log2(jnp.sum(jnp.exp2(parts - peak[None]), axis=0))


def row_kernel(
    score_ref, kernel_ref, top_ref, base_ref, parts_ref, row_aux, col_aux, out_ref,
    g_ref, factor_ref, peak_ref, total_ref,
):
    lse = merged(parts_ref[...])
    g_ref[...] = col_aux[1] - lse * col_aux[0]
    factor_ref[...] = jnp.where(col_aux[0] > 0, jnp.exp2(top_ref[...] - lse + 2.0 * SHIFT), 0.0)
    row_sums(kernel_ref, factor_ref, total_ref, out_ref)
    total = out_ref[...]
    redo = out_of_range(total, row_aux[2] > 0, factor_ref[...], COL_FACTOR_MAX)
    log_b = col_aux[1, 0:1, 0:1]
    out_ref[...] = jnp.where(total > 0, jnp.log2(total) - 2.0 * SHIFT - base_ref[...] + log_b, NEG)

    @pl.when(redo)
    def _():
        row_lse(score_ref, g_ref, peak_ref, total_ref, out_ref)


def last_kernel(*refs, pieces):
    slabs, refs = refs[: len(pieces)], refs[len(pieces) :]
    terms, refs = refs[: len(pieces)], refs[len(pieces) :]
    parts_ref, aux_ref, f_ref, *_, out_ref, f_out, g_out, lse_ref, own_ref, col_ref, sum_ref = refs
    n_col = aux_ref.shape[1]
    lse = merged(parts_ref[:, 0:n_col, :])
    lse_ref[...] = lse
    f_out[...] = f_ref[...] * (1.0 / SCALE)
    g_out[...] = (aux_ref[1] - lse * aux_ref[0]) * (1.0 / SCALE)
    me = lax.axis_index("src")
    n_own = own_ref.shape[0]
    for k in range(n_own):
        spot = pl.ds(me * n_own + k, 1)
        own_ref[k : k + 1, :] = jnp.where(aux_ref[0, spot, :] > 0, -lse_ref[spot, :], NEG)
    to_sublanes(own_ref, col_ref)
    for i, (slab_ref, terms_ref, offsets) in enumerate(zip(slabs, terms, pieces)):
        high, mid = [], []
        start = 0
        for offset in offsets:
            for row in range(n_col, parts_ref.shape[1]):
                add = col_ref[...] + parts_ref[me ^ offset, row : row + 1, :]
                term = split(jnp.exp2(slab_ref[:, start : start + LANES] + add))
                high.append(term[0])
                mid.append(term[1])
                start += LANES
        sums = jnp.dot(
            jnp.concatenate(high + mid, axis=1), jnp.concatenate([terms_ref[...]] * 2, axis=0),
            preferred_element_type=jnp.float32,
        )
        if i == 0:
            sum_ref[...] = sums
        else:
            sum_ref[...] += sums
    sums = sum_ref[...].T
    out_ref[...] = (sums[0:DEPTH] + sums[DEPTH : 2 * DEPTH] + sums[2 * DEPTH :])[0 : out_ref.shape[0]]


def merge(one, two):
    top = jnp.maximum(one, two)
    return top + jnp.log2(1.0 + jnp.exp2(jnp.minimum(one, two) - top))


def swap(value, axis, step):
    return lax.ppermute(value, axis, [(i, i ^ step) for i in range(lax.axis_size(axis))])


def doubling(size):
    return [1 << k for k in range(size.bit_length() - 1)]


def buffer(space, shape):
    return space(*shape) if isinstance(shape[0], tuple) else space(shape, jnp.float32)


def call(kernel, outs, scratch, ins, flops, expos=0, pin=True):
    return pl.pallas_call(
        kernel,
        out_shape=[buffer(pltpu.VMEM if pin else jax.ShapeDtypeStruct, shape) for shape in outs],
        in_specs=[VMEM_SPEC] * len(ins),
        out_specs=[VMEM_SPEC] * len(outs),
        scratch_shapes=[buffer(pltpu.VMEM, shape) for shape in scratch],
        compiler_params=pltpu.CompilerParams(vmem_limit_bytes=VMEM_LIMIT),
        cost_estimate=pl.CostEstimate(flops=flops, bytes_accessed=0, transcendentals=expos),
    )(*[pinned(x) for x in ins])


def tie(*values):
    return lax.optimization_barrier(values)


class Beside:
    def __init__(self, half, own, bits, rows, n_half):
        self.own = own
        self.rows = rows
        self.n_half = n_half
        self.blocks = {0: half}
        self.coming = {}
        if len(bits) >= 3:
            z, w, x = bits[:3]
            self.fetches = [[(0, z), (0, w), (0, x)], [(z, x), (w, z)], [(w, x), (w ^ z, x)], []]
            self.groups = [[], [0, z, w, x], [z ^ x, w ^ z], [w ^ x, w ^ z ^ x]]
            self.bits = bits[3:]
        else:
            self.fetches = [[]] * ITERS
            self.groups = [[]] * (ITERS - 1) + [[0]]
            self.bits = bits
        self.mine = []
        self.theirs = []
        self.offsets = []
        self.todo = []
        self.tokens = []
        self.slabs = []
        self.terms = []
        self.done = []

    def start(self, step, value, exchange):
        used = sorted({offset for offset, _ in self.fetches[step]} | set(self.groups[step]))
        if step and used:
            value, *held = tie(value, *[self.blocks[offset] for offset in used])
            self.blocks.update(zip(used, held))
        others = exchange(value)
        for offset, bit in self.fetches[step]:
            self.coming[offset ^ bit] = swap(self.blocks[offset], "src", bit)
        if self.groups[step]:
            held = [self.blocks[offset] for offset in self.groups[step]]
            self.add(held[0] if len(held) == 1 else jnp.concatenate(held, axis=0), self.groups[step])
        return others

    def add(self, mine, offsets):
        group = len(self.mine)
        self.mine.append(mine)
        self.theirs.append(swap(mine, "tgt", 1))
        self.offsets.append(offsets)
        self.todo += [(group, first, min(2, len(offsets))) for first in range(0, len(offsets), 2)]

    def land(self, value):
        if self.coming:
            value, *held = tie(value, *self.coming.values())
            self.blocks.update(zip(self.coming, held))
            self.coming = {}
        return value

    def piece(self):
        group, first, size = self.todo.pop(0)
        share = self.own.shape[1]
        rows = self.rows
        slab, terms, token = call(
            functools.partial(slab_kernel, first=first, n_half=self.n_half),
            [(share, size * rows), ((size * rows, 3 * DEPTH), jnp.bfloat16), (8, LANES)],
            [(DEPTH, rows), ((share, 6 * DEPTH), jnp.bfloat16), (share // LANES, LANES), (share, LANES)],
            [self.own, self.mine[group], self.theirs[group]],
            12 * DEPTH * share * size * rows,
        )
        self.terms.append(terms)
        self.slabs.append(slab)
        self.done.append(self.offsets[group][first : first + size])
        return token

    def hold(self, value):
        value, self.own = tie(value, self.own)
        return value

    def pieces(self, value, most):
        for _ in range(min(most, len(self.todo))):
            value, token = tie(value, self.piece())
            self.tokens.append(token)
        return value

    def finish(self, value):
        for bit in self.bits:
            for mine, offsets in list(zip(self.mine, self.offsets)):
                self.add(swap(mine, "src", bit), [offset ^ bit for offset in offsets])
        return self.pieces(self.hold(value), len(self.todo))


def shards(sources, targets, pair_active, count_src, count_tgt):
    dims, rows = sources.shape
    cols = targets.shape[1]
    n_src = lax.axis_size("src")
    share = cols // n_src
    column = (rows, LANES)
    by_row = (rows // LANES, LANES)
    by_col = (cols // LANES, LANES)
    pairs = rows * cols
    hbm = [pltpu.with_memory_space_constraint(x, pltpu.HBM) for x in (sources, targets, count_src, count_tgt)]
    n_half = -(-dims // 2)
    packed = -(-n_half * by_row[0] // 8) * 8
    outs = [(rows, cols), by_row, (3, *by_row), (3, *by_col), (DEPTH, share), (1, packed, LANES)]
    score, lse, row_aux, col_aux, own, half = pl.pallas_call(
        first_kernel,
        out_shape=[pltpu.VMEM(shape, jnp.float32) for shape in outs],
        in_specs=[pl.BlockSpec(memory_space=pltpu.HBM)] * 4 + [SMEM_SPEC],
        out_specs=[VMEM_SPEC] * len(outs),
        scratch_shapes=[
            pltpu.VMEM((dims, rows), jnp.float32),
            pltpu.VMEM((dims, cols), jnp.float32),
            pltpu.SMEM(count_src.shape, jnp.int32),
            pltpu.SMEM(count_tgt.shape, jnp.int32),
            pltpu.SemaphoreType.DMA((4,)),
            pltpu.VMEM((DEPTH, 512), jnp.float32),
            pltpu.VMEM((DEPTH, rows), jnp.float32),
            pltpu.VMEM((rows, 6 * DEPTH), jnp.bfloat16),
            pltpu.VMEM(by_row, jnp.float32),
            pltpu.VMEM(column, jnp.float32),
            pltpu.VMEM(column, jnp.float32),
            pltpu.VMEM(column, jnp.float32),
        ],
        compiler_params=pltpu.CompilerParams(vmem_limit_bytes=VMEM_LIMIT),
        cost_estimate=pl.CostEstimate(flops=12 * DEPTH * pairs, bytes_accessed=0, transcendentals=pairs),
    )(*hbm, pair_active)
    over_tgt = doubling(lax.axis_size("tgt"))
    over_src = doubling(n_src)
    over_src = over_src[1:] + over_src[:1]
    side = Beside(half, own, over_src, rows, n_half)
    near = [bit for bit in (2, 3, 1) if bit < lax.axis_size("tgt")]

    def exchange(value):
        return [swap(value, "tgt", bit) for bit in near]

    def combine(value, others):
        values = dict(zip(near, others))
        value = merge(value, values[1])
        return merge(value, merge(values[2], values[3])) if 2 in values else value

    for step in range(ITERS):
        if step == ITERS - 1:
            lse = side.hold(lse)
        others = side.start(step, lse, exchange)
        if step == ITERS - 1:
            others[0] = side.pieces(others[0], 1)
        lse = combine(lse, others)
        for bit in over_tgt[2:]:
            lse = merge(lse, swap(lse, "tgt", bit))
        if step == 0:
            lse, base, masked, kernel, top = call(
                first_col_kernel,
                [by_col, by_row, by_row, (rows, cols), by_col],
                [column], [score, lse, row_aux], 0,
            )
        else:
            lse, f, masked = call(
                col_kernel,
                [by_col, by_row, by_row],
                [by_row, column], [score, kernel, top, base, lse, row_aux], 0,
            )
        if step < ITERS - 1:
            lse = side.land(side.pieces(side.hold(lse), step))
            lse = lax.all_to_all(jnp.broadcast_to(lse, (n_src, *by_col)), "src", 0, 0, tiled=True)
            (lse,) = call(
                row_kernel,
                [by_row],
                [by_col, by_col, column, column],
                [score, kernel, top, base, lse, row_aux, col_aux], 0,
            )
    lse = side.finish(lse)
    both = jnp.concatenate([lse, masked], axis=0)
    both = lax.all_to_all(jnp.broadcast_to(both, (n_src, *both.shape)), "src", 0, 0, tiled=True)
    ancestors, f, g = call(
        functools.partial(last_kernel, pieces=side.done),
        [(dims, share), by_row, by_col],
        [by_col, (share // LANES, LANES), (share, LANES), (share, 3 * DEPTH)],
        [*side.slabs, *side.terms, both, col_aux, f, *side.tokens],
        18 * DEPTH * pairs, pairs, pin=False,
    )
    return (f.reshape(rows), g.reshape(cols), ancestors)


def solution(mesh):
    return jax.shard_map(
        shards,
        mesh=mesh,
        in_specs=(P(None, "src"), P(None, "tgt"), P("src", "tgt"), P(), P()),
        out_specs=(P("src"), P("tgt"), P(None, ("tgt", "src"))),
        check_vma=False,
    )
```

```python
import functools
import math

import jax
import jax.numpy as jnp
from jax import lax
from jax.experimental import pallas as pl
from jax.experimental.pallas import tpu as pltpu
from jax.sharding import PartitionSpec as P

ITERS = 4
EPS = 0.02
NEG = -1e30
LOG2E = math.log2(math.e)
SCALE = LOG2E / EPS
LANES = 128
DEPTH = 64
SHIFT = 40.0
ROW_FACTOR_MAX = 2.0**20
COL_FACTOR_MAX = 2.0**60
SUM_MIN = 2.0**-30
VMEM_LIMIT = 14 * 1024 * 1024

VMEM_SPEC = pl.BlockSpec(memory_space=pltpu.VMEM)
SMEM_SPEC = pl.BlockSpec(memory_space=pltpu.SMEM)


def pinned(x):
    return pltpu.with_memory_space_constraint(x, pltpu.VMEM)


def split(x):
    high = x.astype(jnp.bfloat16)
    rest = x - high.astype(jnp.float32)
    mid = rest.astype(jnp.bfloat16)
    low = (rest - mid.astype(jnp.float32)).astype(jnp.bfloat16)
    return high, mid, low


def put(ref, row):
    for k in range(row.shape[1] // LANES):
        ref[k : k + 1, :] = row[:, k * LANES : (k + 1) * LANES]


def positions(shape):
    return lax.broadcasted_iota(jnp.int32, shape, 0) * LANES + lax.broadcasted_iota(jnp.int32, shape, 1)


def to_sublanes(vector_ref, col_ref):
    for k in range(vector_ref.shape[0]):
        col_ref[k * LANES : (k + 1) * LANES, :] = jnp.broadcast_to(vector_ref[k : k + 1, :], (LANES, LANES)).T


def fold_lanes(peak_ref, total_ref, out_ref):
    for k in range(out_ref.shape[0]):
        here = slice(k * LANES, (k + 1) * LANES)
        peaks = peak_ref[here, :].T
        top = jnp.max(peaks, axis=0, keepdims=True)
        total = jnp.sum(total_ref[here, :].T * jnp.exp2(peaks - top), axis=0, keepdims=True)
        out_ref[k : k + 1, :] = top + jnp.log2(total)


def row_lse(score_ref, add_ref, peak_ref, total_ref, out_ref):
    rows, cols = score_ref.shape

    def block(i, _):
        here = pl.ds(pl.multiple_of(i * 8, 8), 8)
        z = []
        for k in range(cols // LANES):
            z.append(score_ref[here, k * LANES : (k + 1) * LANES] + add_ref[k : k + 1, :])
        peak = functools.reduce(jnp.maximum, z)
        peak_ref[here, :] = peak
        total_ref[here, :] = functools.reduce(jnp.add, [jnp.exp2(v - peak) for v in z])
        return 0

    lax.fori_loop(0, rows // 8, block, 0)
    fold_lanes(peak_ref, total_ref, out_ref)


def col_lse(score_ref, add_ref, out_ref, kernel_ref=None, top_ref=None):
    rows, cols = score_ref.shape
    group = 16
    tall = 4

    for first in range(0, cols // LANES, group):
        lanes = [slice((first + k) * LANES, (first + k + 1) * LANES) for k in range(group)]

        def peaks(i, tops):
            for r in range(tall):
                here = pl.ds(pl.multiple_of((i * tall + r) * 8, 8), 8)
                add = add_ref[here, :]
                tops = tuple(jnp.maximum(t, score_ref[here, s] + add) for t, s in zip(tops, lanes))
            return tops

        start = (jnp.full((8, LANES), -jnp.inf, jnp.float32),) * group
        tops = lax.fori_loop(0, rows // (8 * tall), peaks, start)
        tops = [jnp.max(t, axis=0, keepdims=True) - SHIFT for t in tops]
        wide_tops = [jnp.broadcast_to(t, (8, LANES)) for t in tops]

        def totals(i, sums):
            for r in range(tall):
                here = pl.ds(pl.multiple_of((i * tall + r) * 8, 8), 8)
                add = add_ref[here, :]
                terms = [jnp.exp2(score_ref[here, s] + (add - t)) for t, s in zip(wide_tops, lanes)]
                if kernel_ref is not None:
                    for s, t in zip(lanes, terms):
                        kernel_ref[here, s] = t
                sums = tuple(u + t for u, t in zip(sums, terms))
            return sums

        start = (jnp.zeros((8, LANES), jnp.float32),) * group
        sums = lax.fori_loop(0, rows // (8 * tall), totals, start)
        for k, (t, u) in enumerate(zip(tops, sums)):
            spot = slice(first + k, first + k + 1)
            if top_ref is not None:
                top_ref[spot, :] = t
            out_ref[spot, :] = t + jnp.log2(jnp.sum(u, axis=0, keepdims=True))


def source_terms(x):
    high, mid, low = split(x * (2.0 * SCALE))
    return [high, high, mid, mid, high, low]


def target_terms(y):
    high, mid, low = split(y)
    return [high, mid, high, mid, low, high]


def pad_into(pad_ref, values):
    pad_ref[...] = jnp.zeros(pad_ref.shape, jnp.float32)
    pad_ref[0 : values.shape[0], :] = values


def live_sum(counts):
    total = counts[0]
    for i in range(1, counts.shape[0]):
        total = total + counts[i]
    return jnp.full((1, LANES), total, jnp.int32).astype(jnp.float32)


def wide(x, size):
    return jnp.concatenate([x] * (size // LANES), axis=1)


def first_kernel(
    src_hbm, tgt_hbm, count_src_hbm, count_tgt_hbm, pair,
    score_ref, lse_ref, row_aux, col_aux, own_ref, half_ref,
    src_ref, tgt_ref, count_src, count_tgt, sems,
    right_pad, left_pad, terms_ref, norm_ref, col_ref, peak_ref, total_ref,
):
    rows, cols = score_ref.shape
    dims = src_ref.shape[0]
    copies = [
        pltpu.make_async_copy(one, two, sems.at[i])
        for i, (one, two) in enumerate(
            [(count_src_hbm, count_src), (count_tgt_hbm, count_tgt), (src_hbm, src_ref), (tgt_hbm, tgt_ref)]
        )
    ]
    for copy in copies:
        copy.start()
    for ref in (right_pad, left_pad, own_ref):
        ref[...] = jnp.zeros(ref.shape, jnp.float32)
    n_half = -(-dims // 2)
    for copy in copies[:3]:
        copy.wait()
    n_rows = count_src[lax.axis_index("src")]
    n_cols = count_tgt[lax.axis_index("tgt")]
    listed = pair[0, 0] > 0
    row_live = positions(row_aux.shape[1:]) < n_rows
    col_live = positions(col_aux.shape[1:]) < n_cols
    row_aux[0] = row_live.astype(jnp.float32)
    row_aux[1] = jnp.where(row_live, -jnp.log2(live_sum(count_src)), 0.0)
    row_aux[2] = (row_live & listed).astype(jnp.float32)
    col_aux[0] = col_live.astype(jnp.float32)
    col_aux[1] = jnp.where(col_live, -jnp.log2(live_sum(count_tgt)), 0.0)
    left_pad[0:dims, :] = src_ref[...]
    left = left_pad[...]
    half = jnp.where(lax.axis_index("tgt") % 2 == 0, left[0:n_half], left[n_half : 2 * n_half])
    half_ref[...] = jnp.zeros(half_ref.shape, jnp.float32)
    for k in range(rows // LANES):
        half_ref[0, k * n_half : (k + 1) * n_half, :] = half[:, k * LANES : (k + 1) * LANES]
    put(norm_ref, -SCALE * jnp.sum(left * left, axis=0, keepdims=True))
    norm_ref[...] = jnp.where(row_live, norm_ref[...], NEG)
    to_sublanes(norm_ref, col_ref)
    terms_ref[...] = jnp.concatenate(source_terms(left.T), axis=1)
    copies[3].wait()
    size = 512

    def scores(c):
        here = pl.ds(pl.multiple_of(c * size, size), size)
        right_pad[0:dims, :] = tgt_ref[:, here]
        right = right_pad[...]
        spot = lax.broadcasted_iota(jnp.int32, (1, size), 1) + c * size
        norm = -SCALE * jnp.sum(right * right, axis=0, keepdims=True)
        norm = jnp.where((spot < n_cols) & listed, norm, NEG)
        terms = jnp.concatenate(target_terms(right), axis=0)
        cross = jnp.dot(terms_ref[...], terms, preferred_element_type=jnp.float32)
        score = cross + (wide(col_ref[...], size) + norm)
        score_ref[:, here] = score
        return [score[:, k : k + LANES] for k in range(0, size, LANES)]

    peak_ref[...] = jnp.full(peak_ref.shape, 2.0 * NEG, jnp.float32)
    total_ref[...] = jnp.zeros(total_ref.shape, jnp.float32)

    def block(c, _):
        z = scores(c)
        before = peak_ref[...]
        peak = functools.reduce(jnp.maximum, z, before)
        total_ref[...] = functools.reduce(
            jnp.add, [jnp.exp2(v - peak) for v in z], total_ref[...] * jnp.exp2(before - peak)
        )
        peak_ref[...] = peak
        return 0

    lax.fori_loop(0, cols // size, block, 0)
    share = own_ref.shape[1]
    own_ref[0:dims, :] = tgt_ref[:, pl.ds(pl.multiple_of(lax.axis_index("src") * share, share), share)]
    fold_lanes(peak_ref, total_ref, lse_ref)


def slab_kernel(own_ref, mine_ref, theirs_ref, *refs, first, n_half, prepare):
    if prepare:
        slab_ref, terms_out, token_ref, terms_ref, col_ref, right_pad, norm_ref = refs
        left = own_ref[...]
        put(norm_ref, -SCALE * jnp.sum(left * left, axis=0, keepdims=True))
        to_sublanes(norm_ref, col_ref)
        terms_ref[...] = jnp.concatenate(target_terms(left.T), axis=1)
    else:
        terms_ref, col_ref, slab_ref, terms_out, token_ref, right_pad = refs
    rows = right_pad.shape[1]
    even = lax.axis_index("tgt") % 2 == 0
    right_pad[...] = jnp.zeros(right_pad.shape, jnp.float32)
    for b in range(slab_ref.shape[1] // rows):
        mine, theirs = mine_ref[first + b], theirs_ref[first + b]
        upper = jnp.where(even, mine, theirs)
        lower = jnp.where(even, theirs, mine)
        for k in range(rows // LANES):
            here = slice(k * n_half, (k + 1) * n_half)
            right_pad[0:n_half, k * LANES : (k + 1) * LANES] = upper[here]
            right_pad[n_half : 2 * n_half, k * LANES : (k + 1) * LANES] = lower[here]
        right = right_pad[...]
        norm = -SCALE * jnp.sum(right * right, axis=0, keepdims=True)
        terms = jnp.concatenate(source_terms(right), axis=0)
        cross = jnp.dot(terms_ref[...], terms, preferred_element_type=jnp.float32)
        here = slice(b * rows, (b + 1) * rows)
        slab_ref[:, here] = cross + (wide(col_ref[...], rows) + norm)
        terms_out[here, :] = jnp.concatenate(split(right.T)[:2], axis=1)
    token_ref[...] = jnp.zeros(token_ref.shape, jnp.float32)


def row_sums(kernel_ref, factor_ref, total_ref, out_ref):
    rows, cols = kernel_ref.shape
    tall = 8

    def block(i, _):
        spots = [pl.ds(pl.multiple_of((i * tall + k) * 8, 8), 8) for k in range(tall)]
        sums = [jnp.zeros((8, LANES), jnp.float32)] * tall
        for t in range(cols // LANES):
            lanes = slice(t * LANES, (t + 1) * LANES)
            factor = jnp.broadcast_to(factor_ref[t : t + 1, :], (8, LANES))
            sums = [u + kernel_ref[s, lanes] * factor for u, s in zip(sums, spots)]
        for s, u in zip(spots, sums):
            total_ref[s, :] = u
        return 0

    lax.fori_loop(0, rows // (8 * tall), block, 0)
    for k in range(out_ref.shape[0]):
        out_ref[k : k + 1, :] = jnp.sum(total_ref[k * LANES : (k + 1) * LANES, :].T, axis=0, keepdims=True)


def col_sums(kernel_ref, factor_ref, out_ref):
    rows, cols = kernel_ref.shape
    lanes = [slice(start, start + LANES) for start in range(0, cols, LANES)]
    tall = 4

    def block(i, sums):
        for r in range(tall):
            here = pl.ds(pl.multiple_of((i * tall + r) * 8, 8), 8)
            factor = factor_ref[here, :]
            sums = tuple(u + kernel_ref[here, s] * factor for u, s in zip(sums, lanes))
        return sums

    sums = lax.fori_loop(0, rows // (8 * tall), block, (jnp.zeros((8, LANES), jnp.float32),) * len(lanes))
    for k, u in enumerate(sums):
        out_ref[k : k + 1, :] = jnp.sum(u, axis=0, keepdims=True)


def out_of_range(total, needed, factor, most):
    small = jnp.where(needed & jnp.logical_not(total >= SUM_MIN), 1.0, 0.0)
    large = jnp.where(factor <= most, 0.0, 1.0)
    return jnp.max(jnp.maximum(jnp.max(small, axis=0, keepdims=True), jnp.max(large, axis=0, keepdims=True))) > 0.5


def set_f(lse_ref, aux_ref, f_ref, masked_ref):
    f = aux_ref[1] - lse_ref[...] * aux_ref[0]
    f_ref[...] = f
    masked_ref[...] = jnp.where(aux_ref[2] > 0, f, NEG)


def first_col_kernel(score_ref, lse_ref, aux_ref, out_ref, f_ref, kernel_ref, top_ref, masked_ref, col_ref):
    set_f(lse_ref, aux_ref, f_ref, masked_ref)
    to_sublanes(f_ref, col_ref)
    col_lse(score_ref, col_ref, out_ref, kernel_ref, top_ref)


def col_kernel(
    score_ref, kernel_ref, top_ref, base_ref, lse_ref, aux_ref, out_ref, f_ref, masked_ref, factor_ref, col_ref
):
    set_f(lse_ref, aux_ref, f_ref, masked_ref)
    factor_ref[...] = jnp.exp2(f_ref[...] - base_ref[...])
    to_sublanes(factor_ref, col_ref)
    col_sums(kernel_ref, col_ref, out_ref)
    total = out_ref[...]
    top = top_ref[...]
    redo = out_of_range(total, top > 0.5 * NEG, factor_ref[...], ROW_FACTOR_MAX)
    out_ref[...] = jnp.where(total > 0, top + jnp.log2(total), NEG)

    @pl.when(redo)
    def _():
        to_sublanes(f_ref, col_ref)
        col_lse(score_ref, col_ref, out_ref)


def merged(parts):
    peak = jnp.max(parts, axis=0)
    return peak + jnp.log2(jnp.sum(jnp.exp2(parts - peak[None]), axis=0))


def row_kernel(
    score_ref, kernel_ref, top_ref, base_ref, parts_ref, row_aux, col_aux, out_ref,
    g_ref, factor_ref, peak_ref, total_ref,
):
    lse = merged(parts_ref[...])
    g_ref[...] = col_aux[1] - lse * col_aux[0]
    factor_ref[...] = jnp.where(col_aux[0] > 0, jnp.exp2(top_ref[...] - lse + 2.0 * SHIFT), 0.0)
    row_sums(kernel_ref, factor_ref, total_ref, out_ref)
    total = out_ref[...]
    redo = out_of_range(total, row_aux[2] > 0, factor_ref[...], COL_FACTOR_MAX)
    log_b = col_aux[1, 0:1, 0:1]
    out_ref[...] = jnp.where(total > 0, jnp.log2(total) - 2.0 * SHIFT - base_ref[...] + log_b, NEG)

    @pl.when(redo)
    def _():
        row_lse(score_ref, g_ref, peak_ref, total_ref, out_ref)


def last_kernel(*refs, pieces):
    slabs, refs = refs[: len(pieces)], refs[len(pieces) :]
    terms, refs = refs[: len(pieces)], refs[len(pieces) :]
    parts_ref, aux_ref, f_ref, *_, out_ref, f_out, g_out, lse_ref, own_ref, col_ref, sum_ref = refs
    n_col = aux_ref.shape[1]
    lse = merged(parts_ref[:, 0:n_col, :])
    lse_ref[...] = lse
    f_out[...] = f_ref[...] * (1.0 / SCALE)
    g_out[...] = (aux_ref[1] - lse * aux_ref[0]) * (1.0 / SCALE)
    me = lax.axis_index("src")
    n_own = own_ref.shape[0]
    for k in range(n_own):
        spot = pl.ds(me * n_own + k, 1)
        own_ref[k : k + 1, :] = jnp.where(aux_ref[0, spot, :] > 0, -lse_ref[spot, :], NEG)
    to_sublanes(own_ref, col_ref)
    for i, (slab_ref, terms_ref, offsets) in enumerate(zip(slabs, terms, pieces)):
        high, mid = [], []
        start = 0
        for offset in offsets:
            for row in range(n_col, parts_ref.shape[1]):
                add = col_ref[...] + parts_ref[me ^ offset, row : row + 1, :]
                term = split(jnp.exp2(slab_ref[:, start : start + LANES] + add))
                high.append(term[0])
                mid.append(term[1])
                start += LANES
        sums = jnp.dot(
            jnp.concatenate(high + mid, axis=1), jnp.concatenate([terms_ref[...]] * 2, axis=0),
            preferred_element_type=jnp.float32,
        )
        if i == 0:
            sum_ref[...] = sums
        else:
            sum_ref[...] += sums
    sums = sum_ref[...].T
    out_ref[...] = (sums[0:DEPTH] + sums[DEPTH :])[0 : out_ref.shape[0]]


def merge(one, two):
    top = jnp.maximum(one, two)
    return top + jnp.log2(1.0 + jnp.exp2(jnp.minimum(one, two) - top))


def swap(value, axis, step):
    return lax.ppermute(value, axis, [(i, i ^ step) for i in range(lax.axis_size(axis))])


def doubling(size):
    return [1 << k for k in range(size.bit_length() - 1)]


def buffer(space, shape):
    return space(*shape) if isinstance(shape[0], tuple) else space(shape, jnp.float32)


def call(kernel, outs, scratch, ins, flops, expos=0, pin=True):
    return pl.pallas_call(
        kernel,
        out_shape=[buffer(pltpu.VMEM if pin else jax.ShapeDtypeStruct, shape) for shape in outs],
        in_specs=[VMEM_SPEC] * len(ins),
        out_specs=[VMEM_SPEC] * len(outs),
        scratch_shapes=[buffer(pltpu.VMEM, shape) for shape in scratch],
        compiler_params=pltpu.CompilerParams(vmem_limit_bytes=VMEM_LIMIT),
        cost_estimate=pl.CostEstimate(flops=flops, bytes_accessed=0, transcendentals=expos),
    )(*[pinned(x) for x in ins])


def tie(*values):
    return lax.optimization_barrier(values)


class Beside:
    def __init__(self, half, own, bits, rows, n_half):
        self.own = own
        self.rows = rows
        self.n_half = n_half
        self.blocks = {0: half}
        self.coming = {}
        if len(bits) >= 3:
            z, w, x = bits[:3]
            self.fetches = [[(0, z), (0, w), (0, x)], [(z, x), (w, z)], [(w, x), (w ^ z, x)], []]
            self.groups = [[], [0, z, w, x], [z ^ x, w ^ z], [w ^ x, w ^ z ^ x]]
            self.bits = bits[3:]
        else:
            self.fetches = [[]] * ITERS
            self.groups = [[]] * (ITERS - 1) + [[0]]
            self.bits = bits
        self.ready = None
        self.mine = []
        self.theirs = []
        self.offsets = []
        self.todo = []
        self.tokens = []
        self.slabs = []
        self.terms = []
        self.done = []

    def start(self, step, value, exchange):
        used = sorted({offset for offset, _ in self.fetches[step]} | set(self.groups[step]))
        if step and used:
            value, *held = tie(value, *[self.blocks[offset] for offset in used])
            self.blocks.update(zip(used, held))
        others = exchange(value)
        for offset, bit in self.fetches[step]:
            self.coming[offset ^ bit] = swap(self.blocks[offset], "src", bit)
        if self.groups[step]:
            held = [self.blocks[offset] for offset in self.groups[step]]
            self.add(held[0] if len(held) == 1 else jnp.concatenate(held, axis=0), self.groups[step])
        return others

    def add(self, mine, offsets):
        group = len(self.mine)
        self.mine.append(mine)
        self.theirs.append(swap(mine, "tgt", 1))
        self.offsets.append(offsets)
        self.todo += [(group, first, min(2, len(offsets))) for first in range(0, len(offsets), 2)]

    def land(self, value):
        if self.coming:
            value, *held = tie(value, *self.coming.values())
            self.blocks.update(zip(self.coming, held))
            self.coming = {}
        return value

    def piece(self):
        group, first, size = self.todo.pop(0)
        share = self.own.shape[1]
        rows = self.rows
        prepare = self.ready is None
        slab, terms, token, *ready = call(
            functools.partial(slab_kernel, first=first, n_half=self.n_half, prepare=prepare),
            [(share, size * rows), ((size * rows, 2 * DEPTH), jnp.bfloat16), (8, LANES)]
            + [((share, 6 * DEPTH), jnp.bfloat16), (share, LANES)] * prepare,
            [(DEPTH, rows)] + [(share // LANES, LANES)] * prepare,
            [self.own, self.mine[group], self.theirs[group], *(self.ready or [])],
            12 * DEPTH * share * size * rows,
        )
        self.ready = ready or self.ready
        self.terms.append(terms)
        self.slabs.append(slab)
        self.done.append(self.offsets[group][first : first + size])
        return token

    def hold(self, value):
        value, self.own = tie(value, self.own)
        return value

    def pieces(self, value, most):
        for _ in range(min(most, len(self.todo))):
            value, token = tie(value, self.piece())
            self.tokens.append(token)
        return value

    def finish(self, value):
        for bit in self.bits:
            for mine, offsets in list(zip(self.mine, self.offsets)):
                self.add(swap(mine, "src", bit), [offset ^ bit for offset in offsets])
        return self.pieces(self.hold(value), len(self.todo))


def shards(sources, targets, pair_active, count_src, count_tgt):
    dims, rows = sources.shape
    cols = targets.shape[1]
    n_src = lax.axis_size("src")
    share = cols // n_src
    column = (rows, LANES)
    by_row = (rows // LANES, LANES)
    by_col = (cols // LANES, LANES)
    pairs = rows * cols
    hbm = [pltpu.with_memory_space_constraint(x, pltpu.HBM) for x in (sources, targets, count_src, count_tgt)]
    n_half = -(-dims // 2)
    packed = -(-n_half * by_row[0] // 8) * 8
    outs = [(rows, cols), by_row, (3, *by_row), (3, *by_col), (DEPTH, share), (1, packed, LANES)]
    score, lse, row_aux, col_aux, own, half = pl.pallas_call(
        first_kernel,
        out_shape=[pltpu.VMEM(shape, jnp.float32) for shape in outs],
        in_specs=[pl.BlockSpec(memory_space=pltpu.HBM)] * 4 + [SMEM_SPEC],
        out_specs=[VMEM_SPEC] * len(outs),
        scratch_shapes=[
            pltpu.VMEM((dims, rows), jnp.float32),
            pltpu.VMEM((dims, cols), jnp.float32),
            pltpu.SMEM(count_src.shape, jnp.int32),
            pltpu.SMEM(count_tgt.shape, jnp.int32),
            pltpu.SemaphoreType.DMA((4,)),
            pltpu.VMEM((DEPTH, 512), jnp.float32),
            pltpu.VMEM((DEPTH, rows), jnp.float32),
            pltpu.VMEM((rows, 6 * DEPTH), jnp.bfloat16),
            pltpu.VMEM(by_row, jnp.float32),
            pltpu.VMEM(column, jnp.float32),
            pltpu.VMEM(column, jnp.float32),
            pltpu.VMEM(column, jnp.float32),
        ],
        compiler_params=pltpu.CompilerParams(vmem_limit_bytes=VMEM_LIMIT),
        cost_estimate=pl.CostEstimate(flops=12 * DEPTH * pairs, bytes_accessed=0, transcendentals=pairs),
    )(*hbm, pair_active)
    over_tgt = doubling(lax.axis_size("tgt"))
    over_src = doubling(n_src)
    over_src = over_src[1:] + over_src[:1]
    side = Beside(half, own, over_src, rows, n_half)
    near = [bit for bit in (2, 3, 1) if bit < lax.axis_size("tgt")]

    def exchange(value):
        return [swap(value, "tgt", bit) for bit in near]

    def combine(value, others):
        values = dict(zip(near, others))
        value = merge(value, values[1])
        return merge(value, merge(values[2], values[3])) if 2 in values else value

    for step in range(ITERS):
        if step == ITERS - 1:
            lse = side.hold(lse)
        others = side.start(step, lse, exchange)
        if step == ITERS - 1:
            others[0] = side.pieces(others[0], 1)
        lse = combine(lse, others)
        for bit in over_tgt[2:]:
            lse = merge(lse, swap(lse, "tgt", bit))
        if step == 0:
            lse, base, kernel, top = call(
                first_col_kernel,
                [by_col, by_row, (rows, cols), by_col],
                [by_row, column], [score, lse, row_aux], 0,
            )
        else:
            last = step == ITERS - 1
            outs = [by_col, by_row, by_row] if last else [by_col]
            scratch = [by_row, column] if last else [by_row, by_row, by_row, column]
            lse, *held = call(col_kernel, outs, scratch, [score, kernel, top, base, lse, row_aux], 0)
            if last:
                f, masked = held
        if step < ITERS - 1:
            lse = side.land(side.pieces(side.hold(lse), step))
            lse = lax.all_to_all(jnp.broadcast_to(lse, (n_src, *by_col)), "src", 0, 0, tiled=True)
            (lse,) = call(
                row_kernel,
                [by_row],
                [by_col, by_col, column, column],
                [score, kernel, top, base, lse, row_aux, col_aux], 0,
            )
    lse = side.finish(lse)
    both = jnp.concatenate([lse, masked], axis=0)
    both = lax.all_to_all(jnp.broadcast_to(both, (n_src, *both.shape)), "src", 0, 0, tiled=True)
    ancestors, f, g = call(
        functools.partial(last_kernel, pieces=side.done),
        [(dims, share), by_row, by_col],
        [by_col, (share // LANES, LANES), (share, LANES), (share, 2 * DEPTH)],
        [*side.slabs, *side.terms, both, col_aux, f, *side.tokens],
        18 * DEPTH * pairs, pairs, pin=False,
    )
    return (f.reshape(rows), g.reshape(cols), ancestors)


def solution(mesh):
    return jax.shard_map(
        shards,
        mesh=mesh,
        in_specs=(P(None, "src"), P(None, "tgt"), P("src", "tgt"), P(), P()),
        out_specs=(P("src"), P("tgt"), P(None, ("tgt", "src"))),
        check_vma=False,
    )
```

```python
import functools
import math

import jax
import jax.numpy as jnp
from jax import lax
from jax.experimental import pallas as pl
from jax.experimental.pallas import tpu as pltpu
from jax.sharding import PartitionSpec as P

ITERS = 4
EPS = 0.02
NEG = -1e30
LOG2E = math.log2(math.e)
SCALE = LOG2E / EPS
LANES = 128
DEPTH = 64
SHIFT = 40.0
ROW_FACTOR_MAX = 2.0**20
COL_FACTOR_MAX = 2.0**60
SUM_MIN = 2.0**-30
VMEM_LIMIT = 14 * 1024 * 1024

VMEM_SPEC = pl.BlockSpec(memory_space=pltpu.VMEM)
SMEM_SPEC = pl.BlockSpec(memory_space=pltpu.SMEM)


def pinned(x):
    return pltpu.with_memory_space_constraint(x, pltpu.VMEM)


def split(x):
    high = x.astype(jnp.bfloat16)
    rest = x - high.astype(jnp.float32)
    mid = rest.astype(jnp.bfloat16)
    low = (rest - mid.astype(jnp.float32)).astype(jnp.bfloat16)
    return high, mid, low


def put(ref, row):
    for k in range(row.shape[1] // LANES):
        ref[k : k + 1, :] = row[:, k * LANES : (k + 1) * LANES]


def positions(shape):
    return lax.broadcasted_iota(jnp.int32, shape, 0) * LANES + lax.broadcasted_iota(jnp.int32, shape, 1)


def to_sublanes(vector_ref, col_ref):
    for k in range(vector_ref.shape[0]):
        col_ref[k * LANES : (k + 1) * LANES, :] = jnp.broadcast_to(vector_ref[k : k + 1, :], (LANES, LANES)).T


def fold_lanes(peak_ref, total_ref, out_ref):
    for k in range(out_ref.shape[0]):
        here = slice(k * LANES, (k + 1) * LANES)
        peaks = peak_ref[here, :].T
        top = jnp.max(peaks, axis=0, keepdims=True)
        total = jnp.sum(total_ref[here, :].T * jnp.exp2(peaks - top), axis=0, keepdims=True)
        out_ref[k : k + 1, :] = top + jnp.log2(total)


def row_lse(score_ref, add_ref, peak_ref, total_ref, out_ref):
    rows, cols = score_ref.shape

    def block(i, _):
        here = pl.ds(pl.multiple_of(i * 8, 8), 8)
        z = []
        for k in range(cols // LANES):
            z.append(score_ref[here, k * LANES : (k + 1) * LANES] + add_ref[k : k + 1, :])
        peak = functools.reduce(jnp.maximum, z)
        peak_ref[here, :] = peak
        total_ref[here, :] = functools.reduce(jnp.add, [jnp.exp2(v - peak) for v in z])
        return 0

    lax.fori_loop(0, rows // 8, block, 0)
    fold_lanes(peak_ref, total_ref, out_ref)


def col_lse(score_ref, add_ref, out_ref, kernel_ref=None, top_ref=None):
    rows, cols = score_ref.shape
    group = 16
    tall = 4

    for first in range(0, cols // LANES, group):
        lanes = [slice((first + k) * LANES, (first + k + 1) * LANES) for k in range(group)]

        def peaks(i, tops):
            for r in range(tall):
                here = pl.ds(pl.multiple_of((i * tall + r) * 8, 8), 8)
                add = add_ref[here, :]
                tops = tuple(jnp.maximum(t, score_ref[here, s] + add) for t, s in zip(tops, lanes))
            return tops

        start = (jnp.full((8, LANES), -jnp.inf, jnp.float32),) * group
        tops = lax.fori_loop(0, rows // (8 * tall), peaks, start)
        tops = [jnp.max(t, axis=0, keepdims=True) - SHIFT for t in tops]
        wide_tops = [jnp.broadcast_to(t, (8, LANES)) for t in tops]

        def totals(i, sums):
            for r in range(tall):
                here = pl.ds(pl.multiple_of((i * tall + r) * 8, 8), 8)
                add = add_ref[here, :]
                terms = [jnp.exp2(score_ref[here, s] + (add - t)) for t, s in zip(wide_tops, lanes)]
                if kernel_ref is not None:
                    for s, t in zip(lanes, terms):
                        kernel_ref[here, s] = t
                sums = tuple(u + t for u, t in zip(sums, terms))
            return sums

        start = (jnp.zeros((8, LANES), jnp.float32),) * group
        sums = lax.fori_loop(0, rows // (8 * tall), totals, start)
        for k, (t, u) in enumerate(zip(tops, sums)):
            spot = slice(first + k, first + k + 1)
            if top_ref is not None:
                top_ref[spot, :] = t
            out_ref[spot, :] = t + jnp.log2(jnp.sum(u, axis=0, keepdims=True))


def source_terms(x):
    high, mid, low = split(x * (2.0 * SCALE))
    return [high, high, mid, mid, high, low]


def target_terms(y):
    high, mid, low = split(y)
    return [high, mid, high, mid, low, high]


def pad_into(pad_ref, values):
    pad_ref[...] = jnp.zeros(pad_ref.shape, jnp.float32)
    pad_ref[0 : values.shape[0], :] = values


def live_sum(counts):
    total = counts[0]
    for i in range(1, counts.shape[0]):
        total = total + counts[i]
    return jnp.full((1, LANES), total, jnp.int32).astype(jnp.float32)


def wide(x, size):
    return jnp.concatenate([x] * (size // LANES), axis=1)


def first_kernel(
    src_hbm, tgt_hbm, count_src_hbm, count_tgt_hbm, pair,
    score_ref, lse_ref, row_aux, col_aux, own_ref, half_ref,
    src_ref, tgt_ref, count_src, count_tgt, sems,
    right_pad, left_pad, terms_ref, norm_ref, col_ref, peak_ref, total_ref,
):
    rows, cols = score_ref.shape
    dims = src_ref.shape[0]
    copies = [
        pltpu.make_async_copy(one, two, sems.at[i])
        for i, (one, two) in enumerate(
            [(count_src_hbm, count_src), (count_tgt_hbm, count_tgt), (src_hbm, src_ref), (tgt_hbm, tgt_ref)]
        )
    ]
    for copy in copies:
        copy.start()
    for ref in (right_pad, left_pad, own_ref):
        ref[...] = jnp.zeros(ref.shape, jnp.float32)
    n_half = -(-dims // 2)
    for copy in copies[:3]:
        copy.wait()
    n_rows = count_src[lax.axis_index("src")]
    n_cols = count_tgt[lax.axis_index("tgt")]
    listed = pair[0, 0] > 0
    row_live = positions(row_aux.shape[1:]) < n_rows
    col_live = positions(col_aux.shape[1:]) < n_cols
    row_aux[0] = row_live.astype(jnp.float32)
    row_aux[1] = jnp.where(row_live, -jnp.log2(live_sum(count_src)), 0.0)
    row_aux[2] = (row_live & listed).astype(jnp.float32)
    col_aux[0] = col_live.astype(jnp.float32)
    col_aux[1] = jnp.where(col_live, -jnp.log2(live_sum(count_tgt)), 0.0)
    left_pad[0:dims, :] = src_ref[...]
    left = left_pad[...]
    half = jnp.where(lax.axis_index("tgt") % 2 == 0, left[0:n_half], left[n_half : 2 * n_half])
    half_ref[...] = jnp.zeros(half_ref.shape, jnp.float32)
    for k in range(rows // LANES):
        half_ref[0, k * n_half : (k + 1) * n_half, :] = half[:, k * LANES : (k + 1) * LANES]
    put(norm_ref, -SCALE * jnp.sum(left * left, axis=0, keepdims=True))
    norm_ref[...] = jnp.where(row_live, norm_ref[...], NEG)
    to_sublanes(norm_ref, col_ref)
    terms_ref[...] = jnp.concatenate(source_terms(left.T), axis=1)
    copies[3].wait()
    size = 512

    def scores(c):
        here = slice(c * size, (c + 1) * size)
        right_pad[0:dims, :] = tgt_ref[:, here]
        right = right_pad[...]
        spot = lax.broadcasted_iota(jnp.int32, (1, size), 1) + c * size
        norm = -SCALE * jnp.sum(right * right, axis=0, keepdims=True)
        norm = jnp.where((spot < n_cols) & listed, norm, NEG)
        terms = jnp.concatenate(target_terms(right), axis=0)
        cross = jnp.dot(terms_ref[...], terms, preferred_element_type=jnp.float32)
        score = cross + (wide(col_ref[...], size) + norm)
        score_ref[:, here] = score
        return [score[:, k : k + LANES] for k in range(0, size, LANES)]

    peak_ref[...] = jnp.full(peak_ref.shape, 2.0 * NEG, jnp.float32)
    total_ref[...] = jnp.zeros(total_ref.shape, jnp.float32)

    for c in range(cols // size):
        z = scores(c)
        before = peak_ref[...]
        peak = functools.reduce(jnp.maximum, z, before)
        total_ref[...] = functools.reduce(
            jnp.add, [jnp.exp2(v - peak) for v in z], total_ref[...] * jnp.exp2(before - peak)
        )
        peak_ref[...] = peak
    share = own_ref.shape[1]
    own_ref[0:dims, :] = tgt_ref[:, pl.ds(pl.multiple_of(lax.axis_index("src") * share, share), share)]
    fold_lanes(peak_ref, total_ref, lse_ref)


def slab_kernel(own_ref, mine_ref, theirs_ref, *refs, first, n_half, prepare):
    if prepare:
        slab_ref, terms_out, token_ref, terms_ref, col_ref, right_pad, norm_ref = refs
        left = own_ref[...]
        put(norm_ref, -SCALE * jnp.sum(left * left, axis=0, keepdims=True))
        to_sublanes(norm_ref, col_ref)
        terms_ref[...] = jnp.concatenate(target_terms(left.T), axis=1)
    else:
        terms_ref, col_ref, slab_ref, terms_out, token_ref, right_pad = refs
    rows = right_pad.shape[1]
    even = lax.axis_index("tgt") % 2 == 0
    right_pad[...] = jnp.zeros(right_pad.shape, jnp.float32)
    for b in range(slab_ref.shape[1] // rows):
        mine, theirs = mine_ref[first + b], theirs_ref[first + b]
        upper = jnp.where(even, mine, theirs)
        lower = jnp.where(even, theirs, mine)
        for k in range(rows // LANES):
            here = slice(k * n_half, (k + 1) * n_half)
            right_pad[0:n_half, k * LANES : (k + 1) * LANES] = upper[here]
            right_pad[n_half : 2 * n_half, k * LANES : (k + 1) * LANES] = lower[here]
        right = right_pad[...]
        norm = -SCALE * jnp.sum(right * right, axis=0, keepdims=True)
        terms = jnp.concatenate(source_terms(right), axis=0)
        cross = jnp.dot(terms_ref[...], terms, preferred_element_type=jnp.float32)
        here = slice(b * rows, (b + 1) * rows)
        slab_ref[:, here] = cross + (wide(col_ref[...], rows) + norm)
        terms_out[here, :] = jnp.concatenate(split(right.T)[:2], axis=1)
    token_ref[...] = jnp.zeros(token_ref.shape, jnp.float32)


def row_sums(kernel_ref, factor_ref, total_ref, out_ref):
    rows, cols = kernel_ref.shape
    tall = 8

    def block(i, _):
        spots = [pl.ds(pl.multiple_of((i * tall + k) * 8, 8), 8) for k in range(tall)]
        sums = [jnp.zeros((8, LANES), jnp.float32)] * tall
        for t in range(cols // LANES):
            lanes = slice(t * LANES, (t + 1) * LANES)
            factor = jnp.broadcast_to(factor_ref[t : t + 1, :], (8, LANES))
            sums = [u + kernel_ref[s, lanes] * factor for u, s in zip(sums, spots)]
        for s, u in zip(spots, sums):
            total_ref[s, :] = u
        return 0

    lax.fori_loop(0, rows // (8 * tall), block, 0)
    for k in range(out_ref.shape[0]):
        out_ref[k : k + 1, :] = jnp.sum(total_ref[k * LANES : (k + 1) * LANES, :].T, axis=0, keepdims=True)


def col_sums(kernel_ref, factor_ref, out_ref):
    rows, cols = kernel_ref.shape
    lanes = [slice(start, start + LANES) for start in range(0, cols, LANES)]
    tall = 4

    def block(i, sums):
        for r in range(tall):
            here = pl.ds(pl.multiple_of((i * tall + r) * 8, 8), 8)
            factor = factor_ref[here, :]
            sums = tuple(u + kernel_ref[here, s] * factor for u, s in zip(sums, lanes))
        return sums

    sums = lax.fori_loop(0, rows // (8 * tall), block, (jnp.zeros((8, LANES), jnp.float32),) * len(lanes))
    for k, u in enumerate(sums):
        out_ref[k : k + 1, :] = jnp.sum(u, axis=0, keepdims=True)


def out_of_range(total, needed, factor, most):
    small = jnp.where(needed & jnp.logical_not(total >= SUM_MIN), 1.0, 0.0)
    large = jnp.where(factor <= most, 0.0, 1.0)
    return jnp.max(jnp.maximum(jnp.max(small, axis=0, keepdims=True), jnp.max(large, axis=0, keepdims=True))) > 0.5


def set_f(lse_ref, aux_ref, f_ref, masked_ref):
    f = aux_ref[1] - lse_ref[...] * aux_ref[0]
    f_ref[...] = f
    masked_ref[...] = jnp.where(aux_ref[2] > 0, f, NEG)


def first_col_kernel(score_ref, lse_ref, aux_ref, out_ref, f_ref, kernel_ref, top_ref, masked_ref, col_ref):
    set_f(lse_ref, aux_ref, f_ref, masked_ref)
    to_sublanes(f_ref, col_ref)
    col_lse(score_ref, col_ref, out_ref, kernel_ref, top_ref)


def col_kernel(
    score_ref, kernel_ref, top_ref, base_ref, lse_ref, aux_ref, out_ref, f_ref, masked_ref, factor_ref, col_ref
):
    set_f(lse_ref, aux_ref, f_ref, masked_ref)
    factor_ref[...] = jnp.exp2(f_ref[...] - base_ref[...])
    to_sublanes(factor_ref, col_ref)
    col_sums(kernel_ref, col_ref, out_ref)
    total = out_ref[...]
    top = top_ref[...]
    redo = out_of_range(total, top > 0.5 * NEG, factor_ref[...], ROW_FACTOR_MAX)
    out_ref[...] = jnp.where(total > 0, top + jnp.log2(total), NEG)

    @pl.when(redo)
    def _():
        to_sublanes(f_ref, col_ref)
        col_lse(score_ref, col_ref, out_ref)


def merged(parts):
    peak = jnp.max(parts, axis=0)
    return peak + jnp.log2(jnp.sum(jnp.exp2(parts - peak[None]), axis=0))


def row_kernel(
    score_ref, kernel_ref, top_ref, base_ref, parts_ref, row_aux, col_aux, out_ref,
    g_ref, factor_ref, peak_ref, total_ref,
):
    lse = merged(parts_ref[...])
    g_ref[...] = col_aux[1] - lse * col_aux[0]
    factor_ref[...] = jnp.where(col_aux[0] > 0, jnp.exp2(top_ref[...] - lse + 2.0 * SHIFT), 0.0)
    row_sums(kernel_ref, factor_ref, total_ref, out_ref)
    total = out_ref[...]
    redo = out_of_range(total, row_aux[2] > 0, factor_ref[...], COL_FACTOR_MAX)
    log_b = col_aux[1, 0:1, 0:1]
    out_ref[...] = jnp.where(total > 0, jnp.log2(total) - 2.0 * SHIFT - base_ref[...] + log_b, NEG)

    @pl.when(redo)
    def _():
        row_lse(score_ref, g_ref, peak_ref, total_ref, out_ref)


def last_kernel(*refs, pieces):
    slabs, refs = refs[: len(pieces)], refs[len(pieces) :]
    terms, refs = refs[: len(pieces)], refs[len(pieces) :]
    parts_ref, aux_ref, f_ref, *_, out_ref, f_out, g_out, lse_ref, own_ref, col_ref, sum_ref = refs
    n_col = aux_ref.shape[1]
    lse = merged(parts_ref[:, 0:n_col, :])
    lse_ref[...] = lse
    f_out[...] = f_ref[...] * (1.0 / SCALE)
    g_out[...] = (aux_ref[1] - lse * aux_ref[0]) * (1.0 / SCALE)
    me = lax.axis_index("src")
    n_own = own_ref.shape[0]
    for k in range(n_own):
        spot = pl.ds(me * n_own + k, 1)
        own_ref[k : k + 1, :] = jnp.where(aux_ref[0, spot, :] > 0, -lse_ref[spot, :], NEG)
    to_sublanes(own_ref, col_ref)
    for i, (slab_ref, terms_ref, offsets) in enumerate(zip(slabs, terms, pieces)):
        high, mid = [], []
        start = 0
        for offset in offsets:
            for row in range(n_col, parts_ref.shape[1]):
                add = col_ref[...] + parts_ref[me ^ offset, row : row + 1, :]
                term = split(jnp.exp2(slab_ref[:, start : start + LANES] + add))
                high.append(term[0])
                mid.append(term[1])
                start += LANES
        sums = jnp.dot(
            jnp.concatenate(high + mid, axis=1), jnp.concatenate([terms_ref[...]] * 2, axis=0),
            preferred_element_type=jnp.float32,
        )
        if i == 0:
            sum_ref[...] = sums
        else:
            sum_ref[...] += sums
    sums = sum_ref[...].T
    out_ref[...] = (sums[0:DEPTH] + sums[DEPTH :])[0 : out_ref.shape[0]]


def merge(one, two):
    top = jnp.maximum(one, two)
    return top + jnp.log2(1.0 + jnp.exp2(jnp.minimum(one, two) - top))


def swap(value, axis, step):
    return lax.ppermute(value, axis, [(i, i ^ step) for i in range(lax.axis_size(axis))])


def doubling(size):
    return [1 << k for k in range(size.bit_length() - 1)]


def buffer(space, shape):
    return space(*shape) if isinstance(shape[0], tuple) else space(shape, jnp.float32)


def call(kernel, outs, scratch, ins, flops, expos=0, pin=True):
    return pl.pallas_call(
        kernel,
        out_shape=[buffer(pltpu.VMEM if pin else jax.ShapeDtypeStruct, shape) for shape in outs],
        in_specs=[VMEM_SPEC] * len(ins),
        out_specs=[VMEM_SPEC] * len(outs),
        scratch_shapes=[buffer(pltpu.VMEM, shape) for shape in scratch],
        compiler_params=pltpu.CompilerParams(vmem_limit_bytes=VMEM_LIMIT),
        cost_estimate=pl.CostEstimate(flops=flops, bytes_accessed=0, transcendentals=expos),
    )(*[pinned(x) for x in ins])


def tie(*values):
    return lax.optimization_barrier(values)


class Beside:
    def __init__(self, half, own, bits, rows, n_half):
        self.own = own
        self.rows = rows
        self.n_half = n_half
        self.blocks = {0: half}
        self.coming = {}
        if len(bits) >= 3:
            z, w, x = bits[:3]
            self.fetches = [[(0, z), (0, w), (0, x)], [(z, x), (w, z)], [(w, x), (w ^ z, x)], []]
            self.groups = [[], [0, z, w, x], [z ^ x, w ^ z], [w ^ x, w ^ z ^ x]]
            self.bits = bits[3:]
        else:
            self.fetches = [[]] * ITERS
            self.groups = [[]] * (ITERS - 1) + [[0]]
            self.bits = bits
        self.ready = None
        self.mine = []
        self.theirs = []
        self.offsets = []
        self.todo = []
        self.tokens = []
        self.slabs = []
        self.terms = []
        self.done = []

    def start(self, step, value, exchange):
        used = sorted({offset for offset, _ in self.fetches[step]} | set(self.groups[step]))
        if step and used:
            value, *held = tie(value, *[self.blocks[offset] for offset in used])
            self.blocks.update(zip(used, held))
        others = exchange(value)
        for offset, bit in self.fetches[step]:
            self.coming[offset ^ bit] = swap(self.blocks[offset], "src", bit)
        if self.groups[step]:
            held = [self.blocks[offset] for offset in self.groups[step]]
            self.add(held[0] if len(held) == 1 else jnp.concatenate(held, axis=0), self.groups[step])
        return others

    def add(self, mine, offsets):
        group = len(self.mine)
        self.mine.append(mine)
        self.theirs.append(swap(mine, "tgt", 1))
        self.offsets.append(offsets)
        self.todo += [(group, first, min(2, len(offsets))) for first in range(0, len(offsets), 2)]

    def land(self, value):
        if self.coming:
            value, *held = tie(value, *self.coming.values())
            self.blocks.update(zip(self.coming, held))
            self.coming = {}
        return value

    def piece(self):
        group, first, size = self.todo.pop(0)
        share = self.own.shape[1]
        rows = self.rows
        prepare = self.ready is None
        slab, terms, token, *ready = call(
            functools.partial(slab_kernel, first=first, n_half=self.n_half, prepare=prepare),
            [(share, size * rows), ((size * rows, 2 * DEPTH), jnp.bfloat16), (8, LANES)]
            + [((share, 6 * DEPTH), jnp.bfloat16), (share, LANES)] * prepare,
            [(DEPTH, rows)] + [(share // LANES, LANES)] * prepare,
            [self.own, self.mine[group], self.theirs[group], *(self.ready or [])],
            12 * DEPTH * share * size * rows,
        )
        self.ready = ready or self.ready
        self.terms.append(terms)
        self.slabs.append(slab)
        self.done.append(self.offsets[group][first : first + size])
        return token

    def hold(self, value):
        value, self.own = tie(value, self.own)
        return value

    def pieces(self, value, most):
        for _ in range(min(most, len(self.todo))):
            value, token = tie(value, self.piece())
            self.tokens.append(token)
        return value

    def finish(self, value):
        for bit in self.bits:
            for mine, offsets in list(zip(self.mine, self.offsets)):
                self.add(swap(mine, "src", bit), [offset ^ bit for offset in offsets])
        return self.pieces(self.hold(value), len(self.todo))


def shards(sources, targets, pair_active, count_src, count_tgt):
    dims, rows = sources.shape
    cols = targets.shape[1]
    n_src = lax.axis_size("src")
    share = cols // n_src
    column = (rows, LANES)
    by_row = (rows // LANES, LANES)
    by_col = (cols // LANES, LANES)
    pairs = rows * cols
    hbm = [pltpu.with_memory_space_constraint(x, pltpu.HBM) for x in (sources, targets, count_src, count_tgt)]
    n_half = -(-dims // 2)
    packed = -(-n_half * by_row[0] // 8) * 8
    outs = [(rows, cols), by_row, (3, *by_row), (3, *by_col), (DEPTH, share), (1, packed, LANES)]
    score, lse, row_aux, col_aux, own, half = pl.pallas_call(
        first_kernel,
        out_shape=[pltpu.VMEM(shape, jnp.float32) for shape in outs],
        in_specs=[pl.BlockSpec(memory_space=pltpu.HBM)] * 4 + [SMEM_SPEC],
        out_specs=[VMEM_SPEC] * len(outs),
        scratch_shapes=[
            pltpu.VMEM((dims, rows), jnp.float32),
            pltpu.VMEM((dims, cols), jnp.float32),
            pltpu.SMEM(count_src.shape, jnp.int32),
            pltpu.SMEM(count_tgt.shape, jnp.int32),
            pltpu.SemaphoreType.DMA((4,)),
            pltpu.VMEM((DEPTH, 512), jnp.float32),
            pltpu.VMEM((DEPTH, rows), jnp.float32),
            pltpu.VMEM((rows, 6 * DEPTH), jnp.bfloat16),
            pltpu.VMEM(by_row, jnp.float32),
            pltpu.VMEM(column, jnp.float32),
            pltpu.VMEM(column, jnp.float32),
            pltpu.VMEM(column, jnp.float32),
        ],
        compiler_params=pltpu.CompilerParams(vmem_limit_bytes=VMEM_LIMIT),
        cost_estimate=pl.CostEstimate(flops=12 * DEPTH * pairs, bytes_accessed=0, transcendentals=pairs),
    )(*hbm, pair_active)
    over_tgt = doubling(lax.axis_size("tgt"))
    over_src = doubling(n_src)
    over_src = over_src[1:] + over_src[:1]
    side = Beside(half, own, over_src, rows, n_half)
    near = [bit for bit in (2, 3, 1) if bit < lax.axis_size("tgt")]

    def exchange(value):
        return [swap(value, "tgt", bit) for bit in near]

    def combine(value, others):
        values = dict(zip(near, others))
        value = merge(value, values[1])
        return merge(value, merge(values[2], values[3])) if 2 in values else value

    for step in range(ITERS):
        if step == ITERS - 1:
            lse = side.hold(lse)
        others = side.start(step, lse, exchange)
        if step == ITERS - 1:
            others[0] = side.pieces(others[0], 1)
        lse = combine(lse, others)
        for bit in over_tgt[2:]:
            lse = merge(lse, swap(lse, "tgt", bit))
        if step == 0:
            lse, base, kernel, top = call(
                first_col_kernel,
                [by_col, by_row, (rows, cols), by_col],
                [by_row, column], [score, lse, row_aux], 0,
            )
        else:
            last = step == ITERS - 1
            outs = [by_col, by_row, by_row] if last else [by_col]
            scratch = [by_row, column] if last else [by_row, by_row, by_row, column]
            lse, *held = call(col_kernel, outs, scratch, [score, kernel, top, base, lse, row_aux], 0)
            if last:
                f, masked = held
        if step < ITERS - 1:
            lse = side.land(side.pieces(side.hold(lse), step))
            lse = lax.all_to_all(jnp.broadcast_to(lse, (n_src, *by_col)), "src", 0, 0, tiled=True)
            (lse,) = call(
                row_kernel,
                [by_row],
                [by_col, by_col, column, column],
                [score, kernel, top, base, lse, row_aux, col_aux], 0,
            )
    lse = side.finish(lse)
    both = jnp.concatenate([lse, masked], axis=0)
    both = lax.all_to_all(jnp.broadcast_to(both, (n_src, *both.shape)), "src", 0, 0, tiled=True)
    ancestors, f, g = call(
        functools.partial(last_kernel, pieces=side.done),
        [(dims, share), by_row, by_col],
        [by_col, (share // LANES, LANES), (share, LANES), (share, 2 * DEPTH)],
        [*side.slabs, *side.terms, both, col_aux, f, *side.tokens],
        18 * DEPTH * pairs, pairs, pin=False,
    )
    return (f.reshape(rows), g.reshape(cols), ancestors)


def solution(mesh):
    return jax.shard_map(
        shards,
        mesh=mesh,
        in_specs=(P(None, "src"), P(None, "tgt"), P("src", "tgt"), P(), P()),
        out_specs=(P("src"), P("tgt"), P(None, ("tgt", "src"))),
        check_vma=False,
    )
```

```python
import functools
import math

import jax
import jax.numpy as jnp
from jax import lax
from jax.experimental import pallas as pl
from jax.experimental.pallas import tpu as pltpu
from jax.sharding import PartitionSpec as P

ITERS = 4
EPS = 0.02
NEG = -1e30
LOG2E = math.log2(math.e)
SCALE = LOG2E / EPS
LANES = 128
DEPTH = 64
SHIFT = 40.0
ROW_FACTOR_MAX = 2.0**20
COL_FACTOR_MAX = 2.0**60
SUM_MIN = 2.0**-30
VMEM_LIMIT = 14 * 1024 * 1024

VMEM_SPEC = pl.BlockSpec(memory_space=pltpu.VMEM)
SMEM_SPEC = pl.BlockSpec(memory_space=pltpu.SMEM)


def pinned(x):
    return pltpu.with_memory_space_constraint(x, pltpu.VMEM)


def split(x):
    high = x.astype(jnp.bfloat16)
    rest = x - high.astype(jnp.float32)
    mid = rest.astype(jnp.bfloat16)
    low = (rest - mid.astype(jnp.float32)).astype(jnp.bfloat16)
    return high, mid, low


def put(ref, row):
    for k in range(row.shape[1] // LANES):
        ref[k : k + 1, :] = row[:, k * LANES : (k + 1) * LANES]


def positions(shape):
    return lax.broadcasted_iota(jnp.int32, shape, 0) * LANES + lax.broadcasted_iota(jnp.int32, shape, 1)


def to_sublanes(vector_ref, col_ref):
    for k in range(vector_ref.shape[0]):
        col_ref[k * LANES : (k + 1) * LANES, :] = jnp.broadcast_to(vector_ref[k : k + 1, :], (LANES, LANES)).T


def fold_lanes(peak_ref, total_ref, out_ref):
    for k in range(out_ref.shape[0]):
        here = slice(k * LANES, (k + 1) * LANES)
        peaks = peak_ref[here, :].T
        top = jnp.max(peaks, axis=0, keepdims=True)
        total = jnp.sum(total_ref[here, :].T * jnp.exp2(peaks - top), axis=0, keepdims=True)
        out_ref[k : k + 1, :] = top + jnp.log2(total)


def row_lse(score_ref, add_ref, peak_ref, total_ref, out_ref):
    rows, cols = score_ref.shape

    def block(i, _):
        here = pl.ds(pl.multiple_of(i * 8, 8), 8)
        z = []
        for k in range(cols // LANES):
            z.append(score_ref[here, k * LANES : (k + 1) * LANES] + add_ref[k : k + 1, :])
        peak = functools.reduce(jnp.maximum, z)
        peak_ref[here, :] = peak
        total_ref[here, :] = functools.reduce(jnp.add, [jnp.exp2(v - peak) for v in z])
        return 0

    lax.fori_loop(0, rows // 8, block, 0)
    fold_lanes(peak_ref, total_ref, out_ref)


def col_lse(score_ref, add_ref, out_ref, kernel_ref=None, top_ref=None):
    rows, cols = score_ref.shape
    group = 16
    tall = 4
    written_out = kernel_ref is not None

    for first in range(0, cols // LANES, group):
        lanes = [slice((first + k) * LANES, (first + k + 1) * LANES) for k in range(group)]

        def peaks(i, tops):
            for r in range(tall):
                here = pl.ds(pl.multiple_of((i * tall + r) * 8, 8), 8)
                add = add_ref[here, :]
                tops = tuple(jnp.maximum(t, score_ref[here, s] + add) for t, s in zip(tops, lanes))
            return tops

        start = (jnp.full((8, LANES), -jnp.inf, jnp.float32),) * group
        tops = lax.fori_loop(0, rows // (8 * tall), peaks, start, unroll=written_out)
        tops = [jnp.max(t, axis=0, keepdims=True) - SHIFT for t in tops]
        wide_tops = [jnp.broadcast_to(t, (8, LANES)) for t in tops]

        def totals(i, sums):
            for r in range(tall):
                here = pl.ds(pl.multiple_of((i * tall + r) * 8, 8), 8)
                add = add_ref[here, :]
                terms = [jnp.exp2(score_ref[here, s] + (add - t)) for t, s in zip(wide_tops, lanes)]
                if kernel_ref is not None:
                    for s, t in zip(lanes, terms):
                        kernel_ref[here, s] = t
                sums = tuple(u + t for u, t in zip(sums, terms))
            return sums

        start = (jnp.zeros((8, LANES), jnp.float32),) * group
        sums = lax.fori_loop(0, rows // (8 * tall), totals, start, unroll=written_out)
        for k, (t, u) in enumerate(zip(tops, sums)):
            spot = slice(first + k, first + k + 1)
            if top_ref is not None:
                top_ref[spot, :] = t
            out_ref[spot, :] = t + jnp.log2(jnp.sum(u, axis=0, keepdims=True))


def source_terms(x):
    high, mid, low = split(x * (2.0 * SCALE))
    return [high, high, mid, mid, high, low]


def target_terms(y):
    high, mid, low = split(y)
    return [high, mid, high, mid, low, high]


def pad_into(pad_ref, values):
    pad_ref[...] = jnp.zeros(pad_ref.shape, jnp.float32)
    pad_ref[0 : values.shape[0], :] = values


def live_sum(counts):
    total = counts[0]
    for i in range(1, counts.shape[0]):
        total = total + counts[i]
    return jnp.full((1, LANES), total, jnp.int32).astype(jnp.float32)


def wide(x, size):
    return jnp.concatenate([x] * (size // LANES), axis=1)


def first_kernel(
    src_hbm, tgt_hbm, count_src_hbm, count_tgt_hbm, pair,
    score_ref, lse_ref, row_aux, col_aux, own_ref, half_ref,
    src_ref, tgt_ref, count_src, count_tgt, sems,
    right_pad, left_pad, terms_ref, norm_ref, col_ref, peak_ref, total_ref,
):
    rows, cols = score_ref.shape
    dims = src_ref.shape[0]
    copies = [
        pltpu.make_async_copy(one, two, sems.at[i])
        for i, (one, two) in enumerate(
            [(count_src_hbm, count_src), (count_tgt_hbm, count_tgt), (src_hbm, src_ref), (tgt_hbm, tgt_ref)]
        )
    ]
    for copy in copies:
        copy.start()
    for ref in (right_pad, left_pad, own_ref):
        ref[...] = jnp.zeros(ref.shape, jnp.float32)
    n_half = -(-dims // 2)
    for copy in copies[:3]:
        copy.wait()
    n_rows = count_src[lax.axis_index("src")]
    n_cols = count_tgt[lax.axis_index("tgt")]
    listed = pair[0, 0] > 0
    row_live = positions(row_aux.shape[1:]) < n_rows
    col_live = positions(col_aux.shape[1:]) < n_cols
    row_aux[0] = row_live.astype(jnp.float32)
    row_aux[1] = jnp.where(row_live, -jnp.log2(live_sum(count_src)), 0.0)
    row_aux[2] = (row_live & listed).astype(jnp.float32)
    col_aux[0] = col_live.astype(jnp.float32)
    col_aux[1] = jnp.where(col_live, -jnp.log2(live_sum(count_tgt)), 0.0)
    left_pad[0:dims, :] = src_ref[...]
    left = left_pad[...]
    half = jnp.where(lax.axis_index("tgt") % 2 == 0, left[0:n_half], left[n_half : 2 * n_half])
    half_ref[...] = jnp.zeros(half_ref.shape, jnp.float32)
    for k in range(rows // LANES):
        half_ref[0, k * n_half : (k + 1) * n_half, :] = half[:, k * LANES : (k + 1) * LANES]
    put(norm_ref, -SCALE * jnp.sum(left * left, axis=0, keepdims=True))
    norm_ref[...] = jnp.where(row_live, norm_ref[...], NEG)
    to_sublanes(norm_ref, col_ref)
    terms_ref[...] = jnp.concatenate(source_terms(left.T), axis=1)
    copies[3].wait()
    size = 512

    def scores(c):
        here = slice(c * size, (c + 1) * size)
        right_pad[0:dims, :] = tgt_ref[:, here]
        right = right_pad[...]
        spot = lax.broadcasted_iota(jnp.int32, (1, size), 1) + c * size
        norm = -SCALE * jnp.sum(right * right, axis=0, keepdims=True)
        norm = jnp.where((spot < n_cols) & listed, norm, NEG)
        terms = jnp.concatenate(target_terms(right), axis=0)
        cross = jnp.dot(terms_ref[...], terms, preferred_element_type=jnp.float32)
        score = cross + (wide(col_ref[...], size) + norm)
        score_ref[:, here] = score
        return [score[:, k : k + LANES] for k in range(0, size, LANES)]

    peak_ref[...] = jnp.full(peak_ref.shape, 2.0 * NEG, jnp.float32)
    total_ref[...] = jnp.zeros(total_ref.shape, jnp.float32)

    for c in range(cols // size):
        z = scores(c)
        before = peak_ref[...]
        peak = functools.reduce(jnp.maximum, z, before)
        total_ref[...] = functools.reduce(
            jnp.add, [jnp.exp2(v - peak) for v in z], total_ref[...] * jnp.exp2(before - peak)
        )
        peak_ref[...] = peak
    share = own_ref.shape[1]
    own_ref[0:dims, :] = tgt_ref[:, pl.ds(pl.multiple_of(lax.axis_index("src") * share, share), share)]
    fold_lanes(peak_ref, total_ref, lse_ref)


def slab_kernel(own_ref, mine_ref, theirs_ref, *refs, first, n_half, prepare):
    if prepare:
        slab_ref, terms_out, token_ref, terms_ref, col_ref, right_pad, norm_ref = refs
        left = own_ref[...]
        put(norm_ref, -SCALE * jnp.sum(left * left, axis=0, keepdims=True))
        to_sublanes(norm_ref, col_ref)
        terms_ref[...] = jnp.concatenate(target_terms(left.T), axis=1)
    else:
        terms_ref, col_ref, slab_ref, terms_out, token_ref, right_pad = refs
    rows = right_pad.shape[1]
    even = lax.axis_index("tgt") % 2 == 0
    right_pad[...] = jnp.zeros(right_pad.shape, jnp.float32)
    for b in range(slab_ref.shape[1] // rows):
        mine, theirs = mine_ref[first + b], theirs_ref[first + b]
        upper = jnp.where(even, mine, theirs)
        lower = jnp.where(even, theirs, mine)
        for k in range(rows // LANES):
            here = slice(k * n_half, (k + 1) * n_half)
            right_pad[0:n_half, k * LANES : (k + 1) * LANES] = upper[here]
            right_pad[n_half : 2 * n_half, k * LANES : (k + 1) * LANES] = lower[here]
        right = right_pad[...]
        norm = -SCALE * jnp.sum(right * right, axis=0, keepdims=True)
        terms = jnp.concatenate(source_terms(right), axis=0)
        cross = jnp.dot(terms_ref[...], terms, preferred_element_type=jnp.float32)
        here = slice(b * rows, (b + 1) * rows)
        slab_ref[:, here] = cross + (wide(col_ref[...], rows) + norm)
        terms_out[here, :] = jnp.concatenate(split(right.T)[:2], axis=1)
    token_ref[...] = jnp.zeros(token_ref.shape, jnp.float32)


def row_sums(kernel_ref, factor_ref, total_ref, out_ref):
    rows, cols = kernel_ref.shape
    tall = 8

    def block(i, _):
        spots = [pl.ds(pl.multiple_of((i * tall + k) * 8, 8), 8) for k in range(tall)]
        sums = [jnp.zeros((8, LANES), jnp.float32)] * tall
        for t in range(cols // LANES):
            lanes = slice(t * LANES, (t + 1) * LANES)
            factor = jnp.broadcast_to(factor_ref[t : t + 1, :], (8, LANES))
            sums = [u + kernel_ref[s, lanes] * factor for u, s in zip(sums, spots)]
        for s, u in zip(spots, sums):
            total_ref[s, :] = u
        return 0

    lax.fori_loop(0, rows // (8 * tall), block, 0, unroll=True)
    for k in range(out_ref.shape[0]):
        out_ref[k : k + 1, :] = jnp.sum(total_ref[k * LANES : (k + 1) * LANES, :].T, axis=0, keepdims=True)


def col_sums(kernel_ref, factor_ref, out_ref):
    rows, cols = kernel_ref.shape
    lanes = [slice(start, start + LANES) for start in range(0, cols, LANES)]
    tall = 4

    def block(i, sums):
        for r in range(tall):
            here = pl.ds(pl.multiple_of((i * tall + r) * 8, 8), 8)
            factor = factor_ref[here, :]
            sums = tuple(u + kernel_ref[here, s] * factor for u, s in zip(sums, lanes))
        return sums

    start = (jnp.zeros((8, LANES), jnp.float32),) * len(lanes)
    sums = lax.fori_loop(0, rows // (8 * tall), block, start, unroll=True)
    for k, u in enumerate(sums):
        out_ref[k : k + 1, :] = jnp.sum(u, axis=0, keepdims=True)


def out_of_range(total, needed, factor, most):
    small = jnp.where(needed & jnp.logical_not(total >= SUM_MIN), 1.0, 0.0)
    large = jnp.where(factor <= most, 0.0, 1.0)
    return jnp.max(jnp.maximum(jnp.max(small, axis=0, keepdims=True), jnp.max(large, axis=0, keepdims=True))) > 0.5


def set_f(lse_ref, aux_ref, f_ref, masked_ref):
    f = aux_ref[1] - lse_ref[...] * aux_ref[0]
    f_ref[...] = f
    masked_ref[...] = jnp.where(aux_ref[2] > 0, f, NEG)


def first_col_kernel(score_ref, lse_ref, aux_ref, out_ref, f_ref, kernel_ref, top_ref, masked_ref, col_ref):
    set_f(lse_ref, aux_ref, f_ref, masked_ref)
    to_sublanes(f_ref, col_ref)
    col_lse(score_ref, col_ref, out_ref, kernel_ref, top_ref)


def col_kernel(
    score_ref, kernel_ref, top_ref, base_ref, lse_ref, aux_ref, out_ref, f_ref, masked_ref, factor_ref, col_ref
):
    set_f(lse_ref, aux_ref, f_ref, masked_ref)
    factor_ref[...] = jnp.exp2(f_ref[...] - base_ref[...])
    to_sublanes(factor_ref, col_ref)
    col_sums(kernel_ref, col_ref, out_ref)
    total = out_ref[...]
    top = top_ref[...]
    redo = out_of_range(total, top > 0.5 * NEG, factor_ref[...], ROW_FACTOR_MAX)
    out_ref[...] = jnp.where(total > 0, top + jnp.log2(total), NEG)

    @pl.when(redo)
    def _():
        to_sublanes(f_ref, col_ref)
        col_lse(score_ref, col_ref, out_ref)


def merged(parts):
    peak = jnp.max(parts, axis=0)
    return peak + jnp.log2(jnp.sum(jnp.exp2(parts - peak[None]), axis=0))


def row_kernel(
    score_ref, kernel_ref, top_ref, base_ref, parts_ref, row_aux, col_aux, out_ref,
    g_ref, factor_ref, peak_ref, total_ref,
):
    lse = merged(parts_ref[...])
    g_ref[...] = col_aux[1] - lse * col_aux[0]
    factor_ref[...] = jnp.where(col_aux[0] > 0, jnp.exp2(top_ref[...] - lse + 2.0 * SHIFT), 0.0)
    row_sums(kernel_ref, factor_ref, total_ref, out_ref)
    total = out_ref[...]
    redo = out_of_range(total, row_aux[2] > 0, factor_ref[...], COL_FACTOR_MAX)
    log_b = col_aux[1, 0:1, 0:1]
    out_ref[...] = jnp.where(total > 0, jnp.log2(total) - 2.0 * SHIFT - base_ref[...] + log_b, NEG)

    @pl.when(redo)
    def _():
        row_lse(score_ref, g_ref, peak_ref, total_ref, out_ref)


def last_kernel(*refs, pieces):
    slabs, refs = refs[: len(pieces)], refs[len(pieces) :]
    terms, refs = refs[: len(pieces)], refs[len(pieces) :]
    parts_ref, aux_ref, f_ref, *_, out_ref, f_out, g_out, lse_ref, own_ref, col_ref, sum_ref = refs
    n_col = aux_ref.shape[1]
    lse = merged(parts_ref[:, 0:n_col, :])
    lse_ref[...] = lse
    f_out[...] = f_ref[...] * (1.0 / SCALE)
    g_out[...] = (aux_ref[1] - lse * aux_ref[0]) * (1.0 / SCALE)
    me = lax.axis_index("src")
    n_own = own_ref.shape[0]
    for k in range(n_own):
        spot = pl.ds(me * n_own + k, 1)
        own_ref[k : k + 1, :] = jnp.where(aux_ref[0, spot, :] > 0, -lse_ref[spot, :], NEG)
    to_sublanes(own_ref, col_ref)
    for i, (slab_ref, terms_ref, offsets) in enumerate(zip(slabs, terms, pieces)):
        high, mid = [], []
        start = 0
        for offset in offsets:
            for row in range(n_col, parts_ref.shape[1]):
                add = col_ref[...] + parts_ref[me ^ offset, row : row + 1, :]
                term = split(jnp.exp2(slab_ref[:, start : start + LANES] + add))
                high.append(term[0])
                mid.append(term[1])
                start += LANES
        sums = jnp.dot(
            jnp.concatenate(high + mid, axis=1), jnp.concatenate([terms_ref[...]] * 2, axis=0),
            preferred_element_type=jnp.float32,
        )
        if i == 0:
            sum_ref[...] = sums
        else:
            sum_ref[...] += sums
    sums = sum_ref[...].T
    out_ref[...] = (sums[0:DEPTH] + sums[DEPTH :])[0 : out_ref.shape[0]]


def merge(one, two):
    top = jnp.maximum(one, two)
    return top + jnp.log2(1.0 + jnp.exp2(jnp.minimum(one, two) - top))


def swap(value, axis, step):
    return lax.ppermute(value, axis, [(i, i ^ step) for i in range(lax.axis_size(axis))])


def doubling(size):
    return [1 << k for k in range(size.bit_length() - 1)]


def buffer(space, shape):
    return space(*shape) if isinstance(shape[0], tuple) else space(shape, jnp.float32)


def call(kernel, outs, scratch, ins, flops, expos=0, pin=True):
    return pl.pallas_call(
        kernel,
        out_shape=[buffer(pltpu.VMEM if pin else jax.ShapeDtypeStruct, shape) for shape in outs],
        in_specs=[VMEM_SPEC] * len(ins),
        out_specs=[VMEM_SPEC] * len(outs),
        scratch_shapes=[buffer(pltpu.VMEM, shape) for shape in scratch],
        compiler_params=pltpu.CompilerParams(vmem_limit_bytes=VMEM_LIMIT),
        cost_estimate=pl.CostEstimate(flops=flops, bytes_accessed=0, transcendentals=expos),
    )(*[pinned(x) for x in ins])


def tie(*values):
    return lax.optimization_barrier(values)


class Beside:
    def __init__(self, half, own, bits, rows, n_half):
        self.own = own
        self.rows = rows
        self.n_half = n_half
        self.blocks = {0: half}
        self.coming = {}
        if len(bits) >= 3:
            z, w, x = bits[:3]
            self.fetches = [[(0, w), (0, z), (0, x)], [(z, x), (w, z)], [(w, x), (w ^ z, x)], []]
            self.groups = [[], [0, z, w, x], [z ^ x, w ^ z], [w ^ x, w ^ z ^ x]]
            self.bits = bits[3:]
        else:
            self.fetches = [[]] * ITERS
            self.groups = [[]] * (ITERS - 1) + [[0]]
            self.bits = bits
        self.ready = None
        self.mine = []
        self.theirs = []
        self.offsets = []
        self.todo = []
        self.tokens = []
        self.slabs = []
        self.terms = []
        self.done = []

    def start(self, step, value, exchange):
        used = sorted({offset for offset, _ in self.fetches[step]} | set(self.groups[step]))
        if step and used:
            value, *held = tie(value, *[self.blocks[offset] for offset in used])
            self.blocks.update(zip(used, held))
        others = exchange(value)
        for offset, bit in self.fetches[step]:
            self.coming[offset ^ bit] = swap(self.blocks[offset], "src", bit)
        if self.groups[step]:
            held = [self.blocks[offset] for offset in self.groups[step]]
            self.add(held[0] if len(held) == 1 else jnp.concatenate(held, axis=0), self.groups[step])
        return others

    def add(self, mine, offsets):
        group = len(self.mine)
        self.mine.append(mine)
        self.theirs.append(swap(mine, "tgt", 1))
        self.offsets.append(offsets)
        self.todo += [(group, first, min(2, len(offsets))) for first in range(0, len(offsets), 2)]

    def land(self, value):
        if self.coming:
            value, *held = tie(value, *self.coming.values())
            self.blocks.update(zip(self.coming, held))
            self.coming = {}
        return value

    def piece(self):
        group, first, size = self.todo.pop(0)
        share = self.own.shape[1]
        rows = self.rows
        prepare = self.ready is None
        slab, terms, token, *ready = call(
            functools.partial(slab_kernel, first=first, n_half=self.n_half, prepare=prepare),
            [(share, size * rows), ((size * rows, 2 * DEPTH), jnp.bfloat16), (8, LANES)]
            + [((share, 6 * DEPTH), jnp.bfloat16), (share, LANES)] * prepare,
            [(DEPTH, rows)] + [(share // LANES, LANES)] * prepare,
            [self.own, self.mine[group], self.theirs[group], *(self.ready or [])],
            12 * DEPTH * share * size * rows,
        )
        self.ready = ready or self.ready
        self.terms.append(terms)
        self.slabs.append(slab)
        self.done.append(self.offsets[group][first : first + size])
        return token

    def hold(self, value):
        value, self.own = tie(value, self.own)
        return value

    def pieces(self, value, most):
        for _ in range(min(most, len(self.todo))):
            value, token = tie(value, self.piece())
            self.tokens.append(token)
        return value

    def finish(self, value):
        for bit in self.bits:
            for mine, offsets in list(zip(self.mine, self.offsets)):
                self.add(swap(mine, "src", bit), [offset ^ bit for offset in offsets])
        return self.pieces(self.hold(value), len(self.todo))


def shards(sources, targets, pair_active, count_src, count_tgt):
    dims, rows = sources.shape
    cols = targets.shape[1]
    n_src = lax.axis_size("src")
    share = cols // n_src
    column = (rows, LANES)
    by_row = (rows // LANES, LANES)
    by_col = (cols // LANES, LANES)
    pairs = rows * cols
    hbm = [pltpu.with_memory_space_constraint(x, pltpu.HBM) for x in (sources, targets, count_src, count_tgt)]
    n_half = -(-dims // 2)
    packed = -(-n_half * by_row[0] // 8) * 8
    outs = [(rows, cols), by_row, (3, *by_row), (3, *by_col), (DEPTH, share), (1, packed, LANES)]
    score, lse, row_aux, col_aux, own, half = pl.pallas_call(
        first_kernel,
        out_shape=[pltpu.VMEM(shape, jnp.float32) for shape in outs],
        in_specs=[pl.BlockSpec(memory_space=pltpu.HBM)] * 4 + [SMEM_SPEC],
        out_specs=[VMEM_SPEC] * len(outs),
        scratch_shapes=[
            pltpu.VMEM((dims, rows), jnp.float32),
            pltpu.VMEM((dims, cols), jnp.float32),
            pltpu.SMEM(count_src.shape, jnp.int32),
            pltpu.SMEM(count_tgt.shape, jnp.int32),
            pltpu.SemaphoreType.DMA((4,)),
            pltpu.VMEM((DEPTH, 512), jnp.float32),
            pltpu.VMEM((DEPTH, rows), jnp.float32),
            pltpu.VMEM((rows, 6 * DEPTH), jnp.bfloat16),
            pltpu.VMEM(by_row, jnp.float32),
            pltpu.VMEM(column, jnp.float32),
            pltpu.VMEM(column, jnp.float32),
            pltpu.VMEM(column, jnp.float32),
        ],
        compiler_params=pltpu.CompilerParams(vmem_limit_bytes=VMEM_LIMIT),
        cost_estimate=pl.CostEstimate(flops=12 * DEPTH * pairs, bytes_accessed=0, transcendentals=pairs),
    )(*hbm, pair_active)
    over_tgt = doubling(lax.axis_size("tgt"))
    over_src = doubling(n_src)
    over_src = over_src[1:] + over_src[:1]
    side = Beside(half, own, over_src, rows, n_half)
    near = [bit for bit in (2, 3, 1) if bit < lax.axis_size("tgt")]

    def exchange(value):
        return [swap(value, "tgt", bit) for bit in near]

    def combine(value, others):
        values = dict(zip(near, others))
        value = merge(value, values[1])
        return merge(value, merge(values[2], values[3])) if 2 in values else value

    for step in range(ITERS):
        if step == ITERS - 1:
            lse = side.hold(lse)
        others = side.start(step, lse, exchange)
        if step == ITERS - 1:
            others[0] = side.pieces(others[0], 1)
        lse = combine(lse, others)
        for bit in over_tgt[2:]:
            lse = merge(lse, swap(lse, "tgt", bit))
        if step == 0:
            lse, base, kernel, top = call(
                first_col_kernel,
                [by_col, by_row, (rows, cols), by_col],
                [by_row, column], [score, lse, row_aux], 0,
            )
        else:
            last = step == ITERS - 1
            outs = [by_col, by_row, by_row] if last else [by_col]
            scratch = [by_row, column] if last else [by_row, by_row, by_row, column]
            lse, *held = call(col_kernel, outs, scratch, [score, kernel, top, base, lse, row_aux], 0)
            if last:
                f, masked = held
        if step < ITERS - 1:
            lse = side.land(side.pieces(side.hold(lse), step))
            lse = lax.all_to_all(jnp.broadcast_to(lse, (n_src, *by_col)), "src", 0, 0, tiled=True)
            (lse,) = call(
                row_kernel,
                [by_row],
                [by_col, by_col, column, column],
                [score, kernel, top, base, lse, row_aux, col_aux], 0,
            )
    lse = side.finish(lse)
    both = jnp.concatenate([lse, masked], axis=0)
    both = lax.all_to_all(jnp.broadcast_to(both, (n_src, *both.shape)), "src", 0, 0, tiled=True)
    ancestors, f, g = call(
        functools.partial(last_kernel, pieces=side.done),
        [(dims, share), by_row, by_col],
        [by_col, (share // LANES, LANES), (share, LANES), (share, 2 * DEPTH)],
        [*side.slabs, *side.terms, both, col_aux, f, *side.tokens],
        18 * DEPTH * pairs, pairs, pin=False,
    )
    return (f.reshape(rows), g.reshape(cols), ancestors)


def solution(mesh):
    return jax.shard_map(
        shards,
        mesh=mesh,
        in_specs=(P(None, "src"), P(None, "tgt"), P("src", "tgt"), P(), P()),
        out_specs=(P("src"), P("tgt"), P(None, ("tgt", "src"))),
        check_vma=False,
    )
```

```python
import functools
import math

import jax
import jax.numpy as jnp
from jax import lax
from jax.experimental import pallas as pl
from jax.experimental.pallas import tpu as pltpu
from jax.sharding import PartitionSpec as P

ITERS = 4
EPS = 0.02
NEG = -1e30
LOG2E = math.log2(math.e)
SCALE = LOG2E / EPS
LANES = 128
DEPTH = 64
SHIFT = 40.0
ROW_FACTOR_MAX = 2.0**20
COL_FACTOR_MAX = 2.0**60
SUM_MIN = 2.0**-30
VMEM_LIMIT = 14 * 1024 * 1024

VMEM_SPEC = pl.BlockSpec(memory_space=pltpu.VMEM)
SMEM_SPEC = pl.BlockSpec(memory_space=pltpu.SMEM)


def pinned(x):
    return pltpu.with_memory_space_constraint(x, pltpu.VMEM)


def split(x):
    high = x.astype(jnp.bfloat16)
    rest = x - high.astype(jnp.float32)
    mid = rest.astype(jnp.bfloat16)
    low = (rest - mid.astype(jnp.float32)).astype(jnp.bfloat16)
    return high, mid, low


def put(ref, row):
    for k in range(row.shape[1] // LANES):
        ref[k : k + 1, :] = row[:, k * LANES : (k + 1) * LANES]


def positions(shape):
    return lax.broadcasted_iota(jnp.int32, shape, 0) * LANES + lax.broadcasted_iota(jnp.int32, shape, 1)


def to_sublanes(vector_ref, col_ref):
    for k in range(vector_ref.shape[0]):
        col_ref[k * LANES : (k + 1) * LANES, :] = jnp.broadcast_to(vector_ref[k : k + 1, :], (LANES, LANES)).T


def fold_lanes(peak_ref, total_ref, out_ref):
    for k in range(out_ref.shape[0]):
        here = slice(k * LANES, (k + 1) * LANES)
        peaks = peak_ref[here, :].T
        top = jnp.max(peaks, axis=0, keepdims=True)
        total = jnp.sum(total_ref[here, :].T * jnp.exp2(peaks - top), axis=0, keepdims=True)
        out_ref[k : k + 1, :] = top + jnp.log2(total)


def row_lse(score_ref, add_ref, peak_ref, total_ref, out_ref):
    rows, cols = score_ref.shape

    def block(i, _):
        here = pl.ds(pl.multiple_of(i * 8, 8), 8)
        z = []
        for k in range(cols // LANES):
            z.append(score_ref[here, k * LANES : (k + 1) * LANES] + add_ref[k : k + 1, :])
        peak = functools.reduce(jnp.maximum, z)
        peak_ref[here, :] = peak
        total_ref[here, :] = functools.reduce(jnp.add, [jnp.exp2(v - peak) for v in z])
        return 0

    lax.fori_loop(0, rows // 8, block, 0)
    fold_lanes(peak_ref, total_ref, out_ref)


def col_lse(score_ref, add_ref, out_ref, kernel_ref=None, top_ref=None):
    rows, cols = score_ref.shape
    group = 16
    tall = 4
    written_out = kernel_ref is not None

    for first in range(0, cols // LANES, group):
        lanes = [slice((first + k) * LANES, (first + k + 1) * LANES) for k in range(group)]

        def peaks(i, tops):
            for r in range(tall):
                here = pl.ds(pl.multiple_of((i * tall + r) * 8, 8), 8)
                add = add_ref[here, :]
                tops = tuple(jnp.maximum(t, score_ref[here, s] + add) for t, s in zip(tops, lanes))
            return tops

        start = (jnp.full((8, LANES), -jnp.inf, jnp.float32),) * group
        tops = lax.fori_loop(0, rows // (8 * tall), peaks, start, unroll=written_out)
        tops = [jnp.max(t, axis=0, keepdims=True) - SHIFT for t in tops]
        wide_tops = [jnp.broadcast_to(t, (8, LANES)) for t in tops]

        def totals(i, sums):
            for r in range(tall):
                here = pl.ds(pl.multiple_of((i * tall + r) * 8, 8), 8)
                add = add_ref[here, :]
                terms = [jnp.exp2(score_ref[here, s] + (add - t)) for t, s in zip(wide_tops, lanes)]
                if kernel_ref is not None:
                    for s, t in zip(lanes, terms):
                        kernel_ref[here, s] = t
                sums = tuple(u + t for u, t in zip(sums, terms))
            return sums

        start = (jnp.zeros((8, LANES), jnp.float32),) * group
        sums = lax.fori_loop(0, rows // (8 * tall), totals, start, unroll=written_out)
        for k, (t, u) in enumerate(zip(tops, sums)):
            spot = slice(first + k, first + k + 1)
            if top_ref is not None:
                top_ref[spot, :] = t
            out_ref[spot, :] = t + jnp.log2(jnp.sum(u, axis=0, keepdims=True))


def source_terms(x):
    high, mid, low = split(x * (2.0 * SCALE))
    return [high, high, mid, mid, high, low]


def target_terms(y):
    high, mid, low = split(y)
    return [high, mid, high, mid, low, high]


def pad_into(pad_ref, values):
    pad_ref[...] = jnp.zeros(pad_ref.shape, jnp.float32)
    pad_ref[0 : values.shape[0], :] = values


def live_sum(counts):
    total = counts[0]
    for i in range(1, counts.shape[0]):
        total = total + counts[i]
    return jnp.full((1, LANES), total, jnp.int32).astype(jnp.float32)


def wide(x, size):
    return jnp.concatenate([x] * (size // LANES), axis=1)


def first_kernel(
    src_hbm, tgt_hbm, count_src_hbm, count_tgt_hbm, pair,
    score_ref, lse_ref, row_aux, col_aux, own_ref, half_ref,
    src_ref, tgt_ref, count_src, count_tgt, sems,
    right_pad, left_pad, terms_ref, norm_ref, col_ref, peak_ref, total_ref,
):
    rows, cols = score_ref.shape
    dims = src_ref.shape[0]
    copies = [
        pltpu.make_async_copy(one, two, sems.at[i])
        for i, (one, two) in enumerate(
            [(count_src_hbm, count_src), (count_tgt_hbm, count_tgt), (src_hbm, src_ref), (tgt_hbm, tgt_ref)]
        )
    ]
    for copy in copies:
        copy.start()
    for ref in (right_pad, left_pad, own_ref):
        ref[...] = jnp.zeros(ref.shape, jnp.float32)
    n_half = -(-dims // 2)
    for copy in copies[:3]:
        copy.wait()
    n_rows = count_src[lax.axis_index("src")]
    n_cols = count_tgt[lax.axis_index("tgt")]
    listed = pair[0, 0] > 0
    row_live = positions(row_aux.shape[1:]) < n_rows
    col_live = positions(col_aux.shape[1:]) < n_cols
    row_aux[0] = row_live.astype(jnp.float32)
    row_aux[1] = jnp.where(row_live, -jnp.log2(live_sum(count_src)), 0.0)
    row_aux[2] = (row_live & listed).astype(jnp.float32)
    col_aux[0] = col_live.astype(jnp.float32)
    col_aux[1] = jnp.where(col_live, -jnp.log2(live_sum(count_tgt)), 0.0)
    left_pad[0:dims, :] = src_ref[...]
    left = left_pad[...]
    half = jnp.where(lax.axis_index("tgt") % 2 == 0, left[0:n_half], left[n_half : 2 * n_half])
    half_ref[...] = jnp.zeros(half_ref.shape, jnp.float32)
    for k in range(rows // LANES):
        half_ref[0, k * n_half : (k + 1) * n_half, :] = half[:, k * LANES : (k + 1) * LANES]
    put(norm_ref, -SCALE * jnp.sum(left * left, axis=0, keepdims=True))
    norm_ref[...] = jnp.where(row_live, norm_ref[...], NEG)
    to_sublanes(norm_ref, col_ref)
    terms_ref[...] = jnp.concatenate(source_terms(left.T), axis=1)
    copies[3].wait()
    size = 512

    def scores(c):
        here = slice(c * size, (c + 1) * size)
        right_pad[0:dims, :] = tgt_ref[:, here]
        right = right_pad[...]
        spot = lax.broadcasted_iota(jnp.int32, (1, size), 1) + c * size
        norm = -SCALE * jnp.sum(right * right, axis=0, keepdims=True)
        norm = jnp.where((spot < n_cols) & listed, norm, NEG)
        terms = jnp.concatenate(target_terms(right), axis=0)
        cross = jnp.dot(terms_ref[...], terms, preferred_element_type=jnp.float32)
        score = cross + (wide(col_ref[...], size) + norm)
        score_ref[:, here] = score
        return [score[:, k : k + LANES] for k in range(0, size, LANES)]

    peak_ref[...] = jnp.full(peak_ref.shape, 2.0 * NEG, jnp.float32)
    total_ref[...] = jnp.zeros(total_ref.shape, jnp.float32)

    for c in range(cols // size):
        z = scores(c)
        before = peak_ref[...]
        peak = functools.reduce(jnp.maximum, z, before)
        total_ref[...] = functools.reduce(
            jnp.add, [jnp.exp2(v - peak) for v in z], total_ref[...] * jnp.exp2(before - peak)
        )
        peak_ref[...] = peak
    share = own_ref.shape[1]
    own_ref[0:dims, :] = tgt_ref[:, pl.ds(pl.multiple_of(lax.axis_index("src") * share, share), share)]
    fold_lanes(peak_ref, total_ref, lse_ref)


def slab_kernel(own_ref, mine_ref, theirs_ref, *refs, first, n_half, prepare):
    if prepare:
        slab_ref, terms_out, token_ref, terms_ref, col_ref, right_pad, norm_ref = refs
        left = own_ref[...]
        put(norm_ref, -SCALE * jnp.sum(left * left, axis=0, keepdims=True))
        to_sublanes(norm_ref, col_ref)
        terms_ref[...] = jnp.concatenate(target_terms(left.T), axis=1)
    else:
        terms_ref, col_ref, slab_ref, terms_out, token_ref, right_pad = refs
    rows = right_pad.shape[1]
    even = lax.axis_index("tgt") % 2 == 0
    right_pad[...] = jnp.zeros(right_pad.shape, jnp.float32)
    for b in range(slab_ref.shape[1] // rows):
        mine, theirs = mine_ref[first + b], theirs_ref[first + b]
        upper = jnp.where(even, mine, theirs)
        lower = jnp.where(even, theirs, mine)
        for k in range(rows // LANES):
            here = slice(k * n_half, (k + 1) * n_half)
            right_pad[0:n_half, k * LANES : (k + 1) * LANES] = upper[here]
            right_pad[n_half : 2 * n_half, k * LANES : (k + 1) * LANES] = lower[here]
        right = right_pad[...]
        norm = -SCALE * jnp.sum(right * right, axis=0, keepdims=True)
        terms = jnp.concatenate(source_terms(right), axis=0)
        cross = jnp.dot(terms_ref[...], terms, preferred_element_type=jnp.float32)
        here = slice(b * rows, (b + 1) * rows)
        slab_ref[:, here] = cross + (wide(col_ref[...], rows) + norm)
        terms_out[here, :] = jnp.concatenate(split(right.T)[:2], axis=1)
    token_ref[...] = jnp.zeros(token_ref.shape, jnp.float32)


def row_sums(kernel_ref, factor_ref, total_ref, out_ref):
    rows, cols = kernel_ref.shape
    tall = 8

    def block(i, _):
        spots = [pl.ds(pl.multiple_of((i * tall + k) * 8, 8), 8) for k in range(tall)]
        sums = [jnp.zeros((8, LANES), jnp.float32)] * tall
        for t in range(cols // LANES):
            lanes = slice(t * LANES, (t + 1) * LANES)
            factor = jnp.broadcast_to(factor_ref[t : t + 1, :], (8, LANES))
            sums = [u + kernel_ref[s, lanes] * factor for u, s in zip(sums, spots)]
        for s, u in zip(spots, sums):
            total_ref[s, :] = u
        return 0

    lax.fori_loop(0, rows // (8 * tall), block, 0, unroll=True)
    for k in range(out_ref.shape[0]):
        out_ref[k : k + 1, :] = jnp.sum(total_ref[k * LANES : (k + 1) * LANES, :].T, axis=0, keepdims=True)


def col_sums(kernel_ref, factor_ref, out_ref):
    rows, cols = kernel_ref.shape
    lanes = [slice(start, start + LANES) for start in range(0, cols, LANES)]
    tall = 4

    def block(i, sums):
        for r in range(tall):
            here = pl.ds(pl.multiple_of((i * tall + r) * 8, 8), 8)
            factor = factor_ref[here, :]
            sums = tuple(u + kernel_ref[here, s] * factor for u, s in zip(sums, lanes))
        return sums

    start = (jnp.zeros((8, LANES), jnp.float32),) * len(lanes)
    sums = lax.fori_loop(0, rows // (8 * tall), block, start, unroll=True)
    for k, u in enumerate(sums):
        out_ref[k : k + 1, :] = jnp.sum(u, axis=0, keepdims=True)


def out_of_range(total, needed, factor, most):
    small = jnp.where(needed & jnp.logical_not(total >= SUM_MIN), 1.0, 0.0)
    large = jnp.where(factor <= most, 0.0, 1.0)
    return jnp.max(jnp.maximum(jnp.max(small, axis=0, keepdims=True), jnp.max(large, axis=0, keepdims=True))) > 0.5


def set_f(lse_ref, aux_ref, f_ref, masked_ref):
    f = aux_ref[1] - lse_ref[...] * aux_ref[0]
    f_ref[...] = f
    masked_ref[...] = jnp.where(aux_ref[2] > 0, f, NEG)


def spread(lse, send_ref, masked=None):
    n_col = lse.shape[0]
    for k in range(send_ref.shape[0]):
        send_ref[k, 0:n_col, :] = lse
        if masked is not None:
            send_ref[k, n_col:, :] = masked


def first_col_kernel(
    score_ref, lse_ref, aux_ref, send_ref, f_ref, kernel_ref, top_ref, out_ref, masked_ref, col_ref
):
    set_f(lse_ref, aux_ref, f_ref, masked_ref)
    to_sublanes(f_ref, col_ref)
    col_lse(score_ref, col_ref, out_ref, kernel_ref, top_ref)
    spread(out_ref[...], send_ref)


def col_kernel(
    score_ref, kernel_ref, top_ref, base_ref, lse_ref, aux_ref, send_ref, f_ref, out_ref, masked_ref, factor_ref,
    col_ref, *, last,
):
    set_f(lse_ref, aux_ref, f_ref, masked_ref)
    factor_ref[...] = jnp.exp2(f_ref[...] - base_ref[...])
    to_sublanes(factor_ref, col_ref)
    col_sums(kernel_ref, col_ref, out_ref)
    total = out_ref[...]
    top = top_ref[...]
    redo = out_of_range(total, top > 0.5 * NEG, factor_ref[...], ROW_FACTOR_MAX)
    masked = masked_ref[...] if last else None
    spread(jnp.where(total > 0, top + jnp.log2(total), NEG), send_ref, masked)

    @pl.when(redo)
    def _():
        to_sublanes(f_ref, col_ref)
        col_lse(score_ref, col_ref, out_ref)
        spread(out_ref[...], send_ref, masked)


def merged(parts):
    peak = jnp.max(parts, axis=0)
    return peak + jnp.log2(jnp.sum(jnp.exp2(parts - peak[None]), axis=0))


def row_kernel(
    score_ref, kernel_ref, top_ref, base_ref, parts_ref, row_aux, col_aux, out_ref,
    g_ref, factor_ref, peak_ref, total_ref,
):
    lse = merged(parts_ref[...])
    g_ref[...] = col_aux[1] - lse * col_aux[0]
    factor_ref[...] = jnp.where(col_aux[0] > 0, jnp.exp2(top_ref[...] - lse + 2.0 * SHIFT), 0.0)
    row_sums(kernel_ref, factor_ref, total_ref, out_ref)
    total = out_ref[...]
    redo = out_of_range(total, row_aux[2] > 0, factor_ref[...], COL_FACTOR_MAX)
    log_b = col_aux[1, 0:1, 0:1]
    out_ref[...] = jnp.where(total > 0, jnp.log2(total) - 2.0 * SHIFT - base_ref[...] + log_b, NEG)

    @pl.when(redo)
    def _():
        row_lse(score_ref, g_ref, peak_ref, total_ref, out_ref)


def last_kernel(*refs, pieces):
    slabs, refs = refs[: len(pieces)], refs[len(pieces) :]
    terms, refs = refs[: len(pieces)], refs[len(pieces) :]
    parts_ref, aux_ref, f_ref, *_, out_ref, f_out, g_out, lse_ref, own_ref, col_ref, sum_ref = refs
    n_col = aux_ref.shape[1]
    lse = merged(parts_ref[:, 0:n_col, :])
    lse_ref[...] = lse
    f_out[...] = f_ref[...] * (1.0 / SCALE)
    g_out[...] = (aux_ref[1] - lse * aux_ref[0]) * (1.0 / SCALE)
    me = lax.axis_index("src")
    n_own = own_ref.shape[0]
    for k in range(n_own):
        spot = pl.ds(me * n_own + k, 1)
        own_ref[k : k + 1, :] = jnp.where(aux_ref[0, spot, :] > 0, -lse_ref[spot, :], NEG)
    to_sublanes(own_ref, col_ref)
    for i, (slab_ref, terms_ref, offsets) in enumerate(zip(slabs, terms, pieces)):
        high, mid = [], []
        start = 0
        for offset in offsets:
            for row in range(n_col, parts_ref.shape[1]):
                add = col_ref[...] + parts_ref[me ^ offset, row : row + 1, :]
                term = split(jnp.exp2(slab_ref[:, start : start + LANES] + add))
                high.append(term[0])
                mid.append(term[1])
                start += LANES
        sums = jnp.dot(
            jnp.concatenate(high + mid, axis=1), jnp.concatenate([terms_ref[...]] * 2, axis=0),
            preferred_element_type=jnp.float32,
        )
        if i == 0:
            sum_ref[...] = sums
        else:
            sum_ref[...] += sums
    sums = sum_ref[...].T
    out_ref[...] = (sums[0:DEPTH] + sums[DEPTH :])[0 : out_ref.shape[0]]


def merge(one, two):
    top = jnp.maximum(one, two)
    return top + jnp.log2(1.0 + jnp.exp2(jnp.minimum(one, two) - top))


def swap(value, axis, step):
    return lax.ppermute(value, axis, [(i, i ^ step) for i in range(lax.axis_size(axis))])


def doubling(size):
    return [1 << k for k in range(size.bit_length() - 1)]


def buffer(space, shape):
    return space(*shape) if isinstance(shape[0], tuple) else space(shape, jnp.float32)


def call(kernel, outs, scratch, ins, flops, expos=0, pin=True):
    return pl.pallas_call(
        kernel,
        out_shape=[buffer(pltpu.VMEM if pin else jax.ShapeDtypeStruct, shape) for shape in outs],
        in_specs=[VMEM_SPEC] * len(ins),
        out_specs=[VMEM_SPEC] * len(outs),
        scratch_shapes=[buffer(pltpu.VMEM, shape) for shape in scratch],
        compiler_params=pltpu.CompilerParams(vmem_limit_bytes=VMEM_LIMIT),
        cost_estimate=pl.CostEstimate(flops=flops, bytes_accessed=0, transcendentals=expos),
    )(*[pinned(x) for x in ins])


def tie(*values):
    return lax.optimization_barrier(values)


class Beside:
    def __init__(self, half, own, bits, rows, n_half):
        self.own = own
        self.rows = rows
        self.n_half = n_half
        self.blocks = {0: half}
        self.coming = {}
        if len(bits) >= 3:
            z, w, x = bits[:3]
            self.fetches = [[(0, w), (0, z), (0, x)], [(z, x), (w, z)], [(w, x), (w ^ z, x)], []]
            self.groups = [[], [0, z, w, x], [z ^ x, w ^ z], [w ^ x, w ^ z ^ x]]
            self.bits = bits[3:]
        else:
            self.fetches = [[]] * ITERS
            self.groups = [[]] * (ITERS - 1) + [[0]]
            self.bits = bits
        self.ready = None
        self.mine = []
        self.theirs = []
        self.offsets = []
        self.todo = []
        self.tokens = []
        self.slabs = []
        self.terms = []
        self.done = []

    def start(self, step, value, exchange):
        used = sorted({offset for offset, _ in self.fetches[step]} | set(self.groups[step]))
        if step and used:
            value, *held = tie(value, *[self.blocks[offset] for offset in used])
            self.blocks.update(zip(used, held))
        others = exchange(value)
        for offset, bit in self.fetches[step]:
            self.coming[offset ^ bit] = swap(self.blocks[offset], "src", bit)
        if self.groups[step]:
            held = [self.blocks[offset] for offset in self.groups[step]]
            self.add(held[0] if len(held) == 1 else jnp.concatenate(held, axis=0), self.groups[step])
        return others

    def add(self, mine, offsets):
        group = len(self.mine)
        self.mine.append(mine)
        self.theirs.append(swap(mine, "tgt", 1))
        self.offsets.append(offsets)
        self.todo += [(group, first, min(2, len(offsets))) for first in range(0, len(offsets), 2)]

    def land(self, value):
        if self.coming:
            value, *held = tie(value, *self.coming.values())
            self.blocks.update(zip(self.coming, held))
            self.coming = {}
        if self.theirs:
            value, self.theirs[-1] = tie(value, self.theirs[-1])
        return value

    def piece(self):
        group, first, size = self.todo.pop(0)
        share = self.own.shape[1]
        rows = self.rows
        prepare = self.ready is None
        slab, terms, token, *ready = call(
            functools.partial(slab_kernel, first=first, n_half=self.n_half, prepare=prepare),
            [(share, size * rows), ((size * rows, 2 * DEPTH), jnp.bfloat16), (8, LANES)]
            + [((share, 6 * DEPTH), jnp.bfloat16), (share, LANES)] * prepare,
            [(DEPTH, rows)] + [(share // LANES, LANES)] * prepare,
            [self.own, self.mine[group], self.theirs[group], *(self.ready or [])],
            12 * DEPTH * share * size * rows,
        )
        self.ready = ready or self.ready
        self.terms.append(terms)
        self.slabs.append(slab)
        self.done.append(self.offsets[group][first : first + size])
        return token

    def hold(self, value):
        value, self.own = tie(value, self.own)
        return value

    def pieces(self, value, most):
        for _ in range(min(most, len(self.todo))):
            value, token = tie(value, self.piece())
            self.tokens.append(token)
        return value

    def finish(self, value):
        for bit in self.bits:
            for mine, offsets in list(zip(self.mine, self.offsets)):
                self.add(swap(mine, "src", bit), [offset ^ bit for offset in offsets])
        return self.pieces(self.hold(value), len(self.todo))


def shards(sources, targets, pair_active, count_src, count_tgt):
    dims, rows = sources.shape
    cols = targets.shape[1]
    n_src = lax.axis_size("src")
    share = cols // n_src
    column = (rows, LANES)
    by_row = (rows // LANES, LANES)
    by_col = (cols // LANES, LANES)
    pairs = rows * cols
    hbm = [pltpu.with_memory_space_constraint(x, pltpu.HBM) for x in (sources, targets, count_src, count_tgt)]
    n_half = -(-dims // 2)
    packed = -(-n_half * by_row[0] // 8) * 8
    outs = [(rows, cols), by_row, (3, *by_row), (3, *by_col), (DEPTH, share), (1, packed, LANES)]
    score, lse, row_aux, col_aux, own, half = pl.pallas_call(
        first_kernel,
        out_shape=[pltpu.VMEM(shape, jnp.float32) for shape in outs],
        in_specs=[pl.BlockSpec(memory_space=pltpu.HBM)] * 4 + [SMEM_SPEC],
        out_specs=[VMEM_SPEC] * len(outs),
        scratch_shapes=[
            pltpu.VMEM((dims, rows), jnp.float32),
            pltpu.VMEM((dims, cols), jnp.float32),
            pltpu.SMEM(count_src.shape, jnp.int32),
            pltpu.SMEM(count_tgt.shape, jnp.int32),
            pltpu.SemaphoreType.DMA((4,)),
            pltpu.VMEM((DEPTH, 512), jnp.float32),
            pltpu.VMEM((DEPTH, rows), jnp.float32),
            pltpu.VMEM((rows, 6 * DEPTH), jnp.bfloat16),
            pltpu.VMEM(by_row, jnp.float32),
            pltpu.VMEM(column, jnp.float32),
            pltpu.VMEM(column, jnp.float32),
            pltpu.VMEM(column, jnp.float32),
        ],
        compiler_params=pltpu.CompilerParams(vmem_limit_bytes=VMEM_LIMIT),
        cost_estimate=pl.CostEstimate(flops=12 * DEPTH * pairs, bytes_accessed=0, transcendentals=pairs),
    )(*hbm, pair_active)
    over_tgt = doubling(lax.axis_size("tgt"))
    over_src = doubling(n_src)
    over_src = over_src[1:] + over_src[:1]
    side = Beside(half, own, over_src, rows, n_half)
    near = [bit for bit in (2, 3, 1) if bit < lax.axis_size("tgt")]

    def exchange(value):
        return [swap(value, "tgt", bit) for bit in near]

    def combine(value, others):
        values = dict(zip(near, others))
        value = merge(value, values[1])
        return merge(value, merge(values[2], values[3])) if 2 in values else value

    for step in range(ITERS):
        if step == ITERS - 1:
            lse = side.hold(lse)
        others = side.start(step, lse, exchange)
        if step == ITERS - 1:
            others[0] = side.pieces(others[0], len(side.todo))
        lse = combine(lse, others)
        for bit in over_tgt[2:]:
            lse = merge(lse, swap(lse, "tgt", bit))
        if step == 0:
            lse, base, kernel, top = call(
                first_col_kernel,
                [(n_src, *by_col), by_row, (rows, cols), by_col],
                [by_col, by_row, column], [score, lse, row_aux], 0,
            )
        else:
            last = step == ITERS - 1
            extra = by_row[0] if last else 0
            lse, *held = call(
                functools.partial(col_kernel, last=last),
                [(n_src, by_col[0] + extra, LANES)] + [by_row] * last,
                [by_row] * (not last) + [by_col, by_row, by_row, column],
                [score, kernel, top, base, lse, row_aux], 0,
            )
            if last:
                (f,) = held
        if step < ITERS - 1:
            lse = side.land(side.pieces(side.hold(lse), min(step, 1)))
            lse = lax.all_to_all(lse, "src", 0, 0, tiled=True)
            (lse,) = call(
                row_kernel,
                [by_row],
                [by_col, by_col, column, column],
                [score, kernel, top, base, lse, row_aux, col_aux], 0,
            )
    lse = side.finish(lse)
    both = lax.all_to_all(lse, "src", 0, 0, tiled=True)
    ancestors, f, g = call(
        functools.partial(last_kernel, pieces=side.done),
        [(dims, share), by_row, by_col],
        [by_col, (share // LANES, LANES), (share, LANES), (share, 2 * DEPTH)],
        [*side.slabs, *side.terms, both, col_aux, f, *side.tokens],
        18 * DEPTH * pairs, pairs, pin=False,
    )
    return (f.reshape(rows), g.reshape(cols), ancestors)


def solution(mesh):
    return jax.shard_map(
        shards,
        mesh=mesh,
        in_specs=(P(None, "src"), P(None, "tgt"), P("src", "tgt"), P(), P()),
        out_specs=(P("src"), P("tgt"), P(None, ("tgt", "src"))),
        check_vma=False,
    )
```

```python
import functools
import math

import jax
import jax.numpy as jnp
from jax import lax
from jax.experimental import pallas as pl
from jax.experimental.pallas import tpu as pltpu
from jax.sharding import PartitionSpec as P

ITERS = 4
EPS = 0.02
NEG = -1e30
LOG2E = math.log2(math.e)
SCALE = LOG2E / EPS
LANES = 128
DEPTH = 64
SHIFT = 40.0
ROW_FACTOR_MAX = 2.0**20
COL_FACTOR_MAX = 2.0**60
SUM_MIN = 2.0**-30
VMEM_LIMIT = 14 * 1024 * 1024

VMEM_SPEC = pl.BlockSpec(memory_space=pltpu.VMEM)
SMEM_SPEC = pl.BlockSpec(memory_space=pltpu.SMEM)


def pinned(x):
    return pltpu.with_memory_space_constraint(x, pltpu.VMEM)


def split(x):
    high = x.astype(jnp.bfloat16)
    rest = x - high.astype(jnp.float32)
    mid = rest.astype(jnp.bfloat16)
    low = (rest - mid.astype(jnp.float32)).astype(jnp.bfloat16)
    return high, mid, low


def put(ref, row):
    for k in range(row.shape[1] // LANES):
        ref[k : k + 1, :] = row[:, k * LANES : (k + 1) * LANES]


def positions(shape):
    return lax.broadcasted_iota(jnp.int32, shape, 0) * LANES + lax.broadcasted_iota(jnp.int32, shape, 1)


def to_sublanes(vector_ref, col_ref):
    for k in range(vector_ref.shape[0]):
        col_ref[k * LANES : (k + 1) * LANES, :] = jnp.broadcast_to(vector_ref[k : k + 1, :], (LANES, LANES)).T


def fold_lanes(peak_ref, total_ref, out_ref):
    for k in range(out_ref.shape[0]):
        here = slice(k * LANES, (k + 1) * LANES)
        peaks = peak_ref[here, :].T
        top = jnp.max(peaks, axis=0, keepdims=True)
        total = jnp.sum(total_ref[here, :].T * jnp.exp2(peaks - top), axis=0, keepdims=True)
        out_ref[k : k + 1, :] = top + jnp.log2(total)


def row_lse(score_ref, add_ref, peak_ref, total_ref, out_ref):
    rows, cols = score_ref.shape

    def block(i, _):
        here = pl.ds(pl.multiple_of(i * 8, 8), 8)
        z = []
        for k in range(cols // LANES):
            z.append(score_ref[here, k * LANES : (k + 1) * LANES] + add_ref[k : k + 1, :])
        peak = functools.reduce(jnp.maximum, z)
        peak_ref[here, :] = peak
        total_ref[here, :] = functools.reduce(jnp.add, [jnp.exp2(v - peak) for v in z])
        return 0

    lax.fori_loop(0, rows // 8, block, 0)
    fold_lanes(peak_ref, total_ref, out_ref)


def col_lse(score_ref, add_ref, out_ref, kernel_ref=None, top_ref=None):
    rows, cols = score_ref.shape
    group = 16
    tall = 4
    written_out = kernel_ref is not None

    for first in range(0, cols // LANES, group):
        lanes = [slice((first + k) * LANES, (first + k + 1) * LANES) for k in range(group)]

        def peaks(i, tops):
            for r in range(tall):
                here = pl.ds(pl.multiple_of((i * tall + r) * 8, 8), 8)
                add = add_ref[here, :]
                tops = tuple(jnp.maximum(t, score_ref[here, s] + add) for t, s in zip(tops, lanes))
            return tops

        start = (jnp.full((8, LANES), -jnp.inf, jnp.float32),) * group
        tops = lax.fori_loop(0, rows // (8 * tall), peaks, start, unroll=written_out)
        tops = [jnp.max(t, axis=0, keepdims=True) - SHIFT for t in tops]
        wide_tops = [jnp.broadcast_to(t, (8, LANES)) for t in tops]

        def totals(i, sums):
            for r in range(tall):
                here = pl.ds(pl.multiple_of((i * tall + r) * 8, 8), 8)
                add = add_ref[here, :]
                terms = [jnp.exp2(score_ref[here, s] + (add - t)) for t, s in zip(wide_tops, lanes)]
                if kernel_ref is not None:
                    for s, t in zip(lanes, terms):
                        kernel_ref[here, s] = t
                sums = tuple(u + t for u, t in zip(sums, terms))
            return sums

        start = (jnp.zeros((8, LANES), jnp.float32),) * group
        sums = lax.fori_loop(0, rows // (8 * tall), totals, start, unroll=written_out)
        for k, (t, u) in enumerate(zip(tops, sums)):
            spot = slice(first + k, first + k + 1)
            if top_ref is not None:
                top_ref[spot, :] = t
            out_ref[spot, :] = t + jnp.log2(jnp.sum(u, axis=0, keepdims=True))


def source_terms(x):
    high, mid, low = split(x * (2.0 * SCALE))
    return [high, high, mid, mid, high, low]


def target_terms(y):
    high, mid, low = split(y)
    return [high, mid, high, mid, low, high]


def pad_into(pad_ref, values):
    pad_ref[...] = jnp.zeros(pad_ref.shape, jnp.float32)
    pad_ref[0 : values.shape[0], :] = values


def live_sum(counts):
    total = counts[0]
    for i in range(1, counts.shape[0]):
        total = total + counts[i]
    return jnp.full((1, LANES), total, jnp.int32).astype(jnp.float32)


def wide(x, size):
    return jnp.concatenate([x] * (size // LANES), axis=1)


def first_kernel(
    src_hbm, tgt_hbm, count_src_hbm, count_tgt_hbm, pair,
    score_ref, lse_ref, row_aux, col_aux, own_ref, half_ref,
    src_ref, tgt_ref, count_src, count_tgt, sems,
    right_pad, left_pad, terms_ref, norm_ref, col_ref, peak_ref, total_ref,
):
    rows, cols = score_ref.shape
    dims = src_ref.shape[0]
    copies = [
        pltpu.make_async_copy(one, two, sems.at[i])
        for i, (one, two) in enumerate(
            [(count_src_hbm, count_src), (count_tgt_hbm, count_tgt), (src_hbm, src_ref), (tgt_hbm, tgt_ref)]
        )
    ]
    for copy in copies:
        copy.start()
    for ref in (right_pad, left_pad, own_ref):
        ref[...] = jnp.zeros(ref.shape, jnp.float32)
    n_half = -(-dims // 2)
    for copy in copies[:3]:
        copy.wait()
    n_rows = count_src[lax.axis_index("src")]
    n_cols = count_tgt[lax.axis_index("tgt")]
    listed = pair[0, 0] > 0
    row_live = positions(row_aux.shape[1:]) < n_rows
    col_live = positions(col_aux.shape[1:]) < n_cols
    row_aux[0] = row_live.astype(jnp.float32)
    row_aux[1] = jnp.where(row_live, -jnp.log2(live_sum(count_src)), 0.0)
    row_aux[2] = (row_live & listed).astype(jnp.float32)
    col_aux[0] = col_live.astype(jnp.float32)
    col_aux[1] = jnp.where(col_live, -jnp.log2(live_sum(count_tgt)), 0.0)
    left_pad[0:dims, :] = src_ref[...]
    left = left_pad[...]
    half = jnp.where(lax.axis_index("tgt") % 2 == 0, left[0:n_half], left[n_half : 2 * n_half])
    half_ref[...] = jnp.zeros(half_ref.shape, jnp.float32)
    for k in range(rows // LANES):
        half_ref[0, k * n_half : (k + 1) * n_half, :] = half[:, k * LANES : (k + 1) * LANES]
    put(norm_ref, -SCALE * jnp.sum(left * left, axis=0, keepdims=True))
    norm_ref[...] = jnp.where(row_live, norm_ref[...], NEG)
    to_sublanes(norm_ref, col_ref)
    terms_ref[...] = jnp.concatenate(source_terms(left.T), axis=1)
    copies[3].wait()
    size = 512

    def scores(c):
        here = slice(c * size, (c + 1) * size)
        right_pad[0:dims, :] = tgt_ref[:, here]
        right = right_pad[...]
        spot = lax.broadcasted_iota(jnp.int32, (1, size), 1) + c * size
        norm = -SCALE * jnp.sum(right * right, axis=0, keepdims=True)
        norm = jnp.where((spot < n_cols) & listed, norm, NEG)
        terms = jnp.concatenate(target_terms(right), axis=0)
        cross = jnp.dot(terms_ref[...], terms, preferred_element_type=jnp.float32)
        score = cross + (wide(col_ref[...], size) + norm)
        score_ref[:, here] = score
        return [score[:, k : k + LANES] for k in range(0, size, LANES)]

    peak_ref[...] = jnp.full(peak_ref.shape, 2.0 * NEG, jnp.float32)
    total_ref[...] = jnp.zeros(total_ref.shape, jnp.float32)

    for c in range(cols // size):
        z = scores(c)
        before = peak_ref[...]
        peak = functools.reduce(jnp.maximum, z, before)
        total_ref[...] = functools.reduce(
            jnp.add, [jnp.exp2(v - peak) for v in z], total_ref[...] * jnp.exp2(before - peak)
        )
        peak_ref[...] = peak
    share = own_ref.shape[1]
    own_ref[0:dims, :] = tgt_ref[:, pl.ds(pl.multiple_of(lax.axis_index("src") * share, share), share)]
    fold_lanes(peak_ref, total_ref, lse_ref)


def slab_kernel(own_ref, mine_ref, theirs_ref, *refs, first, n_half, prepare):
    if prepare:
        slab_ref, terms_out, token_ref, terms_ref, col_ref, right_pad, norm_ref = refs
        left = own_ref[...]
        put(norm_ref, -SCALE * jnp.sum(left * left, axis=0, keepdims=True))
        to_sublanes(norm_ref, col_ref)
        terms_ref[...] = jnp.concatenate(target_terms(left.T), axis=1)
    else:
        terms_ref, col_ref, slab_ref, terms_out, token_ref, right_pad = refs
    rows = right_pad.shape[1]
    even = lax.axis_index("tgt") % 2 == 0
    right_pad[...] = jnp.zeros(right_pad.shape, jnp.float32)
    for b in range(slab_ref.shape[1] // rows):
        mine, theirs = mine_ref[first + b], theirs_ref[first + b]
        upper = jnp.where(even, mine, theirs)
        lower = jnp.where(even, theirs, mine)
        for k in range(rows // LANES):
            here = slice(k * n_half, (k + 1) * n_half)
            right_pad[0:n_half, k * LANES : (k + 1) * LANES] = upper[here]
            right_pad[n_half : 2 * n_half, k * LANES : (k + 1) * LANES] = lower[here]
        right = right_pad[...]
        norm = -SCALE * jnp.sum(right * right, axis=0, keepdims=True)
        terms = jnp.concatenate(source_terms(right), axis=0)
        cross = jnp.dot(terms_ref[...], terms, preferred_element_type=jnp.float32)
        here = slice(b * rows, (b + 1) * rows)
        slab_ref[:, here] = cross + (wide(col_ref[...], rows) + norm)
        terms_out[here, :] = jnp.concatenate(split(right.T)[:2], axis=1)
    token_ref[...] = jnp.zeros(token_ref.shape, jnp.float32)


def row_sums(kernel_ref, factor_ref, total_ref, out_ref):
    rows, cols = kernel_ref.shape
    tall = 8

    def block(i, _):
        spots = [pl.ds(pl.multiple_of((i * tall + k) * 8, 8), 8) for k in range(tall)]
        sums = [jnp.zeros((8, LANES), jnp.float32)] * tall
        for t in range(cols // LANES):
            lanes = slice(t * LANES, (t + 1) * LANES)
            factor = jnp.broadcast_to(factor_ref[t : t + 1, :], (8, LANES))
            sums = [u + kernel_ref[s, lanes] * factor for u, s in zip(sums, spots)]
        for s, u in zip(spots, sums):
            total_ref[s, :] = u
        return 0

    lax.fori_loop(0, rows // (8 * tall), block, 0, unroll=True)
    for k in range(out_ref.shape[0]):
        out_ref[k : k + 1, :] = jnp.sum(total_ref[k * LANES : (k + 1) * LANES, :].T, axis=0, keepdims=True)


def col_sums(kernel_ref, factor_ref, out_ref):
    rows, cols = kernel_ref.shape
    lanes = [slice(start, start + LANES) for start in range(0, cols, LANES)]
    tall = 4

    def block(i, sums):
        for r in range(tall):
            here = pl.ds(pl.multiple_of((i * tall + r) * 8, 8), 8)
            factor = factor_ref[here, :]
            sums = tuple(u + kernel_ref[here, s] * factor for u, s in zip(sums, lanes))
        return sums

    start = (jnp.zeros((8, LANES), jnp.float32),) * len(lanes)
    sums = lax.fori_loop(0, rows // (8 * tall), block, start, unroll=True)
    for k, u in enumerate(sums):
        out_ref[k : k + 1, :] = jnp.sum(u, axis=0, keepdims=True)


def out_of_range(total, needed, factor, most):
    small = jnp.where(needed & jnp.logical_not(total >= SUM_MIN), 1.0, 0.0)
    large = jnp.where(factor <= most, 0.0, 1.0)
    return jnp.max(jnp.maximum(jnp.max(small, axis=0, keepdims=True), jnp.max(large, axis=0, keepdims=True))) > 0.5


def set_f(lse_ref, aux_ref, f_ref, masked_ref):
    f = aux_ref[1] - lse_ref[...] * aux_ref[0]
    f_ref[...] = f
    masked_ref[...] = jnp.where(aux_ref[2] > 0, f, NEG)


def spread(lse, send_ref, masked=None):
    n_col = lse.shape[0]
    for k in range(send_ref.shape[0]):
        send_ref[k, 0:n_col, :] = lse
        if masked is not None:
            send_ref[k, n_col:, :] = masked


def first_col_kernel(
    score_ref, lse_ref, aux_ref, send_ref, f_ref, kernel_ref, top_ref, out_ref, masked_ref, col_ref
):
    set_f(lse_ref, aux_ref, f_ref, masked_ref)
    to_sublanes(f_ref, col_ref)
    col_lse(score_ref, col_ref, out_ref, kernel_ref, top_ref)
    spread(out_ref[...], send_ref)


def col_kernel(
    score_ref, kernel_ref, top_ref, base_ref, lse_ref, aux_ref, send_ref, f_ref, out_ref, masked_ref, factor_ref,
    col_ref, *, last,
):
    set_f(lse_ref, aux_ref, f_ref, masked_ref)
    factor_ref[...] = jnp.exp2(f_ref[...] - base_ref[...])
    to_sublanes(factor_ref, col_ref)
    col_sums(kernel_ref, col_ref, out_ref)
    total = out_ref[...]
    top = top_ref[...]
    redo = out_of_range(total, top > 0.5 * NEG, factor_ref[...], ROW_FACTOR_MAX)
    masked = masked_ref[...] if last else None
    spread(jnp.where(total > 0, top + jnp.log2(total), NEG), send_ref, masked)

    @pl.when(redo)
    def _():
        to_sublanes(f_ref, col_ref)
        col_lse(score_ref, col_ref, out_ref)
        spread(out_ref[...], send_ref, masked)


def merged(parts):
    peak = jnp.max(parts, axis=0)
    return peak + jnp.log2(jnp.sum(jnp.exp2(parts - peak[None]), axis=0))


def row_kernel(
    score_ref, kernel_ref, top_ref, base_ref, parts_ref, row_aux, col_aux, out_ref,
    g_ref, factor_ref, peak_ref, total_ref,
):
    lse = merged(parts_ref[...])
    g_ref[...] = col_aux[1] - lse * col_aux[0]
    factor_ref[...] = jnp.where(col_aux[0] > 0, jnp.exp2(top_ref[...] - lse + 2.0 * SHIFT), 0.0)
    row_sums(kernel_ref, factor_ref, total_ref, out_ref)
    total = out_ref[...]
    redo = out_of_range(total, row_aux[2] > 0, factor_ref[...], COL_FACTOR_MAX)
    log_b = col_aux[1, 0:1, 0:1]
    out_ref[...] = jnp.where(total > 0, jnp.log2(total) - 2.0 * SHIFT - base_ref[...] + log_b, NEG)

    @pl.when(redo)
    def _():
        row_lse(score_ref, g_ref, peak_ref, total_ref, out_ref)


def last_kernel(*refs, pieces):
    slabs, refs = refs[: len(pieces)], refs[len(pieces) :]
    terms, refs = refs[: len(pieces)], refs[len(pieces) :]
    parts_ref, aux_ref, f_ref, *_, out_ref, f_out, g_out, lse_ref, own_ref, col_ref, sum_ref = refs
    n_col = aux_ref.shape[1]
    lse = merged(parts_ref[:, 0:n_col, :])
    lse_ref[...] = lse
    f_out[...] = f_ref[...] * (1.0 / SCALE)
    g_out[...] = (aux_ref[1] - lse * aux_ref[0]) * (1.0 / SCALE)
    me = lax.axis_index("src")
    n_own = own_ref.shape[0]
    for k in range(n_own):
        spot = pl.ds(me * n_own + k, 1)
        own_ref[k : k + 1, :] = jnp.where(aux_ref[0, spot, :] > 0, -lse_ref[spot, :], NEG)
    to_sublanes(own_ref, col_ref)
    for i, (slab_ref, terms_ref, offsets) in enumerate(zip(slabs, terms, pieces)):
        high, mid = [], []
        start = 0
        for offset in offsets:
            for row in range(n_col, parts_ref.shape[1]):
                add = col_ref[...] + parts_ref[me ^ offset, row : row + 1, :]
                term = split(jnp.exp2(slab_ref[:, start : start + LANES] + add))
                high.append(term[0])
                mid.append(term[1])
                start += LANES
        sums = jnp.dot(
            jnp.concatenate(high + mid, axis=1), jnp.concatenate([terms_ref[...]] * 2, axis=0),
            preferred_element_type=jnp.float32,
        )
        if i == 0:
            sum_ref[...] = sums
        else:
            sum_ref[...] += sums
    sums = sum_ref[...].T
    out_ref[...] = (sums[0:DEPTH] + sums[DEPTH :])[0 : out_ref.shape[0]]


def merge(one, two):
    top = jnp.maximum(one, two)
    return top + jnp.log2(1.0 + jnp.exp2(jnp.minimum(one, two) - top))


def swap(value, axis, step):
    return lax.ppermute(value, axis, [(i, i ^ step) for i in range(lax.axis_size(axis))])


def doubling(size):
    return [1 << k for k in range(size.bit_length() - 1)]


def buffer(space, shape):
    return space(*shape) if isinstance(shape[0], tuple) else space(shape, jnp.float32)


def call(kernel, outs, scratch, ins, flops, expos=0, pin=True):
    return pl.pallas_call(
        kernel,
        out_shape=[buffer(pltpu.VMEM if pin else jax.ShapeDtypeStruct, shape) for shape in outs],
        in_specs=[VMEM_SPEC] * len(ins),
        out_specs=[VMEM_SPEC] * len(outs),
        scratch_shapes=[buffer(pltpu.VMEM, shape) for shape in scratch],
        compiler_params=pltpu.CompilerParams(vmem_limit_bytes=VMEM_LIMIT),
        cost_estimate=pl.CostEstimate(flops=flops, bytes_accessed=0, transcendentals=expos),
    )(*[pinned(x) for x in ins])


def tie(*values):
    return lax.optimization_barrier(values)


class Beside:
    def __init__(self, half, own, bits, rows, n_half):
        self.own = own
        self.rows = rows
        self.n_half = n_half
        self.blocks = {(0,): half}
        self.coming = {}
        if len(bits) >= 3:
            z, w, x = bits[:3]
            self.fetches = [
                [([(0,)], w), ([(0,)], z), ([(0,)], x)], [([(z,)], x), ([(w,)], z)], [([(w,), (w ^ z,)], x)], []
            ]
            self.groups = [[], [(0,), (z,), (w,), (x,)], [(z ^ x,), (w ^ z,)], [(w ^ x, w ^ z ^ x)]]
            self.bits = bits[3:]
        else:
            self.fetches = [[]] * ITERS
            self.groups = [[]] * (ITERS - 1) + [[(0,)]]
            self.bits = bits
        self.ready = None
        self.mine = []
        self.theirs = []
        self.offsets = []
        self.todo = []
        self.tokens = []
        self.slabs = []
        self.terms = []
        self.done = []

    def start(self, step, value, exchange):
        used = sorted({key for keys, _ in self.fetches[step] for key in keys} | set(self.groups[step]))
        if step and used:
            value, *held = tie(value, *[self.blocks[key] for key in used])
            self.blocks.update(zip(used, held))
        others = exchange(value)
        for keys, bit in self.fetches[step]:
            self.coming[tuple(offset ^ bit for key in keys for offset in key)] = swap(self.joined(keys), "src", bit)
        if self.groups[step]:
            self.add(self.joined(self.groups[step]), [offset for key in self.groups[step] for offset in key])
        return others

    def joined(self, keys):
        held = [self.blocks[key] for key in keys]
        return held[0] if len(held) == 1 else jnp.concatenate(held, axis=0)

    def add(self, mine, offsets):
        group = len(self.mine)
        self.mine.append(mine)
        self.theirs.append(swap(mine, "tgt", 1))
        self.offsets.append(offsets)
        self.todo += [(group, first, min(2, len(offsets))) for first in range(0, len(offsets), 2)]

    def land(self, value):
        if self.coming:
            value, *held = tie(value, *self.coming.values())
            self.blocks.update(zip(self.coming, held))
            self.coming = {}
        if self.theirs:
            value, self.theirs[-1] = tie(value, self.theirs[-1])
        return value

    def piece(self):
        group, first, size = self.todo.pop(0)
        share = self.own.shape[1]
        rows = self.rows
        prepare = self.ready is None
        slab, terms, token, *ready = call(
            functools.partial(slab_kernel, first=first, n_half=self.n_half, prepare=prepare),
            [(share, size * rows), ((size * rows, 2 * DEPTH), jnp.bfloat16), (8, LANES)]
            + [((share, 6 * DEPTH), jnp.bfloat16), (share, LANES)] * prepare,
            [(DEPTH, rows)] + [(share // LANES, LANES)] * prepare,
            [self.own, self.mine[group], self.theirs[group], *(self.ready or [])],
            12 * DEPTH * share * size * rows,
        )
        self.ready = ready or self.ready
        self.terms.append(terms)
        self.slabs.append(slab)
        self.done.append(self.offsets[group][first : first + size])
        return token

    def hold(self, value):
        value, self.own = tie(value, self.own)
        return value

    def pieces(self, value, most):
        for _ in range(min(most, len(self.todo))):
            value, token = tie(value, self.piece())
            self.tokens.append(token)
        return value

    def finish(self, value):
        for bit in self.bits:
            for mine, offsets in list(zip(self.mine, self.offsets)):
                self.add(swap(mine, "src", bit), [offset ^ bit for offset in offsets])
        return self.pieces(self.hold(value), len(self.todo))


def shards(sources, targets, pair_active, count_src, count_tgt):
    dims, rows = sources.shape
    cols = targets.shape[1]
    n_src = lax.axis_size("src")
    share = cols // n_src
    column = (rows, LANES)
    by_row = (rows // LANES, LANES)
    by_col = (cols // LANES, LANES)
    pairs = rows * cols
    hbm = [pltpu.with_memory_space_constraint(x, pltpu.HBM) for x in (sources, targets, count_src, count_tgt)]
    n_half = -(-dims // 2)
    packed = -(-n_half * by_row[0] // 8) * 8
    outs = [(rows, cols), by_row, (3, *by_row), (3, *by_col), (DEPTH, share), (1, packed, LANES)]
    score, lse, row_aux, col_aux, own, half = pl.pallas_call(
        first_kernel,
        out_shape=[pltpu.VMEM(shape, jnp.float32) for shape in outs],
        in_specs=[pl.BlockSpec(memory_space=pltpu.HBM)] * 4 + [SMEM_SPEC],
        out_specs=[VMEM_SPEC] * len(outs),
        scratch_shapes=[
            pltpu.VMEM((dims, rows), jnp.float32),
            pltpu.VMEM((dims, cols), jnp.float32),
            pltpu.SMEM(count_src.shape, jnp.int32),
            pltpu.SMEM(count_tgt.shape, jnp.int32),
            pltpu.SemaphoreType.DMA((4,)),
            pltpu.VMEM((DEPTH, 512), jnp.float32),
            pltpu.VMEM((DEPTH, rows), jnp.float32),
            pltpu.VMEM((rows, 6 * DEPTH), jnp.bfloat16),
            pltpu.VMEM(by_row, jnp.float32),
            pltpu.VMEM(column, jnp.float32),
            pltpu.VMEM(column, jnp.float32),
            pltpu.VMEM(column, jnp.float32),
        ],
        compiler_params=pltpu.CompilerParams(vmem_limit_bytes=VMEM_LIMIT),
        cost_estimate=pl.CostEstimate(flops=12 * DEPTH * pairs, bytes_accessed=0, transcendentals=pairs),
    )(*hbm, pair_active)
    over_tgt = doubling(lax.axis_size("tgt"))
    over_src = doubling(n_src)
    over_src = over_src[1:] + over_src[:1]
    side = Beside(half, own, over_src, rows, n_half)
    near = [bit for bit in (2, 3, 1) if bit < lax.axis_size("tgt")]

    def exchange(value):
        return [swap(value, "tgt", bit) for bit in near]

    def combine(value, others):
        values = dict(zip(near, others))
        value = merge(value, values[1])
        return merge(value, merge(values[2], values[3])) if 2 in values else value

    for step in range(ITERS):
        if step == ITERS - 1:
            lse = side.hold(lse)
        others = side.start(step, lse, exchange)
        if step == ITERS - 1:
            others[0] = side.pieces(others[0], len(side.todo))
        lse = combine(lse, others)
        for bit in over_tgt[2:]:
            lse = merge(lse, swap(lse, "tgt", bit))
        if step == 0:
            lse, base, kernel, top = call(
                first_col_kernel,
                [(n_src, *by_col), by_row, (rows, cols), by_col],
                [by_col, by_row, column], [score, lse, row_aux], 0,
            )
        else:
            last = step == ITERS - 1
            extra = by_row[0] if last else 0
            lse, *held = call(
                functools.partial(col_kernel, last=last),
                [(n_src, by_col[0] + extra, LANES)] + [by_row] * last,
                [by_row] * (not last) + [by_col, by_row, by_row, column],
                [score, kernel, top, base, lse, row_aux], 0,
            )
            if last:
                (f,) = held
        if step < ITERS - 1:
            lse = side.land(side.pieces(side.hold(lse), min(step, 1)))
            lse = lax.all_to_all(lse, "src", 0, 0, tiled=True)
            (lse,) = call(
                row_kernel,
                [by_row],
                [by_col, by_col, column, column],
                [score, kernel, top, base, lse, row_aux, col_aux], 0,
            )
    lse = side.finish(lse)
    both = lax.all_to_all(lse, "src", 0, 0, tiled=True)
    ancestors, f, g = call(
        functools.partial(last_kernel, pieces=side.done),
        [(dims, share), by_row, by_col],
        [by_col, (share // LANES, LANES), (share, LANES), (share, 2 * DEPTH)],
        [*side.slabs, *side.terms, both, col_aux, f, *side.tokens],
        18 * DEPTH * pairs, pairs, pin=False,
    )
    return (f.reshape(rows), g.reshape(cols), ancestors)


def solution(mesh):
    return jax.shard_map(
        shards,
        mesh=mesh,
        in_specs=(P(None, "src"), P(None, "tgt"), P("src", "tgt"), P(), P()),
        out_specs=(P("src"), P("tgt"), P(None, ("tgt", "src"))),
        check_vma=False,
    )
```
